32 devices in a mesh: seq: 8 (over y, x, core), fsdp: 4 (over z).
Axes of the slice: x: 2, y: 2, z: 4, core: 2. Of those that a mesh axis runs over, the one named last changes fastest.
Arguments:
- tokens: bfloat16 [4, 2048, 1024], P('fsdp', 'seq'), may hold values from -6 to 6
- weight_query: bfloat16 [1024, 1024], P(('seq', 'fsdp')), may hold values from -0.1875 to 0.1875
- weight_key: bfloat16 [1024, 1024], P(('seq', 'fsdp')), may hold values from -0.1875 to 0.1875
- weight_value: bfloat16 [1024, 1024], P(('seq', 'fsdp')), may hold values from -0.1875 to 0.1875
- weight_out: bfloat16 [1024, 1024], P(('seq', 'fsdp')), may hold values from -6 to 6
- weight_gate: bfloat16 [1024, 4096], P(('seq', 'fsdp')), may hold values from -0.1875 to 0.1875
- weight_up: bfloat16 [1024, 4096], P(('seq', 'fsdp')), may hold values from -0.1875 to 0.1875
- weight_down: bfloat16 [4096, 1024], P(('seq', 'fsdp')), may hold values from -0.09375 to 0.09375
- norm_attn: float32 [1024], replicated, may hold values from 0.5 to 1.5
- norm_ffn: float32 [1024], replicated, may hold values from 0.5 to 1.5
- query_gain: float32 [64], replicated, may hold values from 0.5 to 1.5
- key_gain: float32 [64], replicated, may hold values from 0.5 to 1.5
- variate_bias: float32 [2, 16], P(None, 'seq'), may hold values from -1.5 to 1.5
- variate_ids: int32 [4, 2048], P('fsdp', 'seq'), may hold values from 0 to 3
- sample_ids: int32 [4, 2048], P('fsdp', 'seq'), may hold values from 0 to 2, as said below
- time_ids: int32 [4, 2048], P('fsdp', 'seq'), may hold values from 0 to 2047
- out_grad: bfloat16 [4, 2048, 1024], P('fsdp', 'seq'), may hold values from -6 to 6
Outputs:
- layer_out: bfloat16 [4, 2048, 1024], P('fsdp', 'seq')
- in_grad: float32 [4, 2048, 1024], P('fsdp', 'seq')
- grad_weight_query: float32 [1024, 1024], P(('seq', 'fsdp'))
- grad_weight_key: float32 [1024, 1024], P(('seq', 'fsdp'))
- grad_weight_value: float32 [1024, 1024], P(('seq', 'fsdp'))
- grad_weight_out: float32 [1024, 1024], P(('seq', 'fsdp'))
- grad_weight_gate: float32 [1024, 4096], P(('seq', 'fsdp'))
- grad_weight_up: float32 [1024, 4096], P(('seq', 'fsdp'))
- grad_weight_down: float32 [4096, 1024], P(('seq', 'fsdp'))
- grad_norm_attn: float32 [1024], replicated
- grad_norm_ffn: float32 [1024], replicated
- grad_query_gain: float32 [64], replicated
- grad_key_gain: float32 [64], replicated
- grad_variate_bias: float32 [2, 16], P(None, 'seq')
The draws below stay inside these ranges and needn't reach their ends.
Inputs may be any that keep to these rules, and one draw needn't show every extreme that they name: `sample_ids`: in each sequence the ids run 0, then 1, then 2, each run non-empty; the runs of 0 and of 2 are each shorter than 256 tokens.
All inputs are finite; a program needn't handle non-finite values.
Results may differ from the reference program's by a relative error of at most 0.025.
Values may be sent and summed in bfloat16 or wider, within the bound.
No kernel may reach another device: no remote copies, remote signals or barrier semaphores. Data moves between devices by JAX's collectives and lax.ppermute only.
A program may use at most 192 MiB of HBM per device.

```python
import math
import jax
import jax.numpy as jnp
from jax import lax

D = 1024
H = 16
HS = 64
FF = 4096
TOK_DEV = 256
LEN = 2048
SEQS = 4


def draw_sample_ids(key, part):
    key = jax.random.fold_in(key, 11)
    first_key, second_key = jax.random.split(key)
    starts = jax.random.randint(first_key, (SEQS, 1), 1, TOK_DEV)
    finishes = jax.random.randint(second_key, (SEQS, 1), LEN - TOK_DEV + 1, LEN)
    positions = jnp.arange(LEN, dtype=jnp.int32)[None, :]
    return (positions >= starts).astype(jnp.int32) + (positions >= finishes).astype(jnp.int32)


def plant(drawn, rng, smallest, largest):
    longest = drawn.shape.index(max(drawn.shape))
    spots = []
    for shift in (0, 1):
        where = [jax.random.randint(jax.random.fold_in(rng, axis), (), 0, length) for axis, length in enumerate(drawn.shape)]
        where[longest] = (where[longest] + shift) % drawn.shape[longest]
        spots.append(tuple(where))
    return drawn.at[spots[0]].set(smallest).at[spots[1]].set(largest)


def level_of(stream_key, shape, cuts, smallest, top_value):
    loudness = 1.0
    for axis_at, shards_of in cuts:
        draws = jax.random.uniform(jax.random.fold_in(jax.random.fold_in(stream_key, 6), axis_at), (shards_of,), jnp.float32, smallest / len(cuts), top_value / len(cuts))
        loudness = loudness * jnp.repeat(jnp.exp(draws), shape[axis_at] // shards_of).reshape((-1,) + (1,) * (len(shape) - 1 - axis_at))
    return loudness


def gaussian(stream_key, shape, spread, limit, cuts=(), kind=jnp.bfloat16):
    values = jax.random.normal(stream_key, shape, jnp.float32) * spread
    if len(cuts) > 0:
        values = level_of(stream_key, shape, cuts, -0.22, 0.18) * values
    return jnp.clip(values, min=-limit, max=limit).astype(kind)


def setup_inputs(seed: int = 0) -> dict:
    key_list = jax.random.split(jax.random.key(seed), 18)
    return {
        "tokens": gaussian(key_list[0], (SEQS, LEN, D), 1.0, 6.0, ((0, 4), (1, 8))),
        "weight_query": gaussian(key_list[1], (D, D), D ** -0.5, 0.1875, ((0, 32),)),
        "weight_key": gaussian(key_list[2], (D, D), D ** -0.5, 0.1875, ((0, 32),)),
        "weight_value": gaussian(key_list[3], (D, D), D ** -0.5, 0.1875, ((0, 32),)),
        "weight_out": gaussian(key_list[4], (D, D), (max(1, 3 * D // LEN)) ** -0.5, 6.0, ((0, 32),)),
        "weight_gate": gaussian(key_list[5], (D, FF), D ** -0.5, 0.1875, ((0, 32),)),
        "weight_up": gaussian(key_list[6], (D, FF), D ** -0.5, 0.1875, ((0, 32),)),
        "weight_down": gaussian(key_list[7], (FF, D), FF ** -0.5, 0.09375, ((0, 32),)),
        "norm_attn": jnp.clip(1.0 + 0.1 * jax.random.normal(key_list[8], (D,), jnp.float32), 0.5, 1.5),
        "norm_ffn": jnp.clip(1.0 + 0.1 * jax.random.normal(key_list[9], (D,), jnp.float32), 0.5, 1.5),
        "query_gain": jnp.clip(1.0 + 0.1 * jax.random.normal(key_list[10], (HS,), jnp.float32), 0.5, 1.5),
        "key_gain": jnp.clip(1.0 + 0.1 * jax.random.normal(key_list[11], (HS,), jnp.float32), 0.5, 1.5),
        "variate_bias": jnp.clip(jax.random.uniform(key_list[12], (2, H), jnp.float32, -1.5, 1.5) * level_of(key_list[12], (2, H), ((1, 8),), -0.4, 0.0), -1.5, 1.5),
        "variate_ids": plant(jax.random.randint(key_list[13], (SEQS, LEN), 0, 4), jax.random.fold_in(key_list[13], 1), 0, 3).astype(jnp.int32),
        "sample_ids": draw_sample_ids(jax.random.fold_in(key_list[17], 71), 0),
        "time_ids": plant(jax.random.randint(key_list[15], (SEQS, LEN), 0, LEN), jax.random.fold_in(key_list[15], 1), 0, LEN - 1).astype(jnp.int32),
        "out_grad": gaussian(key_list[16], (SEQS, LEN, D), 1.0, 6.0, ((0, 4), (1, 8))),
    }


EPSILON = 1e-06
NEGATIVE = -1e+30

@jax.custom_vjp
def low(v):
    return lax.optimization_barrier(v.astype(jnp.bfloat16)).astype(jnp.float32)

@jax.custom_vjp
def low_back(v):
    return v

def low_keep(v):
    return (low(v), None)

def low_pass(kept, grad):
    return (grad,)

def back_keep(v):
    return (v, None)

def back_low(kept, grad):
    return (low(grad),)
low.defvjp(low_keep, low_pass)
low_back.defvjp(back_keep, back_low)

def product(left_side, right_side):
    return jnp.dot(left_side, right_side, precision=lax.Precision.HIGHEST)

def normed(values, gain):
    return values * lax.rsqrt(lax.optimization_barrier(jnp.mean(values * values, axis=-1, keepdims=True)) + EPSILON) * gain

def rotate(values, positions):
    half_size = values.shape[-1] // 2
    frequency = 10000.0 ** (-2.0 * jnp.arange(half_size).astype(jnp.float32) / values.shape[-1])
    angles = positions.astype(jnp.float32)[:, None] * frequency[None, :]
    cosine_table = jnp.cos(angles)[:, None, :]
    sine_table = jnp.sin(angles)[:, None, :]
    first_half = values[..., :half_size]
    second_half = values[..., half_size:]
    return jnp.concatenate([first_half * cosine_table - second_half * sine_table, first_half * sine_table + second_half * cosine_table], axis=-1)

def encoder_layer(hidden_in, params, variates, samples, positions):
    weight_query, weight_key, weight_value, weight_out, weight_gate, weight_up, weight_down, norm_attn, norm_ffn, query_gain, key_gain, variate_bias = params
    length = hidden_in.shape[0]
    normed_in = low(normed(hidden_in, norm_attn))
    query_lin = low_back(product(normed_in, weight_query)).reshape(length, H, HS)
    key_lin = low_back(product(normed_in, weight_key)).reshape(length, H, HS)
    value_heads = low_back(low(product(normed_in, weight_value))).reshape(length, H, HS)
    queries = low_back(low(rotate(normed(query_lin, query_gain), positions)))
    key_heads = low_back(low(rotate(normed(key_lin, key_gain), positions)))
    block_rows = math.gcd(length, 512)
    block_count = length // block_rows
    factor = HS ** (-0.5)

    def attend(pieces):
        query_block, query_variate, query_sample = pieces
        scores = jnp.einsum('qhd,khd->hqk', query_block, key_heads, precision=lax.Precision.HIGHEST) * factor
        same_variate = query_variate[:, None] == variates[None, :]
        scores = scores + jnp.where(same_variate[None], variate_bias[0][:, None, None], variate_bias[1][:, None, None])
        scores = low_back(scores)
        allowed = (query_sample[:, None] == samples[None, :])[None]
        scores = jnp.where(allowed, scores, NEGATIVE)
        shifted = jnp.exp(scores - lax.optimization_barrier(jnp.max(scores, axis=-1, keepdims=True)))
        weights = shifted / lax.optimization_barrier(jnp.sum(shifted, axis=-1, keepdims=True))
        return jnp.einsum('hqk,khd->qhd', low(weights), value_heads, precision=lax.Precision.HIGHEST)
    mixed_heads = lax.map(jax.checkpoint(attend), (queries.reshape(block_count, block_rows, H, HS), variates.reshape(block_count, block_rows), samples.reshape(block_count, block_rows)))
    mixed_rows = low_back(low(mixed_heads.reshape(length, H * HS)))
    middle = hidden_in + low_back(product(mixed_rows, weight_out))
    normed_mid = low(normed(middle, norm_ffn))
    gate_lin = low_back(product(normed_mid, weight_gate))
    up_lin = low_back(product(normed_mid, weight_up))
    inner_rows = low(jax.nn.silu(gate_lin) * up_lin)
    return middle + low_back(product(inner_rows, weight_down))

def reference(tokens, weight_query, weight_key, weight_value, weight_out, weight_gate, weight_up, weight_down, norm_attn, norm_ffn, query_gain, key_gain, variate_bias, variate_ids, sample_ids, time_ids, out_grad):
    params = tuple((matrix.astype(jnp.float32) for matrix in (weight_query, weight_key, weight_value, weight_out, weight_gate, weight_up, weight_down)))
    params = params + (norm_attn, norm_ffn, query_gain, key_gain, variate_bias)
    zero_grads = jax.tree.map(jnp.zeros_like, params)

    def one_sequence(totals, sequence_item):
        hidden_in, variates, samples, positions, cotangent = sequence_item

        def forward(inputs, weights):
            return encoder_layer(inputs, weights, variates, samples, positions)
        result, pullback = jax.vjp(forward, hidden_in.astype(jnp.float32), params)
        grad_in, grad_params = pullback(cotangent.astype(jnp.float32))
        return (jax.tree.map(jnp.add, totals, grad_params), (result.astype(jnp.bfloat16), grad_in))
    totals, (layer_out, in_grad) = lax.scan(one_sequence, zero_grads, (tokens, variate_ids, sample_ids, time_ids, out_grad))
    return (layer_out, in_grad, totals[0], totals[1], totals[2], totals[3], totals[4], totals[5], totals[6], totals[7], totals[8], totals[9], totals[10], totals[11])
```

```python
import functools
import math

import jax
import jax.numpy as jnp
from jax import lax
from jax.experimental import pallas as pl
from jax.experimental.pallas import tpu as pltpu
from jax.sharding import PartitionSpec as P

EPSILON = 1e-06
FAR = -1e30
LOG2E = math.log2(math.e)
WIDE = 128
ROWS_T = 160
F32 = jnp.float32
BF16 = jnp.bfloat16


def dot_nn(left, right):
    return jnp.dot(left, right, preferred_element_type=F32)


def dot_nt(left, right):
    return lax.dot_general(left, right, (((1,), (1,)), ((), ())), preferred_element_type=F32)


def dot_tn(left, right):
    return lax.dot_general(left, right, (((0,), (0,)), ((), ())), preferred_element_type=F32)


def rms_factor(values):
    return lax.rsqrt(jnp.mean(values * values, axis=-1, keepdims=True) + EPSILON)


def lanes_of(shape):
    return lax.broadcasted_iota(jnp.int32, shape, len(shape) - 1)


def head_sum(values, lane, head_size):
    low = jnp.sum(jnp.where(lane < head_size, values, 0.0), axis=-1, keepdims=True)
    high = jnp.sum(jnp.where(lane < head_size, 0.0, values), axis=-1, keepdims=True)
    return jnp.where(lane < head_size, low, high)


def partner(values, lane, head_size):
    half = head_size // 2
    up = pltpu.roll(values, WIDE - half, 1)
    down = pltpu.roll(values, half, 1)
    return jnp.where(lane % head_size < half, up, down)


def tables(lane_ref, half):
    cosine = lane_ref[0:half, :]
    sine = lane_ref[half : 2 * half, :]
    cos_rows = jnp.concatenate([cosine] * (WIDE // half), axis=0)
    sin_rows = jnp.concatenate([-sine, sine] * (WIDE // (2 * half)), axis=0)
    return cos_rows.T, sin_rows.T


def params(limit=60 * 1024 * 1024):
    return pltpu.CompilerParams(vmem_limit_bytes=limit, dimension_semantics=("arbitrary",))


def qkv_kernel(
    x_ref, w_ref, na_ref, qg_ref, kg_ref, lane_ref, bias_ref,
    nin_ref, qlin_ref, klin_ref, qa_ref, ka_ref, kt_ref, v1_ref, *, heads, head_size,
):
    half = head_size // 2
    x = x_ref[...].astype(F32)
    rows = x.shape[0]
    nin = (x * rms_factor(x) * na_ref[...]).astype(BF16)
    nin_ref[...] = nin
    lin = dot_nn(nin, w_ref[...])
    q, k, v = lin[:, :WIDE], lin[:, WIDE : 2 * WIDE], lin[:, 2 * WIDE :]
    qlin_ref[...] = q
    klin_ref[...] = k
    lane = lanes_of((rows, WIDE))
    cosine, sine = tables(lane_ref, half)

    def finish(u, gain):
        factor = lax.rsqrt(head_sum(u * u, lane, head_size) * (1.0 / head_size) + EPSILON)
        u = u * factor * gain
        return u * cosine + partner(u, lane, head_size) * sine

    q = finish(q, qg_ref[...]) * (LOG2E * head_size**-0.5)
    k = finish(k, kg_ref[...])
    row = lax.broadcasted_iota(jnp.int32, (WIDE, rows), 0)
    variate = lane_ref[2 * half : 2 * half + 1, :].astype(jnp.int32)
    sample = lane_ref[2 * half + 1 : 2 * half + 2, :].astype(jnp.int32)
    same_variate = (row % 4) == variate
    same_sample = (row - 10) == sample
    one = jnp.ones((WIDE, rows), F32)
    nil = jnp.zeros((WIDE, rows), F32)
    aug_q = jnp.where(
        row < 8,
        jnp.where(same_variate, one, nil),
        jnp.where(row < 10, one, jnp.where((row < 13) & same_sample, one, nil)),
    )
    qa_ref[...] = jnp.concatenate([q, aug_q.T], axis=1).astype(BF16)
    k_t = k.T
    for h in range(heads):
        first, second = bias_ref[0, h] * LOG2E, bias_ref[1, h] * LOG2E
        step = jnp.where(row < 8, first - second, second) * one
        high = step.astype(BF16).astype(F32)
        low = step - high
        far = jnp.where(same_sample, nil, FAR)
        plain = jnp.where(((row // 4) == 4 + h) & same_variate, one, nil)
        aug_k = jnp.where(
            row < 4,
            jnp.where(same_variate, high, nil),
            jnp.where(
                row < 8,
                jnp.where(same_variate, low, nil),
                jnp.where(
                    row == 8,
                    high,
                    jnp.where(row == 9, low, jnp.where(row < 13, far, plain)),
                ),
            ),
        )
        mine = (lane // head_size) == h
        mine_t = (row // head_size) == h
        ka_ref[h] = jnp.concatenate([jnp.where(mine, k, 0.0), aug_k.T], axis=1).astype(BF16)
        kt_ref[h] = jnp.concatenate(
            [jnp.where(mine_t, k_t, 0.0), aug_k[: ROWS_T - WIDE]], axis=0
        ).astype(BF16)
        ones_v = jnp.where((lane == h) | (lane == 2 + h), 1.0, 0.0)
        v1_ref[h] = jnp.concatenate([jnp.where(mine, v, 0.0), ones_v], axis=1).astype(BF16)


def project(x, w, norm_attn, q_gain, k_gain, lane_rows, bias, head_size, block=256):
    length, width = x.shape
    heads = bias.shape[1]
    count = lane_rows.shape[0]
    row_block = lambda cols: pl.BlockSpec((block, cols), lambda i: (i, 0))
    whole = lambda a: pl.BlockSpec(a.shape, lambda i: (0, 0))
    head_block = pl.BlockSpec((heads, block, 2 * WIDE), lambda i: (0, i, 0))
    return pl.pallas_call(
        functools.partial(qkv_kernel, heads=heads, head_size=head_size),
        grid=(length // block,),
        in_specs=[
            row_block(width), whole(w), whole(norm_attn), whole(q_gain), whole(k_gain),
            pl.BlockSpec((count, block), lambda i: (0, i)),
            pl.BlockSpec(memory_space=pltpu.SMEM),
        ],
        out_specs=[
            row_block(width), row_block(WIDE), row_block(WIDE), row_block(2 * WIDE),
            head_block, pl.BlockSpec((heads, ROWS_T, block), lambda i: (0, 0, i)), head_block,
        ],
        out_shape=[
            jax.ShapeDtypeStruct((length, width), BF16),
            jax.ShapeDtypeStruct((length, WIDE), F32),
            jax.ShapeDtypeStruct((length, WIDE), F32),
            jax.ShapeDtypeStruct((length, 2 * WIDE), BF16),
            jax.ShapeDtypeStruct((heads, length, 2 * WIDE), BF16),
            jax.ShapeDtypeStruct((heads, ROWS_T, length), BF16),
            jax.ShapeDtypeStruct((heads, length, 2 * WIDE), BF16),
        ],
        compiler_params=params(),
        cost_estimate=pl.CostEstimate(
            flops=2 * length * width * 3 * WIDE, bytes_accessed=length * width * 8, transcendentals=0
        ),
        name="project",
    )(x, w, norm_attn, q_gain, k_gain, lane_rows, bias)


def attend_kernel(qa_ref, ka_ref, v1_ref, mixed_ref, o_ref, zi_ref, *, heads, head_size, chunk):
    qa = qa_ref[...]
    length = ka_ref.shape[1]
    lane = lanes_of((qa.shape[0], WIDE))
    total = jnp.zeros((qa.shape[0], WIDE), F32)
    inverse = jnp.ones((qa.shape[0], WIDE), F32)
    for h in range(heads):
        acc = jnp.zeros((qa.shape[0], 2 * WIDE), F32)
        for c in range(length // chunk):
            part = pl.ds(c * chunk, chunk)
            e = jnp.exp2(dot_nt(qa, ka_ref[h, part, :])).astype(BF16)
            acc = acc + dot_nn(e, v1_ref[h, part, :])
        z_inv = 1.0 / acc[:, WIDE + h : WIDE + h + 1]
        total = total + acc[:, :WIDE] * z_inv
        inverse = jnp.where((lane // head_size) == h, z_inv, inverse)
    mixed_ref[...] = total.astype(BF16)
    o_ref[...] = total
    zi_ref[...] = inverse


def attend(qa, ka, v1, half, head_size, block=256, chunk=512):
    heads, length, _ = ka.shape
    rows = length // 2
    steps = rows // block
    whole = pl.BlockSpec(ka.shape, lambda i: (0, 0, 0))
    out_block = pl.BlockSpec((block, WIDE), lambda i: (i, 0))
    return pl.pallas_call(
        functools.partial(attend_kernel, heads=heads, head_size=head_size, chunk=chunk),
        grid=(steps,),
        in_specs=[
            pl.BlockSpec((block, 2 * WIDE), lambda i: (i + half * steps, 0)), whole, whole,
        ],
        out_specs=[out_block, out_block, out_block],
        out_shape=[
            jax.ShapeDtypeStruct((rows, WIDE), BF16),
            jax.ShapeDtypeStruct((rows, WIDE), F32),
            jax.ShapeDtypeStruct((rows, WIDE), F32),
        ],
        compiler_params=params(),
        cost_estimate=pl.CostEstimate(
            flops=2 * heads * rows * length * 4 * WIDE,
            bytes_accessed=length * WIDE * 16,
            transcendentals=heads * rows * length,
        ),
        name="attend",
    )(qa, ka, v1)


def attend_back_kernel(
    qa_ref, g_ref, o_ref, zi_ref, lane_ref, ka_ref, kt_ref, v1_ref,
    dq_ref, dk_ref, dv_ref, bias_ref, dk_s, dv_s, *, heads, head_size, chunk,
):
    step = pl.program_id(0)

    @pl.when(step == 0)
    def _():
        dk_s[...] = jnp.zeros_like(dk_s)
        dv_s[...] = jnp.zeros_like(dv_s)
        bias_ref[...] = jnp.zeros_like(bias_ref)

    qa = qa_ref[...]
    rows = qa.shape[0]
    length = ka_ref.shape[1]
    lane = lanes_of((rows, WIDE))
    q = qa[:, :WIDE]
    gz = (g_ref[...].astype(F32) * zi_ref[...]).astype(BF16)
    inner = gz.astype(F32) * o_ref[...]
    aug = jnp.zeros((rows, WIDE), F32)
    for h in range(heads):
        mean = -jnp.sum(
            jnp.where((lane // head_size) == h, inner, 0.0), axis=-1, keepdims=True
        ) * jnp.ones((rows, WIDE), F32)
        high = mean.astype(BF16).astype(F32)
        aug = jnp.where(lane == h, high, jnp.where(lane == 2 + h, mean - high, aug))
    ga = jnp.concatenate([gz, aug.astype(BF16)], axis=1)
    dq_t = jnp.zeros((ROWS_T, rows), F32)
    for h in range(heads):
        mine = (lane // head_size) == h
        q_h = jnp.where(mine, q, jnp.zeros_like(q))
        g_h = jnp.where(mine, gz, jnp.zeros_like(gz))
        for c in range(length // chunk):
            part = pl.ds(c * chunk, chunk)
            e = jnp.exp2(dot_nt(ka_ref[h, part, :], qa))
            ds = (e * dot_nt(v1_ref[h, part, :], ga)).astype(BF16)
            dv_s[part, :] += dot_nn(e.astype(BF16), g_h)
            dk_s[part, :] += dot_nn(ds, q_h)
            dq_t = dq_t + dot_nn(kt_ref[h, :, part], ds)
    dq_ref[...] = (dq_t[:WIDE].T * (head_size**-0.5)).astype(BF16)
    half = head_size // 2
    variate = lane_ref[2 * half : 2 * half + 1, :].astype(jnp.int32)
    columns = dq_t[WIDE + 16 : WIDE + 24]
    row = lax.broadcasted_iota(jnp.int32, columns.shape, 0)
    bias_ref[...] += jnp.concatenate(
        [jnp.where((row % 4) == variate, columns, 0.0), columns], axis=0
    )

    @pl.when(step == pl.num_programs(0) - 1)
    def _():
        dk_ref[...] = (dk_s[...] * (1.0 / LOG2E)).astype(BF16)
        dv_ref[...] = dv_s[...].astype(BF16)


def attend_back(qa, g, o, zi, lane_rows, ka, kt, v1, head_size, block=256, chunk=512):
    heads, length, _ = ka.shape
    count = lane_rows.shape[0]
    wide = pl.BlockSpec((block, WIDE), lambda i: (i, 0))
    whole = lambda a: pl.BlockSpec(a.shape, lambda i: (0,) * a.ndim)
    full = pl.BlockSpec((length, WIDE), lambda i: (0, 0))
    return pl.pallas_call(
        functools.partial(attend_back_kernel, heads=heads, head_size=head_size, chunk=chunk),
        grid=(length // block,),
        in_specs=[
            pl.BlockSpec((block, 2 * WIDE), lambda i: (i, 0)), wide, wide, wide,
            pl.BlockSpec((count, block), lambda i: (0, i)), whole(ka), whole(kt), whole(v1),
        ],
        out_specs=[wide, full, full, pl.BlockSpec((16, block), lambda i: (0, 0))],
        out_shape=[
            jax.ShapeDtypeStruct((length, WIDE), BF16),
            jax.ShapeDtypeStruct((length, WIDE), BF16),
            jax.ShapeDtypeStruct((length, WIDE), BF16),
            jax.ShapeDtypeStruct((16, block), F32),
        ],
        scratch_shapes=[pltpu.VMEM((length, WIDE), F32), pltpu.VMEM((length, WIDE), F32)],
        compiler_params=params(),
        cost_estimate=pl.CostEstimate(
            flops=2 * heads * length * length * 8 * WIDE,
            bytes_accessed=length * WIDE * 32,
            transcendentals=heads * length * length,
        ),
        name="attend_back",
    )(qa, g, o, zi, lane_rows, ka, kt, v1)


def ffn_kernel(*refs, chips, own):
    mixed = refs[: 2 * chips]
    x_ref, dout_ref, wo_ref, ws_ref, wgu_ref, wd_ref, nf_ref = refs[2 * chips : 2 * chips + 7]
    nm_ref, gnm_ref, lay_ref, inner_ref, ggu_ref, gnf_ref = refs[2 * chips + 7 : 2 * chips + 13]
    cat_own = jnp.concatenate([m[...] for m in mixed[:chips]], axis=1)
    cat_sib = jnp.concatenate([m[...] for m in mixed[chips:]], axis=1)
    hidden = wd_ref.shape[0]
    middle = x_ref[...].astype(F32) + (dot_nn(cat_own, wo_ref[...]) + dot_nn(cat_sib, ws_ref[...]))
    factor = rms_factor(middle)
    scaled = middle * factor
    nm = (scaled * nf_ref[...]).astype(BF16)
    nm_ref[...] = nm
    lin = dot_nn(nm, wgu_ref[...])
    gate, up = lin[:, :hidden], lin[:, hidden:]
    sig = jax.nn.sigmoid(gate)
    silu = gate * sig
    inner = (silu * up).astype(BF16)
    inner_ref[...] = inner
    lay_ref[...] = dot_nn(inner, wd_ref[...]).astype(BF16)
    back = dot_nt(dout_ref[...], wd_ref[...])
    g_gate = (back * up * (sig * (1.0 + gate * (1.0 - sig)))).astype(BF16)
    g_up = (back * silu).astype(BF16)
    ggu = jnp.concatenate([g_gate, g_up], axis=1)
    ggu_ref[...] = ggu
    gnm = dot_nt(ggu, wgu_ref[...])
    gnm_ref[...] = gnm.astype(BF16)

    @pl.when(pl.program_id(0) == 0)
    def _():
        gnf_ref[...] = jnp.zeros_like(gnf_ref)
        if own:
            refs[2 * chips + 13][...] = middle
            refs[2 * chips + 14][...] = jnp.concatenate([cat_own, cat_sib], axis=1)

    gnf_ref[...] += jnp.sum(gnm * scaled, axis=0, keepdims=True)


def ffn(own_parts, sib_parts, x, dout, wo_own, wo_sib, wgu, wd, norm_ffn, half, chips):
    length, width = x.shape
    rows = length // 2
    block = rows // chips
    hidden = wd.shape[0]
    own = half == 0
    base = half * chips
    row_in = pl.BlockSpec((block, width), lambda i: (i + base, 0))
    row_out = lambda cols: pl.BlockSpec((block, cols), lambda i: (i, 0))
    whole = lambda a: pl.BlockSpec(a.shape, lambda i: (0, 0))
    piece = lambda r: pl.BlockSpec((block, WIDE), lambda i: (i ^ r, 0))
    out_specs = [
        row_out(width), row_out(width), row_out(width), row_out(hidden), row_out(2 * hidden),
        pl.BlockSpec((1, width), lambda i: (0, 0)),
    ]
    out_shape = [
        jax.ShapeDtypeStruct((rows, width), BF16),
        jax.ShapeDtypeStruct((rows, width), BF16),
        jax.ShapeDtypeStruct((rows, width), BF16),
        jax.ShapeDtypeStruct((rows, hidden), BF16),
        jax.ShapeDtypeStruct((rows, 2 * hidden), BF16),
        jax.ShapeDtypeStruct((1, width), F32),
    ]
    if own:
        out_specs += [
            pl.BlockSpec((block, width), lambda i: (0, 0)),
            pl.BlockSpec((block, 2 * chips * WIDE), lambda i: (0, 0)),
        ]
        out_shape += [
            jax.ShapeDtypeStruct((block, width), F32),
            jax.ShapeDtypeStruct((block, 2 * chips * WIDE), BF16),
        ]
    return pl.pallas_call(
        functools.partial(ffn_kernel, chips=chips, own=own),
        grid=(chips,),
        in_specs=[piece(r) for r in range(chips)] * 2
        + [row_in, row_in, whole(wo_own), whole(wo_sib), whole(wgu), whole(wd), whole(norm_ffn)],
        out_specs=out_specs,
        out_shape=out_shape,
        compiler_params=params(),
        cost_estimate=pl.CostEstimate(
            flops=2 * rows * width * (2 * chips * WIDE + 6 * hidden),
            bytes_accessed=rows * width * 12,
            transcendentals=rows * hidden,
        ),
        name="ffn_half",
    )(*own_parts, *sib_parts, x, dout, wo_own, wo_sib, wgu, wd, norm_ffn)


def middle_back_kernel(*refs, chips):
    pieces = refs[:chips]
    mid_ref, dout_ref, nf_ref, wo_ref, ws_ref = refs[chips : chips + 5]
    gm_ref, gb_ref, go_ref, gs_ref = refs[chips + 5 :]
    incoming = pieces[0][...].astype(F32)
    for piece in pieces[1:]:
        incoming = incoming + piece[...].astype(F32)
    middle = mid_ref[...]
    factor = rms_factor(middle)
    weighted = incoming * nf_ref[...]
    grad = (
        dout_ref[...].astype(F32)
        + factor * weighted
        - middle * (factor * factor * factor) * jnp.mean(weighted * middle, axis=-1, keepdims=True)
    )
    gm_ref[...] = grad
    branch = grad.astype(BF16)
    gb_ref[...] = branch
    for r in range(chips):
        part = pl.ds(r * WIDE, WIDE)
        go_ref[r] = dot_nt(branch, wo_ref[part, :]).astype(BF16)
        gs_ref[r] = dot_nt(branch, ws_ref[part, :]).astype(BF16)


def middle_back(pieces, middle, dout, norm_ffn, wo_own, wo_sib):
    chips = len(pieces)
    rows, width = middle.shape
    return pl.pallas_call(
        functools.partial(middle_back_kernel, chips=chips),
        out_shape=[
            jax.ShapeDtypeStruct((rows, width), F32),
            jax.ShapeDtypeStruct((rows, width), BF16),
            jax.ShapeDtypeStruct((chips, rows, WIDE), BF16),
            jax.ShapeDtypeStruct((chips, rows, WIDE), BF16),
        ],
        compiler_params=pltpu.CompilerParams(vmem_limit_bytes=60 * 1024 * 1024),
        cost_estimate=pl.CostEstimate(
            flops=2 * rows * width * 2 * chips * WIDE, bytes_accessed=rows * width * 12, transcendentals=0
        ),
        name="middle_back",
    )(*pieces, middle, dout, norm_ffn, wo_own, wo_sib)


def input_back_kernel(*refs, chips):
    pieces = refs[:chips]
    x_ref, gm_ref, na_ref, out_ref = refs[chips:]
    incoming = pieces[0][...].astype(F32)
    for piece in pieces[1:]:
        incoming = incoming + piece[...].astype(F32)
    x = x_ref[...].astype(F32)
    factor = rms_factor(x)
    weighted = incoming * na_ref[...]
    out_ref[...] = (
        gm_ref[...]
        + factor * weighted
        - x * (factor * factor * factor) * jnp.mean(weighted * x, axis=-1, keepdims=True)
    )


def input_back(pieces, x, grad_middle, norm_attn):
    chips = len(pieces)
    return pl.pallas_call(
        functools.partial(input_back_kernel, chips=chips),
        out_shape=jax.ShapeDtypeStruct(x.shape, F32),
        compiler_params=pltpu.CompilerParams(vmem_limit_bytes=60 * 1024 * 1024),
        name="input_back",
    )(*pieces, x, grad_middle, norm_attn)


def qkv_back_kernel(
    dq_ref, dk_ref, dv_ref, qlin_ref, klin_ref, lane_ref, w_ref, x_ref, qg_ref, kg_ref,
    gni_ref, gl_ref, gain_ref, gna_ref, *, head_size,
):
    half = head_size // 2
    rows = x_ref.shape[0]
    lane = lanes_of((rows, WIDE))
    cosine, sine = tables(lane_ref, half)

    @pl.when(pl.program_id(0) == 0)
    def _():
        gain_ref[...] = jnp.zeros_like(gain_ref)
        gna_ref[...] = jnp.zeros_like(gna_ref)

    def back(grad, u, gain, at):
        grad = grad.astype(F32)
        grad = grad * cosine - partner(grad, lane, head_size) * sine
        factor = lax.rsqrt(head_sum(u * u, lane, head_size) * (1.0 / head_size) + EPSILON)
        gain_ref[at : at + 1, :] += jnp.sum(grad * u * factor, axis=0, keepdims=True)
        weighted = grad * gain
        mean = head_sum(weighted * u, lane, head_size) * (1.0 / head_size)
        return (factor * weighted - u * (factor * factor * factor) * mean).astype(BF16)

    gq = back(dq_ref[...], qlin_ref[...], qg_ref[...], 0)
    gk = back(dk_ref[...], klin_ref[...], kg_ref[...], 1)
    gl = jnp.concatenate([gq, gk, dv_ref[...]], axis=1)
    gl_ref[...] = gl
    gni = dot_nt(gl, w_ref[...])
    gni_ref[...] = gni.astype(BF16)
    x = x_ref[...].astype(F32)
    gna_ref[...] += jnp.sum(gni * x * rms_factor(x), axis=0, keepdims=True)


def qkv_back(dq, dk, dv, qlin, klin, lane_rows, w, x, q_gain, k_gain, head_size, half, block=256):
    length, width = x.shape
    count = lane_rows.shape[0]
    rows = length // 2
    base = half * (rows // block)
    row_in = lambda cols: pl.BlockSpec((block, cols), lambda i: (i + base, 0))
    row_out = lambda cols: pl.BlockSpec((block, cols), lambda i: (i, 0))
    whole = lambda a: pl.BlockSpec(a.shape, lambda i: (0, 0))
    return pl.pallas_call(
        functools.partial(qkv_back_kernel, head_size=head_size),
        grid=(rows // block,),
        in_specs=[row_in(WIDE)] * 5
        + [
            pl.BlockSpec((count, block), lambda i: (0, i + base)), whole(w), row_in(width),
            whole(q_gain), whole(k_gain),
        ],
        out_specs=[
            row_out(width), row_out(3 * WIDE),
            pl.BlockSpec((8, WIDE), lambda i: (0, 0)), pl.BlockSpec((1, width), lambda i: (0, 0)),
        ],
        out_shape=[
            jax.ShapeDtypeStruct((rows, width), BF16),
            jax.ShapeDtypeStruct((rows, 3 * WIDE), BF16),
            jax.ShapeDtypeStruct((8, WIDE), F32),
            jax.ShapeDtypeStruct((1, width), F32),
        ],
        compiler_params=params(),
        cost_estimate=pl.CostEstimate(
            flops=2 * rows * width * 3 * WIDE, bytes_accessed=rows * width * 6, transcendentals=0
        ),
        name="qkv_back",
    )(dq, dk, dv, qlin, klin, lane_rows, w, x, q_gain, k_gain)


def swap(x, seq_count, bits):
    return lax.ppermute(x, "seq", [(i, i ^ bits) for i in range(seq_count)])


def to_chips(x, seq_count):
    return [x] + [swap(x, seq_count, 2 * r) for r in range(1, seq_count // 2)]


def gather_plane(x, seq_count):
    own = jnp.concatenate(to_chips(x, seq_count), axis=0)
    return own, swap(own, seq_count, 1)


def scatter_plane(own, sib, seq_count):
    chips = seq_count // 2
    got = swap(sib, seq_count, 1)
    both = (own.astype(F32) + got.astype(F32)).astype(BF16)
    rows = both.shape[0] // chips
    parts = [both[r * rows : (r + 1) * rows] for r in range(chips)]
    return [parts[0]] + [swap(parts[r], seq_count, 2 * r) for r in range(1, chips)]


def add_up(parts):
    total = parts[0].astype(F32)
    for part in parts[1:]:
        total = total + part.astype(F32)
    return total


def body(
    tokens, weight_query, weight_key, weight_value, weight_out, weight_gate, weight_up, weight_down,
    norm_attn, norm_ffn, query_gain, key_gain, variate_bias, variate_ids, sample_ids, time_ids,
    out_grad,
):
    seq_count = lax.axis_size("seq")
    z_count = lax.axis_size("fsdp")
    chips = seq_count // 2
    _, rows_dev, width = tokens.shape
    heads = variate_bias.shape[1]
    head_size = query_gain.shape[0]
    half_size = head_size // 2
    length = rows_dev * seq_count
    half_rows = length // 2
    shard = weight_query.shape[0]
    features = heads * head_size
    hidden = weight_gate.shape[1] // seq_count
    x_own = tokens.reshape(rows_dev, width)
    dout_own = out_grad.reshape(rows_dev, width)

    lanes_pad = ((0, 0), (0, 0), (0, WIDE - features))
    columns = jnp.concatenate(
        [
            jnp.pad(w.reshape(shard, seq_count, features), lanes_pad)
            for w in (weight_query, weight_key, weight_value)
        ],
        axis=2,
    )
    columns = jnp.broadcast_to(
        columns.transpose(1, 0, 2)[:, None], (seq_count, z_count, shard, 3 * WIDE)
    ).reshape(seq_count * z_count, shard, 3 * WIDE)
    w_qkv = lax.all_to_all(
        columns, ("seq", "fsdp"), split_axis=0, concat_axis=0, tiled=True
    ).reshape(width, 3 * WIDE)
    x_halves = gather_plane(x_own, seq_count)

    down_out = lax.all_gather(
        jnp.concatenate([weight_down, weight_out], axis=0), "fsdp", axis=0, tiled=False
    )
    w_down = down_out[:, : weight_down.shape[0]].reshape(hidden, width)
    w_out_rows = down_out[:, weight_down.shape[0] :].reshape(features, width)
    if features < WIDE:
        w_out_rows = jnp.pad(w_out_rows, ((0, WIDE - features), (0, 0)))
    gate_up = jnp.concatenate(
        [w.reshape(shard, seq_count, hidden) for w in (weight_gate, weight_up)], axis=2
    ).transpose(1, 0, 2)
    gate_up = lax.all_to_all(gate_up, "seq", split_axis=0, concat_axis=0, tiled=True)
    w_gu = (
        lax.all_gather(gate_up, "fsdp", axis=0, tiled=False)
        .transpose(1, 0, 2, 3)
        .reshape(width, 2 * hidden)
    )

    ids = lax.all_gather(
        jnp.concatenate([variate_ids, sample_ids, time_ids], axis=0), "seq", axis=0, tiled=False
    )
    me = lax.axis_index("seq")
    order = jnp.concatenate([me ^ (2 * jnp.arange(chips)), me ^ (2 * jnp.arange(chips) + 1)])
    ids = ids[order].transpose(1, 0, 2).reshape(3, length).astype(F32)
    frequency = 10000.0 ** (-2.0 * jnp.arange(half_size).astype(F32) / head_size)
    angles = frequency[:, None] * ids[2][None, :]
    lane_rows = jnp.concatenate(
        [jnp.cos(angles), jnp.sin(angles), ids[:2], jnp.zeros((6, length), F32)], axis=0
    )

    gain_attn = norm_attn.reshape(1, width)
    gain_ffn = norm_ffn.reshape(1, width)
    q_gain = jnp.tile(query_gain, WIDE // head_size).reshape(1, WIDE)
    k_gain = jnp.tile(key_gain, WIDE // head_size).reshape(1, WIDE)

    x_all = jnp.concatenate(x_halves, axis=0)
    normed_in, q_lin, k_lin, q_aug, k_aug, k_trans, v_aug = project(
        x_all, w_qkv, gain_attn, q_gain, k_gain, lane_rows, variate_bias, head_size
    )
    dout_all = jnp.concatenate(gather_plane(dout_own, seq_count), axis=0)
    wo_own, wo_sib = gather_plane(w_out_rows, seq_count)

    mixed, mixed_full, z_inverse = zip(
        *[attend(q_aug, k_aug, v_aug, half, head_size) for half in (0, 1)]
    )
    own_parts = [to_chips(mixed[half], seq_count) for half in (0, 1)]
    sib_stack = [swap(jnp.concatenate(own_parts[half], axis=0), seq_count, 1) for half in (0, 1)]
    sib_parts = [
        [sib_stack[1 - half][r * half_rows : (r + 1) * half_rows] for r in range(chips)]
        for half in (0, 1)
    ]
    o_all = jnp.concatenate(mixed_full, axis=0)
    zi_all = jnp.concatenate(z_inverse, axis=0)

    far = ffn(
        own_parts[1], sib_parts[1], x_all, dout_all, wo_own, wo_sib, w_gu, w_down, gain_ffn, 1, chips
    )
    near = ffn(
        own_parts[0], sib_parts[0], x_all, dout_all, wo_own, wo_sib, w_gu, w_down, gain_ffn, 0, chips
    )
    nm_near, gnm_near, lay_near, inner_near, ggu_near, gnf_near, middle, mixed_own = near
    nm_far, gnm_far, lay_far, inner_far, ggu_far, gnf_far = far

    gnm_parts = scatter_plane(gnm_near, gnm_far, seq_count)
    grad_middle, grad_branch, gm_own, gm_sib = middle_back(
        gnm_parts, middle, dout_own, gain_ffn, wo_own, wo_sib
    )
    gm_got = swap(gm_sib, seq_count, 1)
    gm_pairs = jnp.stack([gm_own, gm_got], axis=1)
    gm_here = [gm_pairs[0]] + [swap(gm_pairs[r], seq_count, 2 * r) for r in range(1, chips)]
    g_all = jnp.concatenate([p[0] for p in gm_here] + [p[1] for p in gm_here], axis=0)

    grad_gu = (dot_tn(nm_near, ggu_near) + dot_tn(nm_far, ggu_far)).astype(BF16)
    grad_gu = grad_gu.reshape(seq_count, z_count, shard, 2 * hidden).transpose(1, 0, 2, 3)
    grad_gu = lax.psum_scatter(
        grad_gu.reshape(width, 2 * hidden), "fsdp", scatter_dimension=0, tiled=True
    ).reshape(seq_count, shard, 2 * hidden)
    grad_gu = lax.all_to_all(grad_gu, "seq", split_axis=0, concat_axis=0, tiled=True)
    grad_gu = grad_gu.transpose(1, 0, 2).astype(F32)
    grad_gate = grad_gu[:, :, :hidden].reshape(shard, seq_count * hidden)
    grad_up = grad_gu[:, :, hidden:].reshape(shard, seq_count * hidden)

    dout_near, dout_far = dout_all[:half_rows], dout_all[half_rows:]
    grad_down = (dot_tn(inner_near, dout_near) + dot_tn(inner_far, dout_far)).astype(BF16)
    grad_out = dot_tn(mixed_own, grad_branch).astype(BF16)
    grad_out = add_up(
        scatter_plane(grad_out[: chips * WIDE], grad_out[chips * WIDE :], seq_count)
    ).astype(BF16)[:features]
    down_out = jnp.concatenate(
        [
            grad_down.reshape(z_count, hidden // z_count, width),
            grad_out.reshape(z_count, features // z_count, width),
        ],
        axis=1,
    )
    down_out = lax.psum_scatter(down_out, "fsdp", scatter_dimension=0, tiled=False).astype(F32)
    grad_down = down_out[: hidden // z_count]
    grad_out = down_out[hidden // z_count :]
    layer_out = (middle + add_up(scatter_plane(lay_near, lay_far, seq_count))).astype(BF16)

    dq, dk, dv, bias_rows = attend_back(
        q_aug, g_all, o_all, zi_all, lane_rows, k_aug, k_trans, v_aug, head_size
    )
    back = [
        qkv_back(dq, dk, dv, q_lin, k_lin, lane_rows, w_qkv, x_all, q_gain, k_gain, head_size, half)
        for half in (0, 1)
    ]
    gni_parts = scatter_plane(back[0][0], back[1][0], seq_count)
    in_grad = input_back(gni_parts, x_own, grad_middle, gain_attn)
    grad_qkv = (
        dot_tn(normed_in[:half_rows], back[0][1]) + dot_tn(normed_in[half_rows:], back[1][1])
    ).astype(BF16)
    grad_qkv = lax.all_to_all(
        grad_qkv.reshape(seq_count * z_count, shard, 3 * WIDE),
        ("seq", "fsdp"), split_axis=0, concat_axis=0, tiled=True,
    ).reshape(seq_count, z_count, shard, 3 * WIDE)
    grad_qkv = jnp.sum(grad_qkv.astype(F32), axis=1).transpose(1, 0, 2)
    grad_query, grad_key, grad_value = (
        grad_qkv[:, :, i * WIDE : i * WIDE + features].reshape(shard, width) for i in range(3)
    )

    gain_rows = back[0][2] + back[1][2]
    grad_qk_gain = gain_rows[:2, :features].reshape(2, heads, head_size).sum(axis=1)
    bias_cols = jnp.sum(bias_rows, axis=1).reshape(2, 2, 4).sum(axis=2)[:, :heads]
    bias_both = jnp.stack([bias_cols[0], bias_cols[1] - bias_cols[0]])
    spread = lax.dynamic_update_slice(
        jnp.zeros((2, heads * seq_count), F32), bias_both, (0, me * heads)
    )
    small = jnp.concatenate(
        [
            (back[0][3] + back[1][3]).reshape(-1),
            (gnf_near + gnf_far).reshape(-1),
            grad_qk_gain.reshape(-1),
            spread.reshape(-1),
        ]
    )
    small = lax.psum(small, ("seq", "fsdp"))
    cut = 2 * width + 2 * head_size
    grad_bias = lax.dynamic_slice(
        small[cut:].reshape(2, heads * seq_count), (0, me * heads), (2, heads)
    )
    return (
        layer_out.reshape(tokens.shape),
        in_grad.reshape(tokens.shape),
        grad_query,
        grad_key,
        grad_value,
        grad_out,
        grad_gate,
        grad_up,
        grad_down,
        small[:width],
        small[width : 2 * width],
        small[2 * width : 2 * width + head_size],
        small[2 * width + head_size : cut],
        grad_bias,
    )


def solution(mesh):
    rows = P("fsdp", "seq", None)
    shards = P(("seq", "fsdp"), None)
    ids = P("fsdp", "seq")
    bias = P(None, "seq")
    return jax.shard_map(
        body,
        mesh=mesh,
        in_specs=(rows,) + (shards,) * 7 + (P(),) * 4 + (bias, ids, ids, ids, rows),
        out_specs=(rows, rows) + (shards,) * 7 + (P(),) * 4 + (bias,),
        check_vma=False,
    )
```

```python
import functools
import math

import jax
import jax.numpy as jnp
from jax import lax
from jax.experimental import pallas as pl
from jax.experimental.pallas import tpu as pltpu
from jax.sharding import PartitionSpec as P

EPSILON = 1e-06
FAR = -1e30
LOG2E = math.log2(math.e)
WIDE = 128
ROWS_T = 160
F32 = jnp.float32
BF16 = jnp.bfloat16


def dot_nn(left, right):
    return jnp.dot(left, right, preferred_element_type=F32)


def dot_nt(left, right):
    return lax.dot_general(left, right, (((1,), (1,)), ((), ())), preferred_element_type=F32)


def dot_tn(left, right):
    return lax.dot_general(left, right, (((0,), (0,)), ((), ())), preferred_element_type=F32)


def rms_factor(values):
    return lax.rsqrt(jnp.mean(values * values, axis=-1, keepdims=True) + EPSILON)


def lanes_of(shape):
    return lax.broadcasted_iota(jnp.int32, shape, len(shape) - 1)


def head_sum(values, blocks):
    high = values.astype(BF16)
    low = (values - high.astype(F32)).astype(BF16)
    return dot_nn(high, blocks) + dot_nn(low, blocks)


def head_blocks(head_size):
    row = lax.broadcasted_iota(jnp.int32, (WIDE, WIDE), 0) // head_size
    column = lax.broadcasted_iota(jnp.int32, (WIDE, WIDE), 1) // head_size
    return jnp.where(row == column, 1.0, 0.0).astype(BF16)


def partner(values, lane, head_size):
    half = head_size // 2
    up = pltpu.roll(values, WIDE - half, 1)
    down = pltpu.roll(values, half, 1)
    return jnp.where(lane % head_size < half, up, down)


def tables(cosine, sine):
    times = WIDE // (2 * cosine.shape[0])
    cos_rows = jnp.concatenate([cosine, cosine] * times, axis=0)
    sin_rows = jnp.concatenate([-sine, sine] * times, axis=0)
    return cos_rows.T, sin_rows.T


def params(grid=True):
    return pltpu.CompilerParams(
        vmem_limit_bytes=60 * 1024 * 1024,
        dimension_semantics=("arbitrary",) if grid else None,
    )


def whole(array):
    return pl.BlockSpec(array.shape, lambda *_: (0,) * len(array.shape))


def shaped(shape, dtype):
    return jax.ShapeDtypeStruct(shape, dtype)


ANY = pl.BlockSpec(memory_space=pl.ANY)


def assemble(out_ref, in_ref):
    if len(in_ref.shape) == 2:
        out_ref[...] = in_ref[...]
        return
    z_count, seq_count, shard, _ = in_ref.shape
    for f in range(z_count):
        for s in range(seq_count):
            at = (s * z_count + f) * shard
            out_ref[at : at + shard, :] = in_ref[f, s]


def gathered(w):
    if w.shape[2] % 16 == 0:
        return w
    return w.transpose(1, 0, 2, 3).reshape(-1, w.shape[-1])


def columns_kernel(*refs):
    *weights, out_ref = refs
    at = 0
    for w_ref in weights:
        wide = w_ref.shape[1] // out_ref.shape[0]
        for s in range(out_ref.shape[0]):
            out_ref[s, :, at : at + wide] = w_ref[:, s * wide : (s + 1) * wide]
        at += wide


def columns_by_device(weights, seq_count):
    shard = weights[0].shape[0]
    wides = [w.shape[1] // seq_count for w in weights]
    if shard % 16 == 0 and all(wide % WIDE == 0 for wide in wides):
        return pl.pallas_call(
            columns_kernel,
            out_shape=shaped((seq_count, shard, sum(wides)), BF16),
            compiler_params=params(False),
            name="columns",
        )(*weights)
    pieces = []
    for w, wide in zip(weights, wides):
        short = -wide % WIDE
        pieces.append(jnp.pad(w.reshape(shard, seq_count, wide), ((0, 0), (0, 0), (0, short))))
    return jnp.concatenate(pieces, axis=2).transpose(1, 0, 2)


def project_kernel(
    x_ref, w_ref, na_ref, qg_ref, kg_ref, freq_ref, bias_ref,
    nin_ref, qlin_ref, klin_ref, lane_ref, qa_ref, ka_ref, kt_ref, v1_ref, w_s, *, heads, head_size,
):
    half = head_size // 2
    rows = nin_ref.shape[0]

    @pl.when(pl.program_id(0) == 0)
    def _():
        assemble(w_s, w_ref)

    x = x_ref[:rows, :].astype(F32)
    ids = x_ref[rows:, :rows].astype(F32)
    nin = (x * rms_factor(x) * na_ref[...]).astype(BF16)
    nin_ref[...] = nin
    lin = dot_nn(nin, w_s[...])
    q, k, v = lin[:, :WIDE], lin[:, WIDE : 2 * WIDE], lin[:, 2 * WIDE :]
    qlin_ref[...] = q
    klin_ref[...] = k
    angles = freq_ref[...] * (ids[2:3] * 64.0 + ids[3:4])
    cosine, sine = jnp.cos(angles), jnp.sin(angles)
    lane_ref[...] = jnp.concatenate([cosine, sine, ids[:8]], axis=0)
    cosine, sine = tables(cosine, sine)
    lane = lanes_of((rows, WIDE))
    blocks = head_blocks(head_size)

    def finish(u, gain):
        factor = lax.rsqrt(head_sum(u * u, blocks) * (1.0 / head_size) + EPSILON)
        u = u * factor * gain
        return u * cosine + partner(u, lane, head_size) * sine

    q = finish(q, qg_ref[...]) * (LOG2E * head_size**-0.5)
    k = finish(k, kg_ref[...])
    few = ROWS_T - WIDE
    row = lax.broadcasted_iota(jnp.int32, (few, rows), 0)
    variate = ids[0:1].astype(jnp.int32)
    sample = ids[1:2].astype(jnp.int32)
    same_variate = (row % 4) == variate
    same_sample = (row - 10) == sample
    one = jnp.ones((few, rows), F32)
    nil = jnp.zeros((few, rows), F32)
    rest = jnp.zeros((WIDE - few, rows), F32)

    def columns(few_rows):
        return jnp.concatenate([few_rows, rest], axis=0).T

    aug_q = jnp.where(
        row < 8,
        jnp.where(same_variate, one, nil),
        jnp.where(row < 10, one, jnp.where((row < 13) & same_sample, one, nil)),
    )
    qa_ref[...] = jnp.concatenate([q, columns(aug_q)], axis=1).astype(BF16)
    k_t = k.T
    row_k = lax.broadcasted_iota(jnp.int32, (WIDE, rows), 0)
    for h in range(heads):
        first, second = bias_ref[0, h] * LOG2E, bias_ref[1, h] * LOG2E
        step_up = jnp.where(row < 8, first - second, second) * one
        high = step_up.astype(BF16).astype(F32)
        low = step_up - high
        far = jnp.where(same_sample, nil, FAR)
        plain = jnp.where(((row // 4) == 4 + h) & same_variate, one, nil)
        aug_k = jnp.where(
            row < 4,
            jnp.where(same_variate, high, nil),
            jnp.where(
                row < 8,
                jnp.where(same_variate, low, nil),
                jnp.where(
                    row == 8,
                    high,
                    jnp.where(row == 9, low, jnp.where(row < 13, far, plain)),
                ),
            ),
        )
        mine = (lane // head_size) == h
        mine_t = (row_k // head_size) == h
        ka_ref[h] = jnp.concatenate([jnp.where(mine, k, 0.0), columns(aug_k)], axis=1).astype(BF16)
        kt_ref[h] = jnp.concatenate([jnp.where(mine_t, k_t, 0.0), aug_k], axis=0).astype(BF16)
        ones_v = jnp.where((lane == h) | (lane == 2 + h), 1.0, 0.0)
        v1_ref[h] = jnp.concatenate([jnp.where(mine, v, 0.0), ones_v], axis=1).astype(BF16)


def project(x, chips, w, norm_attn, q_gain, k_gain, freq, bias, head_size):
    width, wide = x.shape[1], w.shape[-1]
    rows = x.shape[0] // chips - 16
    heads = bias.shape[1]
    half = chips * rows
    count = head_size + 8
    row_block = lambda cols: pl.BlockSpec((rows, cols), lambda i: (i, 0))
    lane_block = pl.BlockSpec((count, rows), lambda i: (0, i))
    head_block = pl.BlockSpec((heads, rows, 2 * WIDE), lambda i: (0, i, 0))
    return pl.pallas_call(
        functools.partial(project_kernel, heads=heads, head_size=head_size),
        grid=(chips,),
        in_specs=[pl.BlockSpec((rows + 16, width), lambda i: (i, 0))]
        + [whole(a) for a in (w, norm_attn, q_gain, k_gain, freq)]
        + [pl.BlockSpec(memory_space=pltpu.SMEM)],
        out_specs=[
            row_block(width), row_block(WIDE), row_block(WIDE), lane_block, row_block(2 * WIDE),
            head_block, pl.BlockSpec((heads, ROWS_T, rows), lambda i: (0, 0, i)), head_block,
        ],
        out_shape=[
            shaped((half, width), BF16),
            shaped((half, WIDE), F32),
            shaped((half, WIDE), F32),
            shaped((count, half), F32),
            shaped((half, 2 * WIDE), BF16),
            shaped((heads, half, 2 * WIDE), BF16),
            shaped((heads, ROWS_T, half), BF16),
            shaped((heads, half, 2 * WIDE), BF16),
        ],
        scratch_shapes=[pltpu.VMEM((width, wide), BF16)],
        compiler_params=params(),
        cost_estimate=pl.CostEstimate(
            flops=2 * half * width * 3 * WIDE, bytes_accessed=half * width * 8, transcendentals=0
        ),
        name="project",
    )(x, w, norm_attn, q_gain, k_gain, freq, bias)


def attend_kernel(qa_ref, ka0, ka1, v10, v11, mixed_ref, o_ref, zi_ref, *, heads, head_size, chunk):
    qa = qa_ref[...]
    rows = qa.shape[0]
    half = ka0.shape[1]
    lane = lanes_of((rows, WIDE))
    total = jnp.zeros((rows, WIDE), F32)
    inverse = jnp.ones((rows, WIDE), F32)
    for h in range(heads):
        acc = jnp.zeros((rows, 2 * WIDE), F32)
        for ka_ref, v1_ref in ((ka0, v10), (ka1, v11)):
            for c in range(half // chunk):
                part = pl.ds(c * chunk, chunk)
                e = jnp.exp2(dot_nt(qa, ka_ref[h, part, :])).astype(BF16)
                acc = acc + dot_nn(e, v1_ref[h, part, :])
        z_inv = 1.0 / acc[:, WIDE + h : WIDE + h + 1]
        total = total + acc[:, :WIDE] * z_inv
        inverse = jnp.where((lane // head_size) == h, z_inv, inverse)
    mixed_ref[...] = total.astype(BF16)
    o_ref[...] = total
    zi_ref[...] = inverse


def attend(qa, ka, v1, head_size, block=512, chunk=256):
    heads, half, _ = ka[0].shape
    out_block = pl.BlockSpec((block, WIDE), lambda i: (i, 0))
    return pl.pallas_call(
        functools.partial(attend_kernel, heads=heads, head_size=head_size, chunk=chunk),
        grid=(half // block,),
        in_specs=[pl.BlockSpec((block, 2 * WIDE), lambda i: (i, 0))]
        + [whole(a) for a in (*ka, *v1)],
        out_specs=[out_block, out_block, out_block],
        out_shape=[shaped((half, WIDE), BF16), shaped((half, WIDE), F32), shaped((half, WIDE), F32)],
        compiler_params=params(),
        cost_estimate=pl.CostEstimate(
            flops=2 * heads * half * half * 8 * WIDE,
            bytes_accessed=half * WIDE * 32,
            transcendentals=2 * heads * half * half,
        ),
        name="attend",
    )(qa, *ka, *v1)


def attend_back_kernel(*refs, chips, heads, head_size, chunk):
    me_ref, g_ref = refs[:2]
    at = 2
    qa, o, zi, lanes, ka, kt, v1 = [refs[at + 2 * n : at + 2 * n + 2] for n in range(7)]
    at += 14
    dq_refs = refs[at : at + 2]
    dk_ref, dv_ref, bias_ref, g_s, dk_s, dv_s = refs[at + 2 :]
    step = pl.program_id(0)

    @pl.when(step == 0)
    def _():
        dk_s[...] = jnp.zeros_like(dk_s)
        dv_s[...] = jnp.zeros_like(dv_s)
        bias_ref[...] = jnp.zeros_like(bias_ref)
        for j in range(2 * chips):
            g_s[j % 2, j // 2] = g_ref[me_ref[0] ^ j]

    for side in range(2):
        q_rows = qa[side][...]
        rows = q_rows.shape[0]
        half_len = ka[0].shape[1]
        lane = lanes_of((rows, WIDE))
        q = q_rows[:, :WIDE]
        gz = (g_s[side, step].astype(F32) * zi[side][...]).astype(BF16)
        inner = gz.astype(F32) * o[side][...]
        aug = jnp.zeros((rows, WIDE), F32)
        for h in range(heads):
            mean = -jnp.sum(
                jnp.where((lane // head_size) == h, inner, 0.0), axis=-1, keepdims=True
            ) * jnp.ones((rows, WIDE), F32)
            high = mean.astype(BF16).astype(F32)
            aug = jnp.where(lane == h, high, jnp.where(lane == 2 + h, mean - high, aug))
        ga = jnp.concatenate([gz, aug.astype(BF16)], axis=1)
        dq_t = jnp.zeros((ROWS_T, rows), F32)
        for h in range(heads):
            mine = (lane // head_size) == h
            q_h = jnp.where(mine, q, jnp.zeros_like(q))
            g_h = jnp.where(mine, gz, jnp.zeros_like(gz))
            for other in range(2):
                for c in range(half_len // chunk):
                    part = pl.ds(c * chunk, chunk)
                    e = jnp.exp2(dot_nt(ka[other][h, part, :], q_rows))
                    ds = (e * dot_nt(v1[other][h, part, :], ga)).astype(BF16)
                    dv_s[other, part, :] += dot_nn(e.astype(BF16), g_h)
                    dk_s[other, part, :] += dot_nn(ds, q_h)
                    dq_t = dq_t + dot_nn(kt[other][h, :, part], ds)
        dq_refs[side][...] = (dq_t[:WIDE].T * (head_size**-0.5)).astype(BF16)
        variate = lanes[side][head_size : head_size + 1, :].astype(jnp.int32)
        columns = dq_t[WIDE + 16 : WIDE + 24]
        row = lax.broadcasted_iota(jnp.int32, columns.shape, 0)
        bias_ref[...] += jnp.concatenate(
            [jnp.where((row % 4) == variate, columns, 0.0), columns], axis=0
        )

    @pl.when(step == pl.num_programs(0) - 1)
    def _():
        dk_ref[...] = (dk_s[...] * (1.0 / LOG2E)).astype(BF16)
        dv_ref[...] = dv_s[...].astype(BF16)


def attend_back(me, g, qa, o, zi, lane_rows, ka, kt, v1, head_size, chunk=1024):
    heads, half, _ = ka[0].shape
    chips = g.shape[0] // 2
    chunk = math.gcd(half, chunk)
    block = half // chips
    count = lane_rows[0].shape[0]
    row_block = lambda cols: pl.BlockSpec((block, cols), lambda i: (i, 0))
    lane_block = pl.BlockSpec((count, block), lambda i: (0, i))
    full = shaped((2, half, WIDE), BF16)
    return pl.pallas_call(
        functools.partial(
            attend_back_kernel, chips=chips, heads=heads, head_size=head_size, chunk=chunk
        ),
        grid=(chips,),
        in_specs=[pl.BlockSpec(memory_space=pltpu.SMEM), whole(g)]
        + [row_block(2 * WIDE)] * 2
        + [row_block(WIDE)] * 4
        + [lane_block] * 2
        + [whole(a) for a in (*ka, *kt, *v1)],
        out_specs=[row_block(WIDE)] * 2
        + [whole(full), whole(full), pl.BlockSpec((16, block), lambda i: (0, 0))],
        out_shape=[shaped((half, WIDE), BF16)] * 2 + [full, full, shaped((16, block), F32)],
        scratch_shapes=[
            pltpu.VMEM((2, chips, block, WIDE), BF16),
            pltpu.VMEM((2, half, WIDE), F32),
            pltpu.VMEM((2, half, WIDE), F32),
        ],
        compiler_params=params(),
        cost_estimate=pl.CostEstimate(
            flops=2 * heads * half * half * 32 * WIDE,
            bytes_accessed=half * WIDE * 64,
            transcendentals=4 * heads * half * half,
        ),
        name="attend_back",
    )(me, g, *qa, *o, *zi, *lane_rows, *ka, *kt, *v1)


def ffn_kernel(*refs, chips, near):
    mixed = refs[: 2 * chips]
    extra_parts = refs[2 * chips : 4 * chips]
    at = 4 * chips
    x_ref, wgu_ref, wd_ref, nf_ref = refs[at : at + 4]
    at += 4
    if near:
        got_ref, lay_got_ref = refs[at : at + 2]
        at += 2
    nm_ref, inner_ref, ggu_ref, gnf_ref, dout_ref = refs[at : at + 5]
    at += 5
    if near:
        mid_ref, mixed_ref = refs[at : at + 2]
        gnm_refs = refs[at + 2 : at + 2 + chips]
        lay_refs = refs[at + 2 + chips : at + 2 + 2 * chips]
        at += 2 + 2 * chips
    else:
        gnm_ref, lay_ref = refs[at : at + 2]
        at += 2
    w_s, wo_s, extra_s, sems = refs[at:]
    step = pl.program_id(0)
    rows = nm_ref.shape[0]

    @pl.when(step == 0)
    def _():
        copies = [
            pltpu.make_async_copy(part, extra_s.at[j], sems.at[j])
            for j, part in enumerate(extra_parts)
        ]
        for copy in copies:
            copy.start()
        assemble(w_s, wgu_ref)
        for j, copy in enumerate(copies):
            copy.wait()
            wo_s[j * WIDE : (j + 1) * WIDE, :] = extra_s[j, rows:, :]

    cat = jnp.concatenate([m[...] for m in mixed], axis=1)
    hidden = wd_ref.shape[0]
    middle = x_ref[:rows, :].astype(F32) + dot_nn(cat, wo_s[...])
    factor = rms_factor(middle)
    scaled = middle * factor
    nm = (scaled * nf_ref[...]).astype(BF16)
    nm_ref[...] = nm
    lin = dot_nn(nm, w_s[...])
    dout = extra_s[step if near else chips + step, :rows, :]
    dout_ref[...] = dout
    back = dot_nt(dout, wd_ref[...])
    gate, up = lin[:, :hidden], lin[:, hidden:]
    sig = jax.nn.sigmoid(gate)
    silu = gate * sig
    inner = (silu * up).astype(BF16)
    inner_ref[...] = inner
    g_gate = (back * up * (sig * (1.0 + gate * (1.0 - sig)))).astype(BF16)
    g_up = (back * silu).astype(BF16)
    ggu = jnp.concatenate([g_gate, g_up], axis=1)
    ggu_ref[...] = ggu
    gnm = dot_nt(ggu, w_s[...])
    lay = dot_nn(inner, wd_ref[...])

    @pl.when(step == 0)
    def _():
        gnf_ref[...] = jnp.zeros_like(gnf_ref)
        if near:
            mid_ref[...] = middle
            mixed_ref[...] = cat

    gnf_ref[...] += jnp.sum(gnm * scaled, axis=0, keepdims=True)
    if near:
        gnm = (gnm + got_ref[...].astype(F32)).astype(BF16)
        lay = (lay + lay_got_ref[...].astype(F32)).astype(BF16)
        for r in range(chips):

            @pl.when(step == r)
            def _(r=r):
                gnm_refs[r][...] = gnm
                lay_refs[r][...] = lay

    else:
        gnm_ref[...] = gnm.astype(BF16)
        lay_ref[...] = lay.astype(BF16)


def ffn(side, own_parts, sib_stack, x, near_extra, far_extra, wgu, wd, norm_ffn, got=()):
    chips = len(own_parts)
    rows, width = near_extra[0].shape
    rows -= WIDE
    half = rows * chips
    hidden = wd.shape[0]
    near = side == 0
    row_block = lambda cols: pl.BlockSpec((rows, cols), lambda i: (i, 0))
    piece = lambda r: pl.BlockSpec((rows, WIDE), lambda i: (i ^ r, 0))
    stack = lambda r: pl.BlockSpec((rows, WIDE), lambda i: (r * chips + (i ^ r), 0))
    out_shape = [
        shaped((half, width), BF16), shaped((half, hidden), BF16), shaped((half, 2 * hidden), BF16),
        shaped((1, width), F32), shaped((half, width), BF16),
    ]
    out_specs = [
        row_block(width), row_block(hidden), row_block(2 * hidden), whole(out_shape[3]),
        row_block(width),
    ]
    if near:
        more = [shaped((rows, width), F32), shaped((rows, 2 * chips * WIDE), BF16)]
        more += [shaped((rows, width), BF16)] * (2 * chips)
        out_shape += more
        out_specs += [whole(a) for a in more]
    else:
        out_shape += [shaped((half, width), BF16)] * 2
        out_specs += [row_block(width)] * 2
    return pl.pallas_call(
        functools.partial(ffn_kernel, chips=chips, near=near),
        grid=(chips,),
        in_specs=[piece(r) for r in range(chips)]
        + [stack(r) for r in range(chips)]
        + [ANY] * (2 * chips)
        + [pl.BlockSpec((rows + 16, width), lambda i: (i, 0))]
        + [whole(a) for a in (wgu, wd, norm_ffn)]
        + [row_block(width)] * len(got),
        out_specs=out_specs,
        out_shape=out_shape,
        scratch_shapes=[
            pltpu.VMEM((width, 2 * hidden), BF16),
            pltpu.VMEM((2 * chips * WIDE, width), BF16),
            pltpu.VMEM((2 * chips, rows + WIDE, width), BF16),
            pltpu.SemaphoreType.DMA((2 * chips,)),
        ],
        compiler_params=params(),
        cost_estimate=pl.CostEstimate(
            flops=2 * half * width * (2 * chips * WIDE + 6 * hidden),
            bytes_accessed=half * width * 12,
            transcendentals=half * hidden,
        ),
        name="ffn_half",
    )(
        *own_parts, *[sib_stack] * chips, *near_extra, *far_extra, x, wgu, wd, norm_ffn, *got,
    )


def ffn_grads_kernel(nm0, nm1, ggu0, ggu1, in0, in1, dout0, dout1, _, gu_ref, gd_ref):
    gu = dot_tn(nm0[...], ggu0[...]) + dot_tn(nm1[...], ggu1[...])
    gu = gu.astype(BF16)
    if len(gu_ref.shape) == 2:
        gu_ref[...] = gu
    else:
        z_count, parts, shard, _ = gu_ref.shape
        for f in range(z_count):
            for s in range(parts):
                at = (s * z_count + f) * shard
                gu_ref[f, s] = gu[at : at + shard]
    gd_ref[...] = (dot_tn(in0[...], dout0[...]) + dot_tn(in1[...], dout1[...])).astype(BF16)


def ffn_grads(nm, ggu, inner, dout, seq_count, z_count, ticket):
    half, width = nm[0].shape
    hidden = inner[0].shape[1]
    shard = width // (seq_count * z_count)
    steps = max(1, min(4, hidden // WIDE))
    column_block = lambda cols: pl.BlockSpec((half, cols // steps), lambda i: (0, i))
    if shard % 16 == 0 and seq_count % steps == 0:
        gu = shaped((z_count, seq_count, shard, 2 * hidden), BF16)
        gu_spec = pl.BlockSpec(
            (z_count, seq_count // steps, shard, 2 * hidden), lambda i: (0, i, 0, 0)
        )
    else:
        gu = shaped((width, 2 * hidden), BF16)
        gu_spec = pl.BlockSpec((width // steps, 2 * hidden), lambda i: (i, 0))
    gu, gd = pl.pallas_call(
        ffn_grads_kernel,
        grid=(steps,),
        in_specs=[column_block(width)] * 2
        + [whole(a) for a in ggu]
        + [column_block(hidden)] * 2
        + [whole(a) for a in dout]
        + [ANY],
        out_specs=[gu_spec, pl.BlockSpec((hidden // steps, width), lambda i: (i, 0))],
        out_shape=[gu, shaped((hidden, width), BF16)],
        compiler_params=params(),
        cost_estimate=pl.CostEstimate(
            flops=2 * half * width * 6 * hidden, bytes_accessed=half * width * 16, transcendentals=0
        ),
        name="ffn_grads",
    )(*nm, *ggu, *inner, *dout, ticket)
    if len(gu.shape) == 2:
        gu = gu.reshape(seq_count, z_count, shard, 2 * hidden).transpose(1, 0, 2, 3)
    return gu.reshape(width, 2 * hidden), gd


def pair_kernel(a0, a1, b0, b1, w_ref, _, out_ref, sum_ref):
    product = dot_tn(a0[...], b0[...]) + dot_tn(a1[...], b1[...])
    out_ref[...] = product.astype(BF16)
    rows = product.shape[0]
    if len(w_ref.shape) == 2:
        w = w_ref[...].astype(F32)
    else:
        w = w_ref[...].astype(F32)
        z_count, parts, shard, wide = w.shape
        w = jnp.concatenate([w[f, s] for s in range(parts) for f in range(z_count)], axis=0)
    total = jnp.sum(product * w, axis=1, keepdims=True) * jnp.ones((rows, WIDE), F32)
    sum_ref[...] = total.T[:8]


def pair_product(left, right, w, ticket, steps=4):
    half, width = left[0].shape
    wide = right[0].shape[1]
    if len(w.shape) == 2:
        w_spec = pl.BlockSpec((width // steps, wide), lambda i: (i, 0))
    else:
        block = (w.shape[0], w.shape[1] // steps) + w.shape[2:]
        w_spec = pl.BlockSpec(block, lambda i: (0, i, 0, 0))
    return pl.pallas_call(
        pair_kernel,
        grid=(steps,),
        in_specs=[pl.BlockSpec((half, width // steps), lambda i: (0, i))] * 2
        + [whole(a) for a in right]
        + [w_spec, ANY],
        out_specs=[
            pl.BlockSpec((width // steps, wide), lambda i: (i, 0)),
            pl.BlockSpec((8, width // steps), lambda i: (0, i)),
        ],
        out_shape=[shaped((width, wide), BF16), shaped((8, width), F32)],
        compiler_params=params(),
        cost_estimate=pl.CostEstimate(
            flops=4 * half * width * wide, bytes_accessed=half * width * 6, transcendentals=0
        ),
        name="pair_product",
    )(*left, *right, w, ticket)


def added(pieces):
    total = pieces[0][...].astype(F32)
    for piece in pieces[1:]:
        total = total + piece[...].astype(F32)
    return total


def norm_back(values, gain, incoming):
    factor = rms_factor(values)
    weighted = incoming * gain
    return factor * weighted - values * (factor * factor * factor) * jnp.mean(
        weighted * values, axis=-1, keepdims=True
    )


def middle_back_kernel(*refs, chips):
    extra = refs[chips : 3 * chips]
    mid_ref, nf_ref, me_ref, gm_ref, gb_ref, out_ref = refs[3 * chips :]
    rows = mid_ref.shape[0]
    grad = extra[0][:rows, :].astype(F32) + norm_back(mid_ref[...], nf_ref[...], added(refs[:chips]))
    gm_ref[...] = grad
    branch = grad.astype(BF16)
    gb_ref[...] = branch
    for side in range(2):
        for r in range(chips):
            part = dot_nt(branch, extra[side * chips + r][rows:, :])
            out_ref[me_ref[0] ^ (2 * r + side)] = part.astype(BF16)


def middle_back(pieces, middle, norm_ffn, near_extra, far_extra, me):
    chips = len(pieces)
    rows, width = middle.shape
    vmem = pl.BlockSpec(memory_space=pltpu.VMEM)
    return pl.pallas_call(
        functools.partial(middle_back_kernel, chips=chips),
        in_specs=[vmem] * (3 * chips + 2) + [pl.BlockSpec(memory_space=pltpu.SMEM)],
        out_shape=[
            shaped((rows, width), F32), shaped((rows, width), BF16),
            shaped((2 * chips, rows, WIDE), BF16),
        ],
        compiler_params=params(False),
        cost_estimate=pl.CostEstimate(
            flops=2 * rows * width * 2 * chips * WIDE,
            bytes_accessed=rows * width * 12,
            transcendentals=0,
        ),
        name="middle_back",
    )(*pieces, *near_extra, *far_extra, middle, norm_ffn, me)


def input_back_kernel(*refs, chips):
    x_ref, gm_ref, na_ref, out_ref = refs[chips:]
    out_ref[...] = gm_ref[...] + norm_back(x_ref[...].astype(F32), na_ref[...], added(refs[:chips]))


def input_back(pieces, x, grad_middle, norm_attn):
    return pl.pallas_call(
        functools.partial(input_back_kernel, chips=len(pieces)),
        out_shape=shaped(x.shape, F32),
        compiler_params=params(False),
        name="input_back",
    )(*pieces, x, grad_middle, norm_attn)


def project_back_kernel(*refs, head_size):
    dq, qlin, klin, lanes = refs[0:2], refs[2:4], refs[4:6], refs[6:8]
    dk_ref, dv_ref, qg_ref, kg_ref = refs[8:12]
    gl, gain_ref = refs[12:14], refs[14]
    half = head_size // 2
    rows = qlin[0].shape[0]
    lane = lanes_of((rows, WIDE))
    blocks = head_blocks(head_size)

    @pl.when(pl.program_id(0) == 0)
    def _():
        gain_ref[...] = jnp.zeros_like(gain_ref)

    for side in range(2):
        cosine, sine = tables(lanes[side][:half, :], lanes[side][half : 2 * half, :])

        def back(grad, u, gain, at):
            grad = grad.astype(F32)
            grad = grad * cosine - partner(grad, lane, head_size) * sine
            factor = lax.rsqrt(head_sum(u * u, blocks) * (1.0 / head_size) + EPSILON)
            gain_ref[at : at + 1, :] += jnp.sum(grad * u * factor, axis=0, keepdims=True)
            weighted = grad * gain
            mean = head_sum(weighted * u, blocks) * (1.0 / head_size)
            return (factor * weighted - u * (factor * factor * factor) * mean).astype(BF16)

        gq = back(dq[side][...], qlin[side][...], qg_ref[...], 0)
        gk = back(dk_ref[side], klin[side][...], kg_ref[...], 1)
        gl[side][...] = jnp.concatenate([gq, gk, dv_ref[side]], axis=1)


def project_back(dq, qlin, klin, lane_rows, dk, dv, q_gain, k_gain, head_size, chips):
    half = qlin[0].shape[0]
    rows = half // chips
    count = lane_rows[0].shape[0]
    row_block = lambda cols: pl.BlockSpec((rows, cols), lambda i: (i, 0))
    both = pl.BlockSpec((2, rows, WIDE), lambda i: (0, i, 0))
    gain = shaped((8, WIDE), F32)
    return pl.pallas_call(
        functools.partial(project_back_kernel, head_size=head_size),
        grid=(chips,),
        in_specs=[row_block(WIDE)] * 6
        + [pl.BlockSpec((count, rows), lambda i: (0, i))] * 2
        + [both, both, whole(q_gain), whole(k_gain)],
        out_specs=[row_block(3 * WIDE), row_block(3 * WIDE), whole(gain)],
        out_shape=[shaped((half, 3 * WIDE), BF16)] * 2 + [gain],
        compiler_params=params(),
        cost_estimate=pl.CostEstimate(
            flops=2 * half * WIDE * 16 * WIDE, bytes_accessed=half * WIDE * 40, transcendentals=0
        ),
        name="project_back",
    )(*dq, *qlin, *klin, *lane_rows, dk, dv, q_gain, k_gain)


def spread_back_kernel(*refs, chips, near):
    gl_ref, w_ref = refs[:2]
    got = refs[2:3] if near else ()
    outs, w_s = refs[2 + len(got) : -1], refs[-1]
    step = pl.program_id(0)

    @pl.when(step == 0)
    def _():
        assemble(w_s, w_ref)

    out = dot_nt(gl_ref[...], w_s[...])
    if near:
        out = (out + got[0][...].astype(F32)).astype(BF16)
        for r in range(chips):

            @pl.when(step == r)
            def _(r=r):
                outs[r][...] = out

    else:
        outs[0][...] = out.astype(BF16)


def spread_back(gl, w, chips, got=None):
    half, wide = gl.shape
    width = math.prod(w.shape[:-1])
    rows = half // chips
    near = got is not None
    row_block = lambda cols: pl.BlockSpec((rows, cols), lambda i: (i, 0))
    out_shape = [shaped((rows, width), BF16)] * chips if near else [shaped((half, width), BF16)]
    return pl.pallas_call(
        functools.partial(spread_back_kernel, chips=chips, near=near),
        grid=(chips,),
        in_specs=[row_block(wide), whole(w)] + ([row_block(width)] if near else []),
        out_specs=[whole(a) for a in out_shape] if near else [row_block(width)],
        out_shape=out_shape,
        scratch_shapes=[pltpu.VMEM((width, wide), BF16)],
        compiler_params=params(),
        cost_estimate=pl.CostEstimate(
            flops=2 * half * width * wide, bytes_accessed=half * width * 4, transcendentals=0
        ),
        name="spread_back",
    )(gl, w, *([got] if near else []))


def last_kernel(in_ref, *refs, z_count, shard):
    outs, small_ref = refs[:-1], refs[-1]
    seq_count = in_ref.shape[0] // z_count
    small = None
    for s in range(seq_count):
        total = None
        for f in range(z_count):
            block = in_ref[s * z_count + f].astype(F32)
            total = block if total is None else total + block
        for i, out_ref in enumerate(outs):
            out_ref[:, s * WIDE : (s + 1) * WIDE] = total[:shard, i * WIDE : (i + 1) * WIDE]
        small = total[shard:] if small is None else small + total[shard:]
    small_ref[...] = small


def last_sums(blocks, z_count, shard):
    count, rows, wide = blocks.shape
    seq_count = count // z_count
    return pl.pallas_call(
        functools.partial(last_kernel, z_count=z_count, shard=shard),
        out_shape=[shaped((shard, seq_count * WIDE), F32)] * 3 + [shaped((rows - shard, wide), F32)],
        compiler_params=params(False),
        name="last_sums",
    )(blocks)


def swap(x, seq_count, bits):
    return lax.ppermute(x, "seq", [(i, i ^ bits) for i in range(seq_count)])


def to_chips(x, seq_count):
    return [x] + [swap(x, seq_count, 2 * r) for r in range(1, seq_count // 2)]


def spread_slots(slots, seq_count):
    return [slots[0]] + [swap(slots[r], seq_count, 2 * r) for r in range(1, len(slots))]


def after(values, *others):
    kept, _ = lax.optimization_barrier((values, others))
    return kept


def add_up(parts):
    total = parts[0].astype(F32)
    for part in parts[1:]:
        total = total + part.astype(F32)
    return total


def body(
    tokens, weight_query, weight_key, weight_value, weight_out, weight_gate, weight_up, weight_down,
    norm_attn, norm_ffn, query_gain, key_gain, variate_bias, variate_ids, sample_ids, time_ids,
    out_grad,
):
    seq_count = lax.axis_size("seq")
    z_count = lax.axis_size("fsdp")
    everyone = seq_count * z_count
    chips = seq_count // 2
    _, rows, width = tokens.shape
    heads = variate_bias.shape[1]
    head_size = query_gain.shape[0]
    half_size = head_size // 2
    shard = weight_query.shape[0]
    features = heads * head_size
    hidden = weight_gate.shape[1] // seq_count
    me = lax.axis_index("seq")
    x_own = tokens.reshape(rows, width)
    dout_own = out_grad.reshape(rows, width)

    columns = columns_by_device(
        (weight_query, weight_key, weight_value, weight_gate, weight_up), seq_count
    )
    columns = lax.all_to_all(columns, "seq", split_axis=0, concat_axis=0, tiled=True)
    w_out_rows = lax.all_gather(weight_out, "fsdp", axis=0, tiled=True)
    columns = after(columns, w_out_rows)
    w_qkv = jnp.broadcast_to(
        columns[None, :, :, : 3 * WIDE], (z_count, seq_count, shard, 3 * WIDE)
    )
    w_qkv = gathered(lax.all_to_all(w_qkv, "fsdp", split_axis=0, concat_axis=0, tiled=True))
    w_down = lax.all_gather(weight_down, "fsdp", axis=0, tiled=True)
    if features < WIDE:
        w_out_rows = jnp.pad(w_out_rows, ((0, WIDE - features), (0, 0)))
    w_gu = gathered(lax.all_gather(columns[:, :, 3 * WIDE :], "fsdp", axis=0, tiled=False))

    ids = jnp.concatenate([variate_ids, sample_ids, time_ids // 64, time_ids % 64], axis=0)
    ids = jnp.pad(ids.astype(BF16), ((0, 12), (0, width - rows)))
    packed = after(jnp.concatenate([x_own, ids], axis=0), columns, w_out_rows)
    near_x = to_chips(packed, seq_count)
    stack_x = jnp.concatenate(after(near_x, w_qkv), axis=0)
    far_x = swap(stack_x, seq_count, 1)
    extra = after(jnp.concatenate([dout_own, w_out_rows], axis=0), near_x[1:])
    near_extra = to_chips(extra, seq_count)
    far_extra = [swap(e, seq_count, 1) for e in near_extra]

    gain_attn = norm_attn.reshape(1, width)
    gain_ffn = norm_ffn.reshape(1, width)
    q_gain = jnp.tile(query_gain, WIDE // head_size).reshape(1, WIDE)
    k_gain = jnp.tile(key_gain, WIDE // head_size).reshape(1, WIDE)
    frequency = (10000.0 ** (-2.0 * jnp.arange(half_size).astype(F32) / head_size))[:, None]

    def projected(x):
        return project(
            x, chips, w_qkv, gain_attn, q_gain, k_gain, frequency, variate_bias, head_size
        )

    near_all = projected(stack_x)
    far_all = projected(far_x)
    nin, q_lin, k_lin, lane_rows, q_aug, k_aug, k_trans, v_aug = zip(near_all, far_all)
    attend_near = attend(q_aug[0], k_aug, v_aug, head_size)
    attend_far = attend(after(q_aug[1], attend_near, near_extra[1:3]), k_aug, v_aug, head_size)
    mixed, o_full, z_inverse = zip(attend_near, attend_far)
    own_parts = [to_chips(mixed[side], seq_count) for side in (0, 1)]
    own_parts[0] = after(own_parts[0], attend_far)
    sib_stack = [swap(jnp.concatenate(own_parts[side], axis=0), seq_count, 1) for side in (0, 1)]

    nm_far, inner_far, ggu_far, gnf_far, dout_far, gnm_far, lay_far = ffn(
        1, own_parts[1], sib_stack[0], far_x, near_extra, far_extra, w_gu, w_down, gain_ffn
    )
    nm_near, inner_near, ggu_near, gnf_near, dout_near, middle, mixed_own, *slots = ffn(
        0, own_parts[0], sib_stack[1], stack_x, near_extra, far_extra, w_gu, w_down, gain_ffn,
        (swap(gnm_far, seq_count, 1), swap(lay_far, seq_count, 1)),
    )

    gnm_parts = spread_slots(slots[:chips], seq_count)
    grad_gu, grad_down = ffn_grads(
        (nm_near, nm_far), (ggu_near, ggu_far), (inner_near, inner_far), (dout_near, dout_far),
        seq_count, z_count, swap(gnf_near, seq_count, 1),
    )
    me_row = jnp.reshape(me, (1,))
    grad_middle, grad_branch, g_out = middle_back(
        after(gnm_parts, grad_gu, grad_down),
        middle, gain_ffn, near_extra, far_extra, me_row,
    )
    g_all = lax.all_to_all(g_out, "seq", split_axis=0, concat_axis=0, tiled=True)

    grad_gu = lax.psum_scatter(grad_gu, "fsdp", scatter_dimension=0, tiled=True)
    grad_gu = grad_gu.reshape(seq_count, shard, 2 * hidden)
    grad_down = lax.psum_scatter(grad_down, "fsdp", scatter_dimension=0, tiled=True)
    grad_out = dot_tn(mixed_own, grad_branch).astype(BF16)
    half_out = chips * WIDE
    out_slots = add_up([grad_out[:half_out], swap(grad_out[half_out:], seq_count, 1)])
    out_slots = out_slots.astype(BF16)
    both_slots = [
        jnp.concatenate([slots[chips + r], out_slots[r * WIDE : (r + 1) * WIDE]], axis=0)
        for r in range(chips)
    ]
    both_parts = spread_slots(after(both_slots, g_all), seq_count)
    gu_got = lax.all_to_all(
        after(grad_gu, g_all), "seq", split_axis=0, concat_axis=0, tiled=True
    )

    dq_near, dq_far, dk, dv, bias_rows = attend_back(
        me_row, after(g_all, both_slots),
        q_aug, o_full, z_inverse, lane_rows, k_aug, k_trans, v_aug, head_size,
    )
    dq_far = after(dq_far, grad_gu, both_parts)
    gl_near, gl_far, gain_rows = project_back(
        (dq_near, dq_far), q_lin, k_lin, lane_rows, dk, dv, q_gain, k_gain, head_size, chips
    )
    (gni_far,) = spread_back(gl_far, w_qkv, chips)
    gni_got = swap(gni_far, seq_count, 1)
    grad_qkv, gna = pair_product(
        nin, (gl_near, gl_far), w_qkv, swap(gain_rows, seq_count, 1)
    )
    gni_slots = spread_back(
        gl_near, w_qkv, chips, after(gni_got, grad_qkv)
    )
    gni_parts = spread_slots(gni_slots, seq_count)
    both = add_up(after(both_parts, gni_slots))
    grad_out = both[rows : rows + features].astype(BF16)
    z_me = lax.axis_index("fsdp")
    z_parts = []
    for r in range(z_count):
        part = lax.dynamic_slice(grad_out, ((z_me ^ r) * shard, 0), (shard, width))
        if r:
            part = lax.ppermute(part, "fsdp", [(i, i ^ r) for i in range(z_count)])
        z_parts.append(part)
    grad_out = add_up(z_parts)
    in_grad = input_back(gni_parts, x_own, grad_middle, gain_attn)

    grad_qk_gain = gain_rows[:2, :features].reshape(2, heads, head_size).sum(axis=1)
    bias_cols = jnp.sum(bias_rows, axis=1).reshape(2, 2, 4).sum(axis=2)[:, :heads]
    bias_both = jnp.stack([bias_cols[0], bias_cols[1] - bias_cols[0]])
    bias_all = lax.dynamic_update_slice(
        jnp.zeros((2, heads * seq_count), F32), bias_both, (0, me * heads)
    )
    small = jnp.concatenate(
        [
            gna[0] / norm_attn,
            (gnf_near + gnf_far).reshape(-1),
            grad_qk_gain.reshape(-1),
            bias_all.reshape(-1),
        ]
    )
    count = small.shape[0]
    small_rows = -(-count // (8 * 3 * WIDE)) * 8
    small = jnp.pad(small, (0, small_rows * 3 * WIDE - count)).astype(BF16)
    small = jnp.broadcast_to(small.reshape(1, small_rows, 3 * WIDE), (everyone, small_rows, 3 * WIDE))
    grad_qkv = after(grad_qkv, gu_got, gni_slots)
    blocks = jnp.concatenate([grad_qkv.reshape(everyone, shard, 3 * WIDE), small], axis=1)
    last = lax.all_to_all(blocks, ("seq", "fsdp"), split_axis=0, concat_axis=0, tiled=True)
    gu_got = after(gu_got, blocks)
    grad_down = after(grad_down, gni_parts[3:])
    layer_out = (middle + both[:rows]).astype(BF16)
    grad_gu = gu_got.transpose(1, 0, 2).astype(F32)
    grad_gate = grad_gu[:, :, :hidden].reshape(shard, seq_count * hidden)
    grad_up = grad_gu[:, :, hidden:].reshape(shard, seq_count * hidden)
    grad_down = grad_down.astype(F32)
    *grad_qkv, small = last_sums(last, z_count, shard)
    grad_query, grad_key, grad_value = (
        g.reshape(shard, seq_count, WIDE)[:, :, :features].reshape(shard, width)
        if features < WIDE
        else g
        for g in grad_qkv
    )
    small = small.reshape(-1)
    cut = 2 * width + 2 * head_size
    grad_bias = lax.dynamic_slice(
        small[cut:count].reshape(2, heads * seq_count), (0, me * heads), (2, heads)
    )
    return (
        layer_out.reshape(tokens.shape),
        in_grad.reshape(tokens.shape),
        grad_query,
        grad_key,
        grad_value,
        grad_out,
        grad_gate,
        grad_up,
        grad_down,
        small[:width],
        small[width : 2 * width],
        small[2 * width : 2 * width + head_size],
        small[2 * width + head_size : cut],
        grad_bias,
    )


def solution(mesh):
    rows = P("fsdp", "seq", None)
    shards = P(("seq", "fsdp"), None)
    ids = P("fsdp", "seq")
    bias = P(None, "seq")
    return jax.shard_map(
        body,
        mesh=mesh,
        in_specs=(rows,) + (shards,) * 7 + (P(),) * 4 + (bias, ids, ids, ids, rows),
        out_specs=(rows, rows) + (shards,) * 7 + (P(),) * 4 + (bias,),
        check_vma=False,
    )
```

```python
import functools
import math

import jax
import jax.numpy as jnp
from jax import lax
from jax.experimental import pallas as pl
from jax.experimental.pallas import tpu as pltpu
from jax.sharding import PartitionSpec as P

EPSILON = 1e-06
FAR = -1e30
LOG2E = math.log2(math.e)
WIDE = 128
ROWS_T = 160
F32 = jnp.float32
BF16 = jnp.bfloat16


def dot_nn(left, right):
    return jnp.dot(left, right, preferred_element_type=F32)


def dot_nt(left, right):
    return lax.dot_general(left, right, (((1,), (1,)), ((), ())), preferred_element_type=F32)


def dot_tn(left, right):
    return lax.dot_general(left, right, (((0,), (0,)), ((), ())), preferred_element_type=F32)


def rms_factor(values):
    return lax.rsqrt(jnp.mean(values * values, axis=-1, keepdims=True) + EPSILON)


def lanes_of(shape):
    return lax.broadcasted_iota(jnp.int32, shape, len(shape) - 1)


def head_sum(values, blocks):
    high = values.astype(BF16)
    low = (values - high.astype(F32)).astype(BF16)
    return dot_nn(high, blocks) + dot_nn(low, blocks)


def head_blocks(head_size):
    row = lax.broadcasted_iota(jnp.int32, (WIDE, WIDE), 0) // head_size
    column = lax.broadcasted_iota(jnp.int32, (WIDE, WIDE), 1) // head_size
    return jnp.where(row == column, 1.0, 0.0).astype(BF16)


def partner(values, lane, head_size):
    half = head_size // 2
    up = pltpu.roll(values, WIDE - half, 1)
    down = pltpu.roll(values, half, 1)
    return jnp.where(lane % head_size < half, up, down)


def tables(cosine, sine):
    times = WIDE // (2 * cosine.shape[0])
    cos_rows = jnp.concatenate([cosine, cosine] * times, axis=0)
    sin_rows = jnp.concatenate([-sine, sine] * times, axis=0)
    return cos_rows.T, sin_rows.T


def params(grid=True):
    return pltpu.CompilerParams(
        vmem_limit_bytes=60 * 1024 * 1024,
        dimension_semantics=("arbitrary",) if grid else None,
    )


def whole(array):
    return pl.BlockSpec(array.shape, lambda *_: (0,) * len(array.shape))


def shaped(shape, dtype):
    return jax.ShapeDtypeStruct(shape, dtype)


ANY = pl.BlockSpec(memory_space=pl.ANY)


def assemble(out_ref, in_ref):
    if len(in_ref.shape) == 2:
        out_ref[...] = in_ref[...]
        return
    z_count, seq_count, shard, _ = in_ref.shape
    for f in range(z_count):
        for s in range(seq_count):
            at = (s * z_count + f) * shard
            out_ref[at : at + shard, :] = in_ref[f, s]


def gathered(w):
    if w.shape[2] % 16 == 0:
        return w
    return w.transpose(1, 0, 2, 3).reshape(-1, w.shape[-1])


def columns_kernel(*refs):
    *weights, out_ref = refs
    at = 0
    for w_ref in weights:
        wide = w_ref.shape[1] // out_ref.shape[0]
        for s in range(out_ref.shape[0]):
            out_ref[s, :, at : at + wide] = w_ref[:, s * wide : (s + 1) * wide]
        at += wide


def columns_by_device(weights, seq_count):
    shard = weights[0].shape[0]
    wides = [w.shape[1] // seq_count for w in weights]
    if shard % 16 == 0 and all(wide % WIDE == 0 for wide in wides):
        return pl.pallas_call(
            columns_kernel,
            out_shape=shaped((seq_count, shard, sum(wides)), BF16),
            compiler_params=params(False),
            name="columns",
        )(*weights)
    pieces = []
    for w, wide in zip(weights, wides):
        short = -wide % WIDE
        pieces.append(jnp.pad(w.reshape(shard, seq_count, wide), ((0, 0), (0, 0), (0, short))))
    return jnp.concatenate(pieces, axis=2).transpose(1, 0, 2)


def project_kernel(
    x_ref, w_ref, na_ref, qg_ref, kg_ref, freq_ref, bias_ref,
    nin_ref, qlin_ref, klin_ref, lane_ref, qa_ref, ka_ref, kt_ref, v1_ref, w_s, *, heads, head_size,
):
    half = head_size // 2
    rows = nin_ref.shape[0]

    @pl.when(pl.program_id(0) == 0)
    def _():
        assemble(w_s, w_ref)

    x = x_ref[:rows, :].astype(F32)
    ids = x_ref[rows:, :rows].astype(F32)
    nin = (x * rms_factor(x) * na_ref[...]).astype(BF16)
    nin_ref[...] = nin
    lin = dot_nn(nin, w_s[...])
    q, k, v = lin[:, :WIDE], lin[:, WIDE : 2 * WIDE], lin[:, 2 * WIDE :]
    qlin_ref[...] = q
    klin_ref[...] = k
    angles = freq_ref[...] * (ids[2:3] * 64.0 + ids[3:4])
    cosine, sine = jnp.cos(angles), jnp.sin(angles)
    lane_ref[...] = jnp.concatenate([cosine, sine, ids[:8]], axis=0)
    cosine, sine = tables(cosine, sine)
    lane = lanes_of((rows, WIDE))
    blocks = head_blocks(head_size)

    def finish(u, gain):
        factor = lax.rsqrt(head_sum(u * u, blocks) * (1.0 / head_size) + EPSILON)
        u = u * factor * gain
        return u * cosine + partner(u, lane, head_size) * sine

    q = finish(q, qg_ref[...]) * (LOG2E * head_size**-0.5)
    k = finish(k, kg_ref[...])
    few = ROWS_T - WIDE
    row = lax.broadcasted_iota(jnp.int32, (few, rows), 0)
    variate = ids[0:1].astype(jnp.int32)
    sample = ids[1:2].astype(jnp.int32)
    same_variate = (row % 4) == variate
    same_sample = (row - 10) == sample
    one = jnp.ones((few, rows), F32)
    nil = jnp.zeros((few, rows), F32)
    rest = jnp.zeros((WIDE - few, rows), F32)

    def columns(few_rows):
        return jnp.concatenate([few_rows, rest], axis=0).T

    aug_q = jnp.where(
        row < 8,
        jnp.where(same_variate, one, nil),
        jnp.where(row < 10, one, jnp.where((row < 13) & same_sample, one, nil)),
    )
    qa_ref[...] = jnp.concatenate([q, columns(aug_q)], axis=1).astype(BF16)
    k_t = k.T
    row_k = lax.broadcasted_iota(jnp.int32, (WIDE, rows), 0)
    for h in range(heads):
        first, second = bias_ref[0, h] * LOG2E, bias_ref[1, h] * LOG2E
        step_up = jnp.where(row < 8, first - second, second) * one
        high = step_up.astype(BF16).astype(F32)
        low = step_up - high
        far = jnp.where(same_sample, nil, FAR)
        plain = jnp.where(((row // 4) == 4 + h) & same_variate, one, nil)
        aug_k = jnp.where(
            row < 4,
            jnp.where(same_variate, high, nil),
            jnp.where(
                row < 8,
                jnp.where(same_variate, low, nil),
                jnp.where(
                    row == 8,
                    high,
                    jnp.where(row == 9, low, jnp.where(row < 13, far, plain)),
                ),
            ),
        )
        mine = (lane // head_size) == h
        mine_t = (row_k // head_size) == h
        ka_ref[h] = jnp.concatenate([jnp.where(mine, k, 0.0), columns(aug_k)], axis=1).astype(BF16)
        kt_ref[h] = jnp.concatenate([jnp.where(mine_t, k_t, 0.0), aug_k], axis=0).astype(BF16)
        ones_v = jnp.where((lane == h) | (lane == 2 + h), 1.0, 0.0)
        v1_ref[h] = jnp.concatenate([jnp.where(mine, v, 0.0), ones_v], axis=1).astype(BF16)


def project(x, chips, w, norm_attn, q_gain, k_gain, freq, bias, head_size):
    width, wide = x.shape[1], w.shape[-1]
    rows = x.shape[0] // chips - 16
    heads = bias.shape[1]
    half = chips * rows
    count = head_size + 8
    row_block = lambda cols: pl.BlockSpec((rows, cols), lambda i: (i, 0))
    lane_block = pl.BlockSpec((count, rows), lambda i: (0, i))
    head_block = pl.BlockSpec((heads, rows, 2 * WIDE), lambda i: (0, i, 0))
    return pl.pallas_call(
        functools.partial(project_kernel, heads=heads, head_size=head_size),
        grid=(chips,),
        in_specs=[pl.BlockSpec((rows + 16, width), lambda i: (i, 0))]
        + [whole(a) for a in (w, norm_attn, q_gain, k_gain, freq)]
        + [pl.BlockSpec(memory_space=pltpu.SMEM)],
        out_specs=[
            row_block(width), row_block(WIDE), row_block(WIDE), lane_block, row_block(2 * WIDE),
            head_block, pl.BlockSpec((heads, ROWS_T, rows), lambda i: (0, 0, i)), head_block,
        ],
        out_shape=[
            shaped((half, width), BF16),
            shaped((half, WIDE), F32),
            shaped((half, WIDE), F32),
            shaped((count, half), F32),
            shaped((half, 2 * WIDE), BF16),
            shaped((heads, half, 2 * WIDE), BF16),
            shaped((heads, ROWS_T, half), BF16),
            shaped((heads, half, 2 * WIDE), BF16),
        ],
        scratch_shapes=[pltpu.VMEM((width, wide), BF16)],
        compiler_params=params(),
        cost_estimate=pl.CostEstimate(
            flops=2 * half * width * 3 * WIDE, bytes_accessed=half * width * 8, transcendentals=0
        ),
        name="project",
    )(x, w, norm_attn, q_gain, k_gain, freq, bias)


def attend_kernel(qa_ref, ka0, ka1, v10, v11, mixed_ref, o_ref, zi_ref, *, heads, head_size, chunk):
    qa = qa_ref[...]
    rows = qa.shape[0]
    half = ka0.shape[1]
    lane = lanes_of((rows, WIDE))
    total = jnp.zeros((rows, WIDE), F32)
    inverse = jnp.ones((rows, WIDE), F32)
    for h in range(heads):
        acc = jnp.zeros((rows, 2 * WIDE), F32)
        for ka_ref, v1_ref in ((ka0, v10), (ka1, v11)):
            for c in range(half // chunk):
                part = pl.ds(c * chunk, chunk)
                e = jnp.exp2(dot_nt(qa, ka_ref[h, part, :])).astype(BF16)
                acc = acc + dot_nn(e, v1_ref[h, part, :])
        z_inv = 1.0 / acc[:, WIDE + h : WIDE + h + 1]
        total = total + acc[:, :WIDE] * z_inv
        inverse = jnp.where((lane // head_size) == h, z_inv, inverse)
    mixed_ref[...] = total.astype(BF16)
    o_ref[...] = total
    zi_ref[...] = inverse


def attend(qa, ka, v1, head_size, block=512, chunk=256):
    heads, half, _ = ka[0].shape
    out_block = pl.BlockSpec((block, WIDE), lambda i: (i, 0))
    return pl.pallas_call(
        functools.partial(attend_kernel, heads=heads, head_size=head_size, chunk=chunk),
        grid=(half // block,),
        in_specs=[pl.BlockSpec((block, 2 * WIDE), lambda i: (i, 0))]
        + [whole(a) for a in (*ka, *v1)],
        out_specs=[out_block, out_block, out_block],
        out_shape=[shaped((half, WIDE), BF16), shaped((half, WIDE), F32), shaped((half, WIDE), F32)],
        compiler_params=params(),
        cost_estimate=pl.CostEstimate(
            flops=2 * heads * half * half * 8 * WIDE,
            bytes_accessed=half * WIDE * 32,
            transcendentals=2 * heads * half * half,
        ),
        name="attend",
    )(qa, *ka, *v1)


def attend_back_kernel(*refs, chips, heads, head_size, chunk):
    me_ref, g_ref = refs[:2]
    at = 2
    qa, o, zi, lanes, ka, kt, v1 = [refs[at + 2 * n : at + 2 * n + 2] for n in range(7)]
    at += 14
    dq_refs = refs[at : at + 2]
    dk_ref, dv_ref, bias_ref, g_s, dk_s, dv_s = refs[at + 2 :]
    step = pl.program_id(0)

    @pl.when(step == 0)
    def _():
        dk_s[...] = jnp.zeros_like(dk_s)
        dv_s[...] = jnp.zeros_like(dv_s)
        bias_ref[...] = jnp.zeros_like(bias_ref)
        for j in range(2 * chips):
            g_s[j % 2, j // 2] = g_ref[me_ref[0] ^ j]

    for side in range(2):
        q_rows = qa[side][...]
        rows = q_rows.shape[0]
        half_len = ka[0].shape[1]
        lane = lanes_of((rows, WIDE))
        q = q_rows[:, :WIDE]
        gz = (g_s[side, step].astype(F32) * zi[side][...]).astype(BF16)
        inner = gz.astype(F32) * o[side][...]
        aug = jnp.zeros((rows, WIDE), F32)
        for h in range(heads):
            mean = -jnp.sum(
                jnp.where((lane // head_size) == h, inner, 0.0), axis=-1, keepdims=True
            ) * jnp.ones((rows, WIDE), F32)
            high = mean.astype(BF16).astype(F32)
            aug = jnp.where(lane == h, high, jnp.where(lane == 2 + h, mean - high, aug))
        ga = jnp.concatenate([gz, aug.astype(BF16)], axis=1)
        dq_t = jnp.zeros((ROWS_T, rows), F32)
        for h in range(heads):
            mine = (lane // head_size) == h
            q_h = jnp.where(mine, q, jnp.zeros_like(q))
            g_h = jnp.where(mine, gz, jnp.zeros_like(gz))
            for other in range(2):
                for c in range(half_len // chunk):
                    part = pl.ds(c * chunk, chunk)
                    e = jnp.exp2(dot_nt(ka[other][h, part, :], q_rows))
                    ds = (e * dot_nt(v1[other][h, part, :], ga)).astype(BF16)
                    dv_s[other, part, :] += dot_nn(e.astype(BF16), g_h)
                    dk_s[other, part, :] += dot_nn(ds, q_h)
                    dq_t = dq_t + dot_nn(kt[other][h, :, part], ds)
        dq_refs[side][...] = (dq_t[:WIDE].T * (head_size**-0.5)).astype(BF16)
        variate = lanes[side][head_size : head_size + 1, :].astype(jnp.int32)
        columns = dq_t[WIDE + 16 : WIDE + 24]
        row = lax.broadcasted_iota(jnp.int32, columns.shape, 0)
        bias_ref[...] += jnp.concatenate(
            [jnp.where((row % 4) == variate, columns, 0.0), columns], axis=0
        )

    @pl.when(step == pl.num_programs(0) - 1)
    def _():
        dk_ref[...] = (dk_s[...] * (1.0 / LOG2E)).astype(BF16)
        dv_ref[...] = dv_s[...].astype(BF16)


def attend_back(me, g, qa, o, zi, lane_rows, ka, kt, v1, head_size, chunk=1024):
    heads, half, _ = ka[0].shape
    chips = g.shape[0] // 2
    chunk = math.gcd(half, chunk)
    block = half // chips
    count = lane_rows[0].shape[0]
    row_block = lambda cols: pl.BlockSpec((block, cols), lambda i: (i, 0))
    lane_block = pl.BlockSpec((count, block), lambda i: (0, i))
    full = shaped((2, half, WIDE), BF16)
    return pl.pallas_call(
        functools.partial(
            attend_back_kernel, chips=chips, heads=heads, head_size=head_size, chunk=chunk
        ),
        grid=(chips,),
        in_specs=[pl.BlockSpec(memory_space=pltpu.SMEM), whole(g)]
        + [row_block(2 * WIDE)] * 2
        + [row_block(WIDE)] * 4
        + [lane_block] * 2
        + [whole(a) for a in (*ka, *kt, *v1)],
        out_specs=[row_block(WIDE)] * 2
        + [whole(full), whole(full), pl.BlockSpec((16, block), lambda i: (0, 0))],
        out_shape=[shaped((half, WIDE), BF16)] * 2 + [full, full, shaped((16, block), F32)],
        scratch_shapes=[
            pltpu.VMEM((2, chips, block, WIDE), BF16),
            pltpu.VMEM((2, half, WIDE), F32),
            pltpu.VMEM((2, half, WIDE), F32),
        ],
        compiler_params=params(),
        cost_estimate=pl.CostEstimate(
            flops=2 * heads * half * half * 32 * WIDE,
            bytes_accessed=half * WIDE * 64,
            transcendentals=4 * heads * half * half,
        ),
        name="attend_back",
    )(me, g, *qa, *o, *zi, *lane_rows, *ka, *kt, *v1)


def ffn_kernel(*refs, chips, group, near):
    mixed = refs[: 2 * chips]
    extra_parts = refs[2 * chips : 4 * chips]
    at = 4 * chips
    x_ref, wgu_ref, wd_ref, nf_ref = refs[at : at + 4]
    at += 4
    if near:
        got_ref, lay_got_ref = refs[at : at + 2]
        at += 2
    nm_ref, inner_ref, ggu_ref, dout_ref = refs[at : at + 4]
    at += 4
    if near:
        mid_ref, mixed_ref = refs[at : at + 2]
        gnm_refs = refs[at + 2 : at + 2 + chips]
        lay_refs = refs[at + 2 + chips : at + 2 + 2 * chips]
        at += 2 + 2 * chips
    else:
        gnm_ref, lay_ref = refs[at : at + 2]
        at += 2
    w_s, wo_s, extra_s, sems = refs[at:]
    step = pl.program_id(0)
    rows = nm_ref.shape[0] // group

    @pl.when(step == 0)
    def _():
        copies = [
            pltpu.make_async_copy(part, extra_s.at[j], sems.at[j])
            for j, part in enumerate(extra_parts)
        ]
        for copy in copies:
            copy.start()
        assemble(w_s, wgu_ref)
        for j, copy in enumerate(copies):
            copy.wait()
            wo_s[j * WIDE : (j + 1) * WIDE, :] = extra_s[j, rows:, :]

    def own_order(block, r):
        if r % group == 0:
            return block
        slots = [(t ^ (r % group)) * rows for t in range(group)]
        return jnp.concatenate([block[at : at + rows] for at in slots], axis=0)

    cat = jnp.concatenate([own_order(m[...], j % chips) for j, m in enumerate(mixed)], axis=1)
    hidden = wd_ref.shape[0]
    x = [x_ref[t * (rows + 16) : t * (rows + 16) + rows, :] for t in range(group)]
    first = (0 if near else chips) + step * group
    dout = jnp.concatenate([extra_s[first + t, :rows, :] for t in range(group)], axis=0)
    dout_ref[...] = dout
    middle = jnp.concatenate(x, axis=0).astype(F32) + dot_nn(cat, wo_s[...])
    nm = (middle * rms_factor(middle) * nf_ref[...]).astype(BF16)
    nm_ref[...] = nm
    lin = dot_nn(nm, w_s[...])
    back = dot_nt(dout, wd_ref[...])
    gate, up = lin[:, :hidden], lin[:, hidden:]
    sig = jax.nn.sigmoid(gate)
    silu = gate * sig
    inner = (silu * up).astype(BF16)
    inner_ref[...] = inner
    g_gate = (back * up * (sig * (1.0 + gate * (1.0 - sig)))).astype(BF16)
    g_up = (back * silu).astype(BF16)
    ggu = jnp.concatenate([g_gate, g_up], axis=1)
    ggu_ref[...] = ggu
    gnm = dot_nt(ggu, w_s[...])
    lay = dot_nn(inner, wd_ref[...])
    if near:

        @pl.when(step == 0)
        def _():
            mid_ref[...] = middle[:rows]
            mixed_ref[...] = cat[:rows]

        gnm = (gnm + got_ref[...].astype(F32)).astype(BF16)
        lay = (lay + lay_got_ref[...].astype(F32)).astype(BF16)
        for r in range(chips):

            @pl.when(step == r // group)
            def _(r=r):
                at = (r % group) * rows
                gnm_refs[r][...] = gnm[at : at + rows]
                lay_refs[r][...] = lay[at : at + rows]

    else:
        gnm_ref[...] = gnm.astype(BF16)
        lay_ref[...] = lay.astype(BF16)


def ffn(
    side, own_parts, sib_stack, x, near_extra, far_extra, wgu, wd, norm_ffn, got=(), group=2
):
    chips = len(own_parts)
    group = math.gcd(chips, group)
    rows, width = near_extra[0].shape
    rows -= WIDE
    half = rows * chips
    block = rows * group
    steps = chips // group
    hidden = wd.shape[0]
    near = side == 0
    row_block = lambda cols: pl.BlockSpec((block, cols), lambda i: (i, 0))
    piece = lambda r: pl.BlockSpec((block, WIDE), lambda i: (i ^ (r // group), 0))
    stack = lambda r: pl.BlockSpec((block, WIDE), lambda i: (r * steps + (i ^ (r // group)), 0))
    out_shape = [
        shaped((half, width), BF16), shaped((half, hidden), BF16), shaped((half, 2 * hidden), BF16),
        shaped((half, width), BF16),
    ]
    out_specs = [row_block(width), row_block(hidden), row_block(2 * hidden), row_block(width)]
    if near:
        more = [shaped((rows, width), F32), shaped((rows, 2 * chips * WIDE), BF16)]
        more += [shaped((rows, width), BF16)] * (2 * chips)
        out_shape += more
        out_specs += [whole(a) for a in more]
    else:
        out_shape += [shaped((half, width), BF16)] * 2
        out_specs += [row_block(width)] * 2
    return pl.pallas_call(
        functools.partial(ffn_kernel, chips=chips, group=group, near=near),
        grid=(steps,),
        in_specs=[piece(r) for r in range(chips)]
        + [stack(r) for r in range(chips)]
        + [ANY] * (2 * chips)
        + [pl.BlockSpec((group * (rows + 16), width), lambda i: (i, 0))]
        + [whole(a) for a in (wgu, wd, norm_ffn)]
        + [row_block(width)] * len(got),
        out_specs=out_specs,
        out_shape=out_shape,
        scratch_shapes=[
            pltpu.VMEM((width, 2 * hidden), BF16),
            pltpu.VMEM((2 * chips * WIDE, width), BF16),
            pltpu.VMEM((2 * chips, rows + WIDE, width), BF16),
            pltpu.SemaphoreType.DMA((2 * chips,)),
        ],
        compiler_params=params(),
        cost_estimate=pl.CostEstimate(
            flops=2 * half * width * (2 * chips * WIDE + 6 * hidden),
            bytes_accessed=half * width * 12,
            transcendentals=half * hidden,
        ),
        name="ffn_half",
    )(
        *own_parts, *[sib_stack] * chips, *near_extra, *far_extra, x, wgu, wd, norm_ffn, *got,
    )


def row_sums(product, w_ref):
    w = w_ref[...].astype(F32)
    if len(w.shape) == 4:
        z_count, parts, _, _ = w.shape
        w = jnp.concatenate([w[f, s] for s in range(parts) for f in range(z_count)], axis=0)
    total = jnp.sum(product * w, axis=1, keepdims=True)
    return (total * jnp.ones((product.shape[0], WIDE), F32)).T[:8]


def block_of(w, steps):
    if len(w.shape) == 2:
        return pl.BlockSpec((w.shape[0] // steps, w.shape[1]), lambda i: (i, 0))
    block = (w.shape[0], w.shape[1] // steps) + w.shape[2:]
    return pl.BlockSpec(block, lambda i: (0, i, 0, 0))


def ffn_grads_kernel(nm0, nm1, ggu0, ggu1, in0, in1, dout0, dout1, w_ref, _, gu_ref, gd_ref, sum_ref):
    gu = dot_tn(nm0[...], ggu0[...]) + dot_tn(nm1[...], ggu1[...])
    sum_ref[...] = row_sums(gu, w_ref)
    gu = gu.astype(BF16)
    if len(gu_ref.shape) == 2:
        gu_ref[...] = gu
    else:
        z_count, parts, shard, _ = gu_ref.shape
        for f in range(z_count):
            for s in range(parts):
                at = (s * z_count + f) * shard
                gu_ref[f, s] = gu[at : at + shard]
    gd_ref[...] = (dot_tn(in0[...], dout0[...]) + dot_tn(in1[...], dout1[...])).astype(BF16)


def ffn_grads(nm, ggu, inner, dout, w, seq_count, z_count, ticket):
    half, width = nm[0].shape
    hidden = inner[0].shape[1]
    shard = width // (seq_count * z_count)
    steps = max(1, min(4, hidden // WIDE))
    column_block = lambda cols: pl.BlockSpec((half, cols // steps), lambda i: (0, i))
    if shard % 16 == 0 and seq_count % steps == 0:
        gu = shaped((z_count, seq_count, shard, 2 * hidden), BF16)
        gu_spec = pl.BlockSpec(
            (z_count, seq_count // steps, shard, 2 * hidden), lambda i: (0, i, 0, 0)
        )
    else:
        gu = shaped((width, 2 * hidden), BF16)
        gu_spec = pl.BlockSpec((width // steps, 2 * hidden), lambda i: (i, 0))
    gu, gd, sums = pl.pallas_call(
        ffn_grads_kernel,
        grid=(steps,),
        in_specs=[column_block(width)] * 2
        + [whole(a) for a in ggu]
        + [column_block(hidden)] * 2
        + [whole(a) for a in dout]
        + [block_of(w, steps), ANY],
        out_specs=[
            gu_spec,
            pl.BlockSpec((hidden // steps, width), lambda i: (i, 0)),
            pl.BlockSpec((8, width // steps), lambda i: (0, i)),
        ],
        out_shape=[gu, shaped((hidden, width), BF16), shaped((8, width), F32)],
        compiler_params=params(),
        cost_estimate=pl.CostEstimate(
            flops=2 * half * width * 6 * hidden, bytes_accessed=half * width * 16, transcendentals=0
        ),
        name="ffn_grads",
    )(*nm, *ggu, *inner, *dout, w, ticket)
    if len(gu.shape) == 2:
        gu = gu.reshape(seq_count, z_count, shard, 2 * hidden).transpose(1, 0, 2, 3)
    return gu.reshape(width, 2 * hidden), gd, sums[0]


def pair_kernel(a0, a1, b0, b1, w_ref, _, out_ref, sum_ref):
    product = dot_tn(a0[...], b0[...]) + dot_tn(a1[...], b1[...])
    out_ref[...] = product.astype(BF16)
    sum_ref[...] = row_sums(product, w_ref)


def pair_product(left, right, w, ticket, steps=4):
    half, width = left[0].shape
    wide = right[0].shape[1]
    return pl.pallas_call(
        pair_kernel,
        grid=(steps,),
        in_specs=[pl.BlockSpec((half, width // steps), lambda i: (0, i))] * 2
        + [whole(a) for a in right]
        + [block_of(w, steps), ANY],
        out_specs=[
            pl.BlockSpec((width // steps, wide), lambda i: (i, 0)),
            pl.BlockSpec((8, width // steps), lambda i: (0, i)),
        ],
        out_shape=[shaped((width, wide), BF16), shaped((8, width), F32)],
        compiler_params=params(),
        cost_estimate=pl.CostEstimate(
            flops=4 * half * width * wide, bytes_accessed=half * width * 6, transcendentals=0
        ),
        name="pair_product",
    )(*left, *right, w, ticket)


def added(pieces):
    total = pieces[0][...].astype(F32)
    for piece in pieces[1:]:
        total = total + piece[...].astype(F32)
    return total


def norm_back(values, gain, incoming):
    factor = rms_factor(values)
    weighted = incoming * gain
    return factor * weighted - values * (factor * factor * factor) * jnp.mean(
        weighted * values, axis=-1, keepdims=True
    )


def middle_back_kernel(*refs, chips):
    extra = refs[chips : 3 * chips]
    mid_ref, nf_ref, me_ref, gm_ref, gb_ref, out_ref = refs[3 * chips :]
    rows = mid_ref.shape[0]
    grad = extra[0][:rows, :].astype(F32) + norm_back(mid_ref[...], nf_ref[...], added(refs[:chips]))
    gm_ref[...] = grad
    branch = grad.astype(BF16)
    gb_ref[...] = branch
    for side in range(2):
        for r in range(chips):
            part = dot_nt(branch, extra[side * chips + r][rows:, :])
            out_ref[me_ref[0] ^ (2 * r + side)] = part.astype(BF16)


def middle_back(pieces, middle, norm_ffn, near_extra, far_extra, me):
    chips = len(pieces)
    rows, width = middle.shape
    vmem = pl.BlockSpec(memory_space=pltpu.VMEM)
    return pl.pallas_call(
        functools.partial(middle_back_kernel, chips=chips),
        in_specs=[vmem] * (3 * chips + 2) + [pl.BlockSpec(memory_space=pltpu.SMEM)],
        out_shape=[
            shaped((rows, width), F32), shaped((rows, width), BF16),
            shaped((2 * chips, rows, WIDE), BF16),
        ],
        compiler_params=params(False),
        cost_estimate=pl.CostEstimate(
            flops=2 * rows * width * 2 * chips * WIDE,
            bytes_accessed=rows * width * 12,
            transcendentals=0,
        ),
        name="middle_back",
    )(*pieces, *near_extra, *far_extra, middle, norm_ffn, me)


def input_back_kernel(*refs, chips):
    x_ref, gm_ref, na_ref, out_ref = refs[chips:]
    out_ref[...] = gm_ref[...] + norm_back(x_ref[...].astype(F32), na_ref[...], added(refs[:chips]))


def input_back(pieces, x, grad_middle, norm_attn):
    return pl.pallas_call(
        functools.partial(input_back_kernel, chips=len(pieces)),
        out_shape=shaped(x.shape, F32),
        compiler_params=params(False),
        name="input_back",
    )(*pieces, x, grad_middle, norm_attn)


def project_back_kernel(*refs, head_size):
    dq, qlin, klin, lanes = refs[0:2], refs[2:4], refs[4:6], refs[6:8]
    dk_ref, dv_ref, qg_ref, kg_ref = refs[8:12]
    gl, gain_ref = refs[12:14], refs[14]
    half = head_size // 2
    rows = qlin[0].shape[0]
    lane = lanes_of((rows, WIDE))
    blocks = head_blocks(head_size)

    @pl.when(pl.program_id(0) == 0)
    def _():
        gain_ref[...] = jnp.zeros_like(gain_ref)

    for side in range(2):
        cosine, sine = tables(lanes[side][:half, :], lanes[side][half : 2 * half, :])

        def back(grad, u, gain, at):
            grad = grad.astype(F32)
            grad = grad * cosine - partner(grad, lane, head_size) * sine
            factor = lax.rsqrt(head_sum(u * u, blocks) * (1.0 / head_size) + EPSILON)
            gain_ref[at : at + 1, :] += jnp.sum(grad * u * factor, axis=0, keepdims=True)
            weighted = grad * gain
            mean = head_sum(weighted * u, blocks) * (1.0 / head_size)
            return (factor * weighted - u * (factor * factor * factor) * mean).astype(BF16)

        gq = back(dq[side][...], qlin[side][...], qg_ref[...], 0)
        gk = back(dk_ref[side], klin[side][...], kg_ref[...], 1)
        gl[side][...] = jnp.concatenate([gq, gk, dv_ref[side]], axis=1)


def project_back(dq, qlin, klin, lane_rows, dk, dv, q_gain, k_gain, head_size, chips):
    half = qlin[0].shape[0]
    rows = half // chips
    count = lane_rows[0].shape[0]
    row_block = lambda cols: pl.BlockSpec((rows, cols), lambda i: (i, 0))
    both = pl.BlockSpec((2, rows, WIDE), lambda i: (0, i, 0))
    gain = shaped((8, WIDE), F32)
    return pl.pallas_call(
        functools.partial(project_back_kernel, head_size=head_size),
        grid=(chips,),
        in_specs=[row_block(WIDE)] * 6
        + [pl.BlockSpec((count, rows), lambda i: (0, i))] * 2
        + [both, both, whole(q_gain), whole(k_gain)],
        out_specs=[row_block(3 * WIDE), row_block(3 * WIDE), whole(gain)],
        out_shape=[shaped((half, 3 * WIDE), BF16)] * 2 + [gain],
        compiler_params=params(),
        cost_estimate=pl.CostEstimate(
            flops=2 * half * WIDE * 16 * WIDE, bytes_accessed=half * WIDE * 40, transcendentals=0
        ),
        name="project_back",
    )(*dq, *qlin, *klin, *lane_rows, dk, dv, q_gain, k_gain)


def spread_back_kernel(*refs, chips, near):
    gl_ref, w_ref = refs[:2]
    got = refs[2:3] if near else ()
    outs, w_s = refs[2 + len(got) : -1], refs[-1]
    step = pl.program_id(0)

    @pl.when(step == 0)
    def _():
        assemble(w_s, w_ref)

    out = dot_nt(gl_ref[...], w_s[...])
    if near:
        out = (out + got[0][...].astype(F32)).astype(BF16)
        for r in range(chips):

            @pl.when(step == r)
            def _(r=r):
                outs[r][...] = out

    else:
        outs[0][...] = out.astype(BF16)


def spread_back(gl, w, chips, got=None):
    half, wide = gl.shape
    width = math.prod(w.shape[:-1])
    rows = half // chips
    near = got is not None
    row_block = lambda cols: pl.BlockSpec((rows, cols), lambda i: (i, 0))
    out_shape = [shaped((rows, width), BF16)] * chips if near else [shaped((half, width), BF16)]
    return pl.pallas_call(
        functools.partial(spread_back_kernel, chips=chips, near=near),
        grid=(chips,),
        in_specs=[row_block(wide), whole(w)] + ([row_block(width)] if near else []),
        out_specs=[whole(a) for a in out_shape] if near else [row_block(width)],
        out_shape=out_shape,
        scratch_shapes=[pltpu.VMEM((width, wide), BF16)],
        compiler_params=params(),
        cost_estimate=pl.CostEstimate(
            flops=2 * half * width * wide, bytes_accessed=half * width * 4, transcendentals=0
        ),
        name="spread_back",
    )(gl, w, *([got] if near else []))


def last_kernel(in_ref, *refs, z_count, shard):
    outs, small_ref = refs[:-1], refs[-1]
    seq_count = in_ref.shape[0] // z_count
    small = None
    for s in range(seq_count):
        total = None
        for f in range(z_count):
            block = in_ref[s * z_count + f].astype(F32)
            total = block if total is None else total + block
        for i, out_ref in enumerate(outs):
            out_ref[:, s * WIDE : (s + 1) * WIDE] = total[:shard, i * WIDE : (i + 1) * WIDE]
        small = total[shard:] if small is None else small + total[shard:]
    small_ref[...] = small


def last_sums(blocks, z_count, shard):
    count, rows, wide = blocks.shape
    seq_count = count // z_count
    return pl.pallas_call(
        functools.partial(last_kernel, z_count=z_count, shard=shard),
        out_shape=[shaped((shard, seq_count * WIDE), F32)] * 3 + [shaped((rows - shard, wide), F32)],
        compiler_params=params(False),
        name="last_sums",
    )(blocks)


def swap(x, seq_count, bits):
    return lax.ppermute(x, "seq", [(i, i ^ bits) for i in range(seq_count)])


def to_chips(x, seq_count):
    return [x] + [swap(x, seq_count, 2 * r) for r in range(1, seq_count // 2)]


def spread_slots(slots, seq_count):
    return [slots[0]] + [swap(slots[r], seq_count, 2 * r) for r in range(1, len(slots))]


def after(values, *others):
    kept, _ = lax.optimization_barrier((values, others))
    return kept


def add_up(parts):
    total = parts[0].astype(F32)
    for part in parts[1:]:
        total = total + part.astype(F32)
    return total


def body(
    tokens, weight_query, weight_key, weight_value, weight_out, weight_gate, weight_up, weight_down,
    norm_attn, norm_ffn, query_gain, key_gain, variate_bias, variate_ids, sample_ids, time_ids,
    out_grad,
):
    seq_count = lax.axis_size("seq")
    z_count = lax.axis_size("fsdp")
    everyone = seq_count * z_count
    chips = seq_count // 2
    _, rows, width = tokens.shape
    heads = variate_bias.shape[1]
    head_size = query_gain.shape[0]
    half_size = head_size // 2
    shard = weight_query.shape[0]
    features = heads * head_size
    hidden = weight_gate.shape[1] // seq_count
    me = lax.axis_index("seq")
    x_own = tokens.reshape(rows, width)
    dout_own = out_grad.reshape(rows, width)

    columns = columns_by_device(
        (weight_query, weight_key, weight_value, weight_gate, weight_up), seq_count
    )
    columns = lax.all_to_all(columns, "seq", split_axis=0, concat_axis=0, tiled=True)
    w_out_rows = lax.all_gather(weight_out, "fsdp", axis=0, tiled=True)
    columns = after(columns, w_out_rows)
    w_qkv = jnp.broadcast_to(
        columns[None, :, :, : 3 * WIDE], (z_count, seq_count, shard, 3 * WIDE)
    )
    w_qkv = gathered(lax.all_to_all(w_qkv, "fsdp", split_axis=0, concat_axis=0, tiled=True))
    w_down = lax.all_gather(weight_down, "fsdp", axis=0, tiled=True)
    if features < WIDE:
        w_out_rows = jnp.pad(w_out_rows, ((0, WIDE - features), (0, 0)))
    gu_columns = columns[:, :, 3 * WIDE :]
    w_gu = gathered(lax.all_gather(gu_columns, "fsdp", axis=0, tiled=False))

    ids = jnp.concatenate([variate_ids, sample_ids, time_ids // 64, time_ids % 64], axis=0)
    ids = jnp.pad(ids.astype(BF16), ((0, 12), (0, width - rows)))
    packed = after(jnp.concatenate([x_own, ids], axis=0), columns, w_out_rows)
    near_x = to_chips(packed, seq_count)
    extra = after(jnp.concatenate([dout_own, w_out_rows], axis=0), near_x[1:2])
    stack_x = jnp.concatenate(after(near_x, w_qkv, gu_columns, extra), axis=0)
    far_x = swap(stack_x, seq_count, 1)
    near_extra = to_chips(extra, seq_count)

    gain_attn = norm_attn.reshape(1, width)
    gain_ffn = norm_ffn.reshape(1, width)
    q_gain = jnp.tile(query_gain, WIDE // head_size).reshape(1, WIDE)
    k_gain = jnp.tile(key_gain, WIDE // head_size).reshape(1, WIDE)
    frequency = (10000.0 ** (-2.0 * jnp.arange(half_size).astype(F32) / head_size))[:, None]

    def projected(x):
        return project(
            x, chips, w_qkv, gain_attn, q_gain, k_gain, frequency, variate_bias, head_size
        )

    near_all = projected(stack_x)
    far_all = projected(far_x)
    nin, q_lin, k_lin, lane_rows, q_aug, k_aug, k_trans, v_aug = zip(near_all, far_all)
    attend_near = attend(q_aug[0], k_aug, v_aug, head_size)
    attend_far = attend(after(q_aug[1], attend_near, near_extra[1:2]), k_aug, v_aug, head_size)
    far_extra = [swap(e, seq_count, 1) for e in after(near_extra, attend_far)]
    mixed, o_full, z_inverse = zip(attend_near, attend_far)
    own_parts = [to_chips(mixed[side], seq_count) for side in (0, 1)]
    own_parts[0] = after(own_parts[0], attend_far)
    sib_stack = [swap(jnp.concatenate(own_parts[side], axis=0), seq_count, 1) for side in (0, 1)]

    nm_far, inner_far, ggu_far, dout_far, gnm_far, lay_far = ffn(
        1, own_parts[1], sib_stack[0], far_x, near_extra, far_extra, w_gu, w_down, gain_ffn
    )
    nm_near, inner_near, ggu_near, dout_near, middle, mixed_own, *slots = ffn(
        0, own_parts[0], sib_stack[1], stack_x, near_extra, far_extra, w_gu, w_down, gain_ffn,
        (swap(gnm_far, seq_count, 1), swap(lay_far, seq_count, 1)), group=16 // chips,
    )

    gnm_parts = spread_slots(slots[:chips], seq_count)
    grad_gu, grad_down, gnf = ffn_grads(
        (nm_near, nm_far), (ggu_near, ggu_far), (inner_near, inner_far), (dout_near, dout_far),
        w_gu, seq_count, z_count, swap(slots[0][:8, :WIDE], seq_count, 1),
    )
    me_row = jnp.reshape(me, (1,))
    grad_middle, grad_branch, g_out = middle_back(
        after(gnm_parts, grad_gu, grad_down),
        middle, gain_ffn, near_extra, far_extra, me_row,
    )
    g_all = lax.all_to_all(g_out, "seq", split_axis=0, concat_axis=0, tiled=True)

    grad_gu = lax.psum_scatter(grad_gu, "fsdp", scatter_dimension=0, tiled=True)
    grad_gu = grad_gu.reshape(seq_count, shard, 2 * hidden)
    grad_down = lax.psum_scatter(grad_down, "fsdp", scatter_dimension=0, tiled=True)
    grad_out = dot_tn(mixed_own, grad_branch).astype(BF16)
    half_out = chips * WIDE
    out_slots = add_up([grad_out[:half_out], swap(grad_out[half_out:], seq_count, 1)])
    out_slots = out_slots.astype(BF16)
    both_slots = [
        jnp.concatenate([slots[chips + r], out_slots[r * WIDE : (r + 1) * WIDE]], axis=0)
        for r in range(chips)
    ]
    both_parts = spread_slots(after(both_slots, g_all), seq_count)
    gu_got = lax.all_to_all(
        after(grad_gu, g_all), "seq", split_axis=0, concat_axis=0, tiled=True
    )

    dq_near, dq_far, dk, dv, bias_rows = attend_back(
        me_row, after(g_all, both_slots),
        q_aug, o_full, z_inverse, lane_rows, k_aug, k_trans, v_aug, head_size,
    )
    dq_far = after(dq_far, grad_gu, both_parts)
    gl_near, gl_far, gain_rows = project_back(
        (dq_near, dq_far), q_lin, k_lin, lane_rows, dk, dv, q_gain, k_gain, head_size, chips
    )
    (gni_far,) = spread_back(gl_far, w_qkv, chips)
    gni_got = swap(gni_far, seq_count, 1)
    grad_qkv, gna = pair_product(
        nin, (gl_near, gl_far), w_qkv, swap(gain_rows, seq_count, 1)
    )

    grad_qk_gain = gain_rows[:2, :features].reshape(2, heads, head_size).sum(axis=1)
    bias_cols = jnp.sum(bias_rows, axis=1).reshape(2, 2, 4).sum(axis=2)[:, :heads]
    bias_both = jnp.stack([bias_cols[0], bias_cols[1] - bias_cols[0]])
    bias_all = lax.dynamic_update_slice(
        jnp.zeros((2, heads * seq_count), F32), bias_both, (0, me * heads)
    )
    small = jnp.concatenate(
        [
            gna[0] / norm_attn,
            gnf / norm_ffn,
            grad_qk_gain.reshape(-1),
            bias_all.reshape(-1),
        ]
    )
    count = small.shape[0]
    small_rows = -(-count // (8 * 3 * WIDE)) * 8
    small = jnp.pad(small, (0, small_rows * 3 * WIDE - count)).astype(BF16)
    small = jnp.broadcast_to(small.reshape(1, small_rows, 3 * WIDE), (everyone, small_rows, 3 * WIDE))
    grad_qkv = after(grad_qkv, gu_got)
    blocks = jnp.concatenate([grad_qkv.reshape(everyone, shard, 3 * WIDE), small], axis=1)
    last = lax.all_to_all(blocks, ("seq", "fsdp"), split_axis=0, concat_axis=0, tiled=True)
    gni_slots = spread_back(
        gl_near, w_qkv, chips, after(gni_got, blocks)
    )
    gni_parts = spread_slots(gni_slots, seq_count)
    both = add_up(after(both_parts, gni_slots))
    grad_out = both[rows : rows + features]
    z_me = lax.axis_index("fsdp")
    bit = z_count // 2
    while bit:
        low, high = jnp.split(grad_out, 2, axis=0)
        upper = (z_me & bit) > 0
        away = jnp.where(upper, low, high).astype(BF16)
        away = lax.ppermute(away, "fsdp", [(i, i ^ bit) for i in range(z_count)])
        grad_out = jnp.where(upper, high, low) + away.astype(F32)
        bit //= 2
    in_grad = input_back(gni_parts, x_own, grad_middle, gain_attn)

    gu_got = after(gu_got, gni_slots)
    grad_down = after(grad_down, gni_parts[3:])
    layer_out = (middle + both[:rows]).astype(BF16)
    grad_gu = gu_got.transpose(1, 0, 2).astype(F32)
    grad_gate = grad_gu[:, :, :hidden].reshape(shard, seq_count * hidden)
    grad_up = grad_gu[:, :, hidden:].reshape(shard, seq_count * hidden)
    grad_down = grad_down.astype(F32)
    *grad_qkv, small = last_sums(after(last, in_grad, grad_out), z_count, shard)
    grad_query, grad_key, grad_value = (
        g.reshape(shard, seq_count, WIDE)[:, :, :features].reshape(shard, width)
        if features < WIDE
        else g
        for g in grad_qkv
    )
    small = small.reshape(-1)
    cut = 2 * width + 2 * head_size
    grad_bias = lax.dynamic_slice(
        small[cut:count].reshape(2, heads * seq_count), (0, me * heads), (2, heads)
    )
    return (
        layer_out.reshape(tokens.shape),
        in_grad.reshape(tokens.shape),
        grad_query,
        grad_key,
        grad_value,
        grad_out,
        grad_gate,
        grad_up,
        grad_down,
        small[:width],
        small[width : 2 * width],
        small[2 * width : 2 * width + head_size],
        small[2 * width + head_size : cut],
        grad_bias,
    )


def solution(mesh):
    rows = P("fsdp", "seq", None)
    shards = P(("seq", "fsdp"), None)
    ids = P("fsdp", "seq")
    bias = P(None, "seq")
    return jax.shard_map(
        body,
        mesh=mesh,
        in_specs=(rows,) + (shards,) * 7 + (P(),) * 4 + (bias, ids, ids, ids, rows),
        out_specs=(rows, rows) + (shards,) * 7 + (P(),) * 4 + (bias,),
        check_vma=False,
    )
```

```python
import functools
import math

import jax
import jax.numpy as jnp
from jax import lax
from jax.experimental import pallas as pl
from jax.experimental.pallas import tpu as pltpu
from jax.sharding import PartitionSpec as P

EPSILON = 1e-06
FAR = -1e30
LOG2E = math.log2(math.e)
WIDE = 128
ROWS_T = 160
F32 = jnp.float32
BF16 = jnp.bfloat16


def dot_nn(left, right):
    return jnp.dot(left, right, preferred_element_type=F32)


def dot_nt(left, right):
    return lax.dot_general(left, right, (((1,), (1,)), ((), ())), preferred_element_type=F32)


def dot_tn(left, right):
    return lax.dot_general(left, right, (((0,), (0,)), ((), ())), preferred_element_type=F32)


def rms_factor(values):
    return lax.rsqrt(jnp.mean(values * values, axis=-1, keepdims=True) + EPSILON)


def lanes_of(shape):
    return lax.broadcasted_iota(jnp.int32, shape, len(shape) - 1)


def head_sum(values, blocks):
    high = values.astype(BF16)
    low = (values - high.astype(F32)).astype(BF16)
    return dot_nn(high, blocks) + dot_nn(low, blocks)


def head_blocks(head_size):
    row = lax.broadcasted_iota(jnp.int32, (WIDE, WIDE), 0) // head_size
    column = lax.broadcasted_iota(jnp.int32, (WIDE, WIDE), 1) // head_size
    return jnp.where(row == column, 1.0, 0.0).astype(BF16)


def partner(values, lane, head_size):
    half = head_size // 2
    up = pltpu.roll(values, WIDE - half, 1)
    down = pltpu.roll(values, half, 1)
    return jnp.where(lane % head_size < half, up, down)


def tables(cosine, sine):
    times = WIDE // (2 * cosine.shape[0])
    cos_rows = jnp.concatenate([cosine, cosine] * times, axis=0)
    sin_rows = jnp.concatenate([-sine, sine] * times, axis=0)
    return cos_rows.T, sin_rows.T


def params(grid=True):
    return pltpu.CompilerParams(
        vmem_limit_bytes=60 * 1024 * 1024,
        dimension_semantics=("arbitrary",) if grid else None,
    )


def whole(array):
    return pl.BlockSpec(array.shape, lambda *_: (0,) * len(array.shape))


def shaped(shape, dtype):
    return jax.ShapeDtypeStruct(shape, dtype)


ANY = pl.BlockSpec(memory_space=pl.ANY)


def assemble(out_ref, in_ref):
    if len(in_ref.shape) == 2:
        out_ref[...] = in_ref[...]
        return
    z_count, seq_count, shard, _ = in_ref.shape
    for f in range(z_count):
        for s in range(seq_count):
            at = (s * z_count + f) * shard
            out_ref[at : at + shard, :] = in_ref[f, s]


def gathered(w):
    if w.shape[2] % 16 == 0:
        return w
    return w.transpose(1, 0, 2, 3).reshape(-1, w.shape[-1])


def columns_kernel(*refs):
    *weights, out_ref = refs
    at = 0
    for w_ref in weights:
        wide = w_ref.shape[1] // out_ref.shape[0]
        for s in range(out_ref.shape[0]):
            out_ref[s, :, at : at + wide] = w_ref[:, s * wide : (s + 1) * wide]
        at += wide


def columns_by_device(weights, seq_count):
    shard = weights[0].shape[0]
    wides = [w.shape[1] // seq_count for w in weights]
    if shard % 16 == 0 and all(wide % WIDE == 0 for wide in wides):
        return pl.pallas_call(
            columns_kernel,
            out_shape=shaped((seq_count, shard, sum(wides)), BF16),
            compiler_params=params(False),
            name="columns",
        )(*weights)
    pieces = []
    for w, wide in zip(weights, wides):
        short = -wide % WIDE
        pieces.append(jnp.pad(w.reshape(shard, seq_count, wide), ((0, 0), (0, 0), (0, short))))
    return jnp.concatenate(pieces, axis=2).transpose(1, 0, 2)


def project_kernel(
    x_ref, w_ref, na_ref, qg_ref, kg_ref, freq_ref, bias_ref,
    nin_ref, qlin_ref, klin_ref, lane_ref, qa_ref, ka_ref, kt_ref, v1_ref, w_s, *, heads, head_size,
):
    half = head_size // 2
    rows = nin_ref.shape[0]

    @pl.when(pl.program_id(0) == 0)
    def _():
        assemble(w_s, w_ref)

    x = x_ref[:rows, :].astype(F32)
    ids = x_ref[rows:, :rows].astype(F32)
    nin = (x * rms_factor(x) * na_ref[...]).astype(BF16)
    nin_ref[...] = nin
    lin = dot_nn(nin, w_s[...])
    q, k, v = lin[:, :WIDE], lin[:, WIDE : 2 * WIDE], lin[:, 2 * WIDE :]
    qlin_ref[...] = q
    klin_ref[...] = k
    angles = freq_ref[...] * (ids[2:3] * 64.0 + ids[3:4])
    cosine, sine = jnp.cos(angles), jnp.sin(angles)
    lane_ref[...] = jnp.concatenate([cosine, sine, ids[:8]], axis=0)
    cosine, sine = tables(cosine, sine)
    lane = lanes_of((rows, WIDE))
    blocks = head_blocks(head_size)

    def finish(u, gain):
        factor = lax.rsqrt(head_sum(u * u, blocks) * (1.0 / head_size) + EPSILON)
        u = u * factor * gain
        return u * cosine + partner(u, lane, head_size) * sine

    q = finish(q, qg_ref[...]) * (LOG2E * head_size**-0.5)
    k = finish(k, kg_ref[...])
    few = ROWS_T - WIDE
    row = lax.broadcasted_iota(jnp.int32, (few, rows), 0)
    variate = ids[0:1].astype(jnp.int32)
    sample = ids[1:2].astype(jnp.int32)
    same_variate = (row % 4) == variate
    same_sample = (row - 10) == sample
    one = jnp.ones((few, rows), F32)
    nil = jnp.zeros((few, rows), F32)
    rest = jnp.zeros((WIDE - few, rows), F32)

    def columns(few_rows):
        return jnp.concatenate([few_rows, rest], axis=0).T

    aug_q = jnp.where(
        row < 8,
        jnp.where(same_variate, one, nil),
        jnp.where(row < 10, one, jnp.where((row < 13) & same_sample, one, nil)),
    )
    qa_ref[...] = jnp.concatenate([q, columns(aug_q)], axis=1).astype(BF16)
    k_t = k.T
    row_k = lax.broadcasted_iota(jnp.int32, (WIDE, rows), 0)
    for h in range(heads):
        first, second = bias_ref[0, h] * LOG2E, bias_ref[1, h] * LOG2E
        step_up = jnp.where(row < 8, first - second, second) * one
        high = step_up.astype(BF16).astype(F32)
        low = step_up - high
        far = jnp.where(same_sample, nil, FAR)
        plain = jnp.where(((row // 4) == 4 + h) & same_variate, one, nil)
        aug_k = jnp.where(
            row < 4,
            jnp.where(same_variate, high, nil),
            jnp.where(
                row < 8,
                jnp.where(same_variate, low, nil),
                jnp.where(
                    row == 8,
                    high,
                    jnp.where(row == 9, low, jnp.where(row < 13, far, plain)),
                ),
            ),
        )
        mine = (lane // head_size) == h
        mine_t = (row_k // head_size) == h
        ka_ref[h] = jnp.concatenate([jnp.where(mine, k, 0.0), columns(aug_k)], axis=1).astype(BF16)
        kt_ref[h] = jnp.concatenate([jnp.where(mine_t, k_t, 0.0), aug_k], axis=0).astype(BF16)
        ones_v = jnp.where((lane == h) | (lane == 2 + h), 1.0, 0.0)
        v1_ref[h] = jnp.concatenate([jnp.where(mine, v, 0.0), ones_v], axis=1).astype(BF16)


def project(x, chips, w, norm_attn, q_gain, k_gain, freq, bias, head_size):
    width, wide = x.shape[1], w.shape[-1]
    rows = x.shape[0] // chips - 16
    heads = bias.shape[1]
    half = chips * rows
    count = head_size + 8
    row_block = lambda cols: pl.BlockSpec((rows, cols), lambda i: (i, 0))
    lane_block = pl.BlockSpec((count, rows), lambda i: (0, i))
    head_block = pl.BlockSpec((heads, rows, 2 * WIDE), lambda i: (0, i, 0))
    return pl.pallas_call(
        functools.partial(project_kernel, heads=heads, head_size=head_size),
        grid=(chips,),
        in_specs=[pl.BlockSpec((rows + 16, width), lambda i: (i, 0))]
        + [whole(a) for a in (w, norm_attn, q_gain, k_gain, freq)]
        + [pl.BlockSpec(memory_space=pltpu.SMEM)],
        out_specs=[
            row_block(width), row_block(WIDE), row_block(WIDE), lane_block, row_block(2 * WIDE),
            head_block, pl.BlockSpec((heads, ROWS_T, rows), lambda i: (0, 0, i)), head_block,
        ],
        out_shape=[
            shaped((half, width), BF16),
            shaped((half, WIDE), F32),
            shaped((half, WIDE), F32),
            shaped((count, half), F32),
            shaped((half, 2 * WIDE), BF16),
            shaped((heads, half, 2 * WIDE), BF16),
            shaped((heads, ROWS_T, half), BF16),
            shaped((heads, half, 2 * WIDE), BF16),
        ],
        scratch_shapes=[pltpu.VMEM((width, wide), BF16)],
        compiler_params=params(),
        cost_estimate=pl.CostEstimate(
            flops=2 * half * width * 3 * WIDE, bytes_accessed=half * width * 8, transcendentals=0
        ),
        name="project",
    )(x, w, norm_attn, q_gain, k_gain, freq, bias)


def attend_kernel(qa_ref, ka0, ka1, v10, v11, mixed_ref, o_ref, zi_ref, *, heads, head_size, chunk):
    qa = qa_ref[...]
    rows = qa.shape[0]
    half = ka0.shape[1]
    lane = lanes_of((rows, WIDE))
    total = jnp.zeros((rows, WIDE), F32)
    inverse = jnp.ones((rows, WIDE), F32)
    for h in range(heads):
        acc = jnp.zeros((rows, 2 * WIDE), F32)
        for ka_ref, v1_ref in ((ka0, v10), (ka1, v11)):
            for c in range(half // chunk):
                part = pl.ds(c * chunk, chunk)
                e = jnp.exp2(dot_nt(qa, ka_ref[h, part, :])).astype(BF16)
                acc = acc + dot_nn(e, v1_ref[h, part, :])
        z_inv = 1.0 / acc[:, WIDE + h : WIDE + h + 1]
        total = total + acc[:, :WIDE] * z_inv
        inverse = jnp.where((lane // head_size) == h, z_inv, inverse)
    mixed_ref[...] = total.astype(BF16)
    o_ref[...] = total
    zi_ref[...] = inverse


def attend(qa, ka, v1, head_size, block=512, chunk=256):
    heads, half, _ = ka[0].shape
    out_block = pl.BlockSpec((block, WIDE), lambda i: (i, 0))
    return pl.pallas_call(
        functools.partial(attend_kernel, heads=heads, head_size=head_size, chunk=chunk),
        grid=(half // block,),
        in_specs=[pl.BlockSpec((block, 2 * WIDE), lambda i: (i, 0))]
        + [whole(a) for a in (*ka, *v1)],
        out_specs=[out_block, out_block, out_block],
        out_shape=[shaped((half, WIDE), BF16), shaped((half, WIDE), F32), shaped((half, WIDE), F32)],
        compiler_params=params(),
        cost_estimate=pl.CostEstimate(
            flops=2 * heads * half * half * 8 * WIDE,
            bytes_accessed=half * WIDE * 32,
            transcendentals=2 * heads * half * half,
        ),
        name="attend",
    )(qa, *ka, *v1)


def attend_back_kernel(*refs, chips, heads, head_size, chunk):
    me_ref, g_ref = refs[:2]
    at = 2
    qa, o, zi, lanes, ka, kt, v1 = [refs[at + 2 * n : at + 2 * n + 2] for n in range(7)]
    at += 14
    dq_refs = refs[at : at + 2]
    dk_ref, dv_ref, bias_ref, g_s, dk_s, dv_s = refs[at + 2 :]
    step = pl.program_id(0)

    @pl.when(step == 0)
    def _():
        dk_s[...] = jnp.zeros_like(dk_s)
        dv_s[...] = jnp.zeros_like(dv_s)
        bias_ref[...] = jnp.zeros_like(bias_ref)
        for j in range(2 * chips):
            g_s[j % 2, j // 2] = g_ref[me_ref[0] ^ j]

    for side in range(2):
        q_rows = qa[side][...]
        rows = q_rows.shape[0]
        half_len = ka[0].shape[1]
        lane = lanes_of((rows, WIDE))
        q = q_rows[:, :WIDE]
        gz = (g_s[side, step].astype(F32) * zi[side][...]).astype(BF16)
        inner = gz.astype(F32) * o[side][...]
        aug = jnp.zeros((rows, WIDE), F32)
        for h in range(heads):
            mean = -jnp.sum(
                jnp.where((lane // head_size) == h, inner, 0.0), axis=-1, keepdims=True
            ) * jnp.ones((rows, WIDE), F32)
            high = mean.astype(BF16).astype(F32)
            aug = jnp.where(lane == h, high, jnp.where(lane == 2 + h, mean - high, aug))
        ga = jnp.concatenate([gz, aug.astype(BF16)], axis=1)
        dq_t = jnp.zeros((ROWS_T, rows), F32)
        for h in range(heads):
            mine = (lane // head_size) == h
            q_h = jnp.where(mine, q, jnp.zeros_like(q))
            g_h = jnp.where(mine, gz, jnp.zeros_like(gz))
            for other in range(2):
                for c in range(half_len // chunk):
                    part = pl.ds(c * chunk, chunk)
                    e = jnp.exp2(dot_nt(ka[other][h, part, :], q_rows))
                    ds = (e * dot_nt(v1[other][h, part, :], ga)).astype(BF16)
                    dv_s[other, part, :] += dot_nn(e.astype(BF16), g_h)
                    dk_s[other, part, :] += dot_nn(ds, q_h)
                    dq_t = dq_t + dot_nn(kt[other][h, :, part], ds)
        dq_refs[side][...] = (dq_t[:WIDE].T * (head_size**-0.5)).astype(BF16)
        variate = lanes[side][head_size : head_size + 1, :].astype(jnp.int32)
        columns = dq_t[WIDE + 16 : WIDE + 24]
        row = lax.broadcasted_iota(jnp.int32, columns.shape, 0)
        bias_ref[...] += jnp.concatenate(
            [jnp.where((row % 4) == variate, columns, 0.0), columns], axis=0
        )

    @pl.when(step == pl.num_programs(0) - 1)
    def _():
        dk_ref[...] = (dk_s[...] * (1.0 / LOG2E)).astype(BF16)
        dv_ref[...] = dv_s[...].astype(BF16)


def attend_back(me, g, qa, o, zi, lane_rows, ka, kt, v1, head_size, chunk=1024):
    heads, half, _ = ka[0].shape
    chips = g.shape[0] // 2
    chunk = math.gcd(half, chunk)
    block = half // chips
    count = lane_rows[0].shape[0]
    row_block = lambda cols: pl.BlockSpec((block, cols), lambda i: (i, 0))
    lane_block = pl.BlockSpec((count, block), lambda i: (0, i))
    full = shaped((2, half, WIDE), BF16)
    return pl.pallas_call(
        functools.partial(
            attend_back_kernel, chips=chips, heads=heads, head_size=head_size, chunk=chunk
        ),
        grid=(chips,),
        in_specs=[pl.BlockSpec(memory_space=pltpu.SMEM), whole(g)]
        + [row_block(2 * WIDE)] * 2
        + [row_block(WIDE)] * 4
        + [lane_block] * 2
        + [whole(a) for a in (*ka, *kt, *v1)],
        out_specs=[row_block(WIDE)] * 2
        + [whole(full), whole(full), pl.BlockSpec((16, block), lambda i: (0, 0))],
        out_shape=[shaped((half, WIDE), BF16)] * 2 + [full, full, shaped((16, block), F32)],
        scratch_shapes=[
            pltpu.VMEM((2, chips, block, WIDE), BF16),
            pltpu.VMEM((2, half, WIDE), F32),
            pltpu.VMEM((2, half, WIDE), F32),
        ],
        compiler_params=params(),
        cost_estimate=pl.CostEstimate(
            flops=2 * heads * half * half * 32 * WIDE,
            bytes_accessed=half * WIDE * 64,
            transcendentals=4 * heads * half * half,
        ),
        name="attend_back",
    )(me, g, *qa, *o, *zi, *lane_rows, *ka, *kt, *v1)


def ffn_kernel(*refs, chips, group, near):
    mixed = refs[: 2 * chips]
    extra_parts = refs[2 * chips : 4 * chips]
    at = 4 * chips
    x_ref, wgu_ref, wd_ref, nf_ref = refs[at : at + 4]
    at += 4
    if near:
        got_ref = refs[at]
        at += 1
    nm_ref, inner_ref, ggu_ref, dout_ref = refs[at : at + 4]
    at += 4
    if near:
        mid_ref, mixed_ref = refs[at : at + 2]
        gnm_refs = refs[at + 2 : at + 2 + chips]
        lay_refs = refs[at + 2 + chips : at + 2 + 2 * chips]
        at += 2 + 2 * chips
    else:
        gnm_ref, lay_ref = refs[at : at + 2]
        at += 2
    w_s, wo_s, extra_s, sems = refs[at:]
    step = pl.program_id(0)
    rows = nm_ref.shape[0] // group

    @pl.when(step == 0)
    def _():
        copies = [
            pltpu.make_async_copy(part, extra_s.at[j], sems.at[j])
            for j, part in enumerate(extra_parts)
        ]
        for copy in copies:
            copy.start()
        assemble(w_s, wgu_ref)
        for j, copy in enumerate(copies):
            copy.wait()
            wo_s[j * WIDE : (j + 1) * WIDE, :] = extra_s[j, rows:, :]

    def own_order(block, r):
        if r % group == 0:
            return block
        slots = [(t ^ (r % group)) * rows for t in range(group)]
        return jnp.concatenate([block[at : at + rows] for at in slots], axis=0)

    cat = jnp.concatenate([own_order(m[...], j % chips) for j, m in enumerate(mixed)], axis=1)
    hidden = wd_ref.shape[0]
    x = [x_ref[t * (rows + 16) : t * (rows + 16) + rows, :] for t in range(group)]
    first = (0 if near else chips) + step * group
    dout = jnp.concatenate([extra_s[first + t, :rows, :] for t in range(group)], axis=0)
    dout_ref[...] = dout
    middle = jnp.concatenate(x, axis=0).astype(F32) + dot_nn(cat, wo_s[...])
    nm = (middle * rms_factor(middle) * nf_ref[...]).astype(BF16)
    nm_ref[...] = nm
    lin = dot_nn(nm, w_s[...])
    back = dot_nt(dout, wd_ref[...])
    gate, up = lin[:, :hidden], lin[:, hidden:]
    sig = jax.nn.sigmoid(gate)
    silu = gate * sig
    inner = (silu * up).astype(BF16)
    inner_ref[...] = inner
    g_gate = (back * up * (sig * (1.0 + gate * (1.0 - sig)))).astype(BF16)
    g_up = (back * silu).astype(BF16)
    ggu = jnp.concatenate([g_gate, g_up], axis=1)
    ggu_ref[...] = ggu
    gnm = dot_nt(ggu, w_s[...])
    lay = dot_nn(inner, wd_ref[...])
    if near:

        @pl.when(step == 0)
        def _():
            mid_ref[...] = middle[:rows]
            mixed_ref[...] = cat[:rows]

        gnm = (gnm + got_ref[...].astype(F32)).astype(BF16)
        lay = lay.astype(BF16)
        for r in range(chips):

            @pl.when(step == r // group)
            def _(r=r):
                at = (r % group) * rows
                gnm_refs[r][...] = gnm[at : at + rows]
                lay_refs[r][...] = lay[at : at + rows]

    else:
        gnm_ref[...] = gnm.astype(BF16)
        lay_ref[...] = lay.astype(BF16)


def ffn(
    side, own_parts, sib_stack, x, near_extra, far_extra, wgu, wd, norm_ffn, got=None, group=2
):
    chips = len(own_parts)
    group = math.gcd(chips, group)
    rows, width = near_extra[0].shape
    rows -= WIDE
    half = rows * chips
    block = rows * group
    steps = chips // group
    hidden = wd.shape[0]
    near = side == 0
    row_block = lambda cols: pl.BlockSpec((block, cols), lambda i: (i, 0))
    piece = lambda r: pl.BlockSpec((block, WIDE), lambda i: (i ^ (r // group), 0))
    stack = lambda r: pl.BlockSpec((block, WIDE), lambda i: (r * steps + (i ^ (r // group)), 0))
    out_shape = [
        shaped((half, width), BF16), shaped((half, hidden), BF16), shaped((half, 2 * hidden), BF16),
        shaped((half, width), BF16),
    ]
    out_specs = [row_block(width), row_block(hidden), row_block(2 * hidden), row_block(width)]
    if near:
        more = [shaped((rows, width), F32), shaped((rows, 2 * chips * WIDE), BF16)]
        more += [shaped((rows, width), BF16)] * (2 * chips)
        out_shape += more
        out_specs += [whole(a) for a in more]
    else:
        out_shape += [shaped((half, width), BF16)] * 2
        out_specs += [row_block(width)] * 2
    return pl.pallas_call(
        functools.partial(ffn_kernel, chips=chips, group=group, near=near),
        grid=(steps,),
        in_specs=[piece(r) for r in range(chips)]
        + [stack(r) for r in range(chips)]
        + [ANY] * (2 * chips)
        + [pl.BlockSpec((group * (rows + 16), width), lambda i: (i, 0))]
        + [whole(a) for a in (wgu, wd, norm_ffn)]
        + ([row_block(width)] if near else []),
        out_specs=out_specs,
        out_shape=out_shape,
        scratch_shapes=[
            pltpu.VMEM((width, 2 * hidden), BF16),
            pltpu.VMEM((2 * chips * WIDE, width), BF16),
            pltpu.VMEM((2 * chips, rows + WIDE, width), BF16),
            pltpu.SemaphoreType.DMA((2 * chips,)),
        ],
        compiler_params=params(),
        cost_estimate=pl.CostEstimate(
            flops=2 * half * width * (2 * chips * WIDE + 6 * hidden),
            bytes_accessed=half * width * 12,
            transcendentals=half * hidden,
        ),
        name="ffn_half",
    )(
        *own_parts, *[sib_stack] * chips, *near_extra, *far_extra, x, wgu, wd, norm_ffn,
        *([got] if near else []),
    )


def row_sums(product, w_ref):
    w = w_ref[...].astype(F32)
    if len(w.shape) == 4:
        z_count, parts, _, _ = w.shape
        w = jnp.concatenate([w[f, s] for s in range(parts) for f in range(z_count)], axis=0)
    total = jnp.sum(product * w, axis=1, keepdims=True)
    return (total * jnp.ones((product.shape[0], WIDE), F32)).T[:8]


def block_of(w, steps):
    if len(w.shape) == 2:
        return pl.BlockSpec((w.shape[0] // steps, w.shape[1]), lambda i: (i, 0))
    block = (w.shape[0], w.shape[1] // steps) + w.shape[2:]
    return pl.BlockSpec(block, lambda i: (0, i, 0, 0))


def ffn_grads_kernel(nm0, nm1, ggu0, ggu1, in0, in1, dout0, dout1, w_ref, _, gu_ref, gd_ref, sum_ref):
    gu = dot_tn(nm0[...], ggu0[...]) + dot_tn(nm1[...], ggu1[...])
    sum_ref[...] = row_sums(gu, w_ref)
    gu = gu.astype(BF16)
    if len(gu_ref.shape) == 2:
        gu_ref[...] = gu
    else:
        z_count, parts, shard, _ = gu_ref.shape
        for f in range(z_count):
            for s in range(parts):
                at = (s * z_count + f) * shard
                gu_ref[f, s] = gu[at : at + shard]
    gd_ref[...] = (dot_tn(in0[...], dout0[...]) + dot_tn(in1[...], dout1[...])).astype(BF16)


def ffn_grads(nm, ggu, inner, dout, w, seq_count, z_count, ticket):
    half, width = nm[0].shape
    hidden = inner[0].shape[1]
    shard = width // (seq_count * z_count)
    steps = max(1, min(4, hidden // WIDE))
    column_block = lambda cols: pl.BlockSpec((half, cols // steps), lambda i: (0, i))
    if shard % 16 == 0 and seq_count % steps == 0:
        gu = shaped((z_count, seq_count, shard, 2 * hidden), BF16)
        gu_spec = pl.BlockSpec(
            (z_count, seq_count // steps, shard, 2 * hidden), lambda i: (0, i, 0, 0)
        )
    else:
        gu = shaped((width, 2 * hidden), BF16)
        gu_spec = pl.BlockSpec((width // steps, 2 * hidden), lambda i: (i, 0))
    gu, gd, sums = pl.pallas_call(
        ffn_grads_kernel,
        grid=(steps,),
        in_specs=[column_block(width)] * 2
        + [whole(a) for a in ggu]
        + [column_block(hidden)] * 2
        + [whole(a) for a in dout]
        + [block_of(w, steps), ANY],
        out_specs=[
            gu_spec,
            pl.BlockSpec((hidden // steps, width), lambda i: (i, 0)),
            pl.BlockSpec((8, width // steps), lambda i: (0, i)),
        ],
        out_shape=[gu, shaped((hidden, width), BF16), shaped((8, width), F32)],
        compiler_params=params(),
        cost_estimate=pl.CostEstimate(
            flops=2 * half * width * 6 * hidden, bytes_accessed=half * width * 16, transcendentals=0
        ),
        name="ffn_grads",
    )(*nm, *ggu, *inner, *dout, w, ticket)
    if len(gu.shape) == 2:
        gu = gu.reshape(seq_count, z_count, shard, 2 * hidden).transpose(1, 0, 2, 3)
    return gu.reshape(width, 2 * hidden), gd, sums[0]


def pair_kernel(a0, a1, b0, b1, w_ref, _, out_ref, sum_ref):
    product = dot_tn(a0[...], b0[...]) + dot_tn(a1[...], b1[...])
    out_ref[...] = product.astype(BF16)
    sum_ref[...] = row_sums(product, w_ref)


def pair_product(left, right, w, ticket, steps=4):
    half, width = left[0].shape
    wide = right[0].shape[1]
    return pl.pallas_call(
        pair_kernel,
        grid=(steps,),
        in_specs=[pl.BlockSpec((half, width // steps), lambda i: (0, i))] * 2
        + [whole(a) for a in right]
        + [block_of(w, steps), ANY],
        out_specs=[
            pl.BlockSpec((width // steps, wide), lambda i: (i, 0)),
            pl.BlockSpec((8, width // steps), lambda i: (0, i)),
        ],
        out_shape=[shaped((width, wide), BF16), shaped((8, width), F32)],
        compiler_params=params(),
        cost_estimate=pl.CostEstimate(
            flops=4 * half * width * wide, bytes_accessed=half * width * 6, transcendentals=0
        ),
        name="pair_product",
    )(*left, *right, w, ticket)


def added(pieces):
    total = pieces[0][...].astype(F32)
    for piece in pieces[1:]:
        total = total + piece[...].astype(F32)
    return total


def norm_back(values, gain, incoming):
    factor = rms_factor(values)
    weighted = incoming * gain
    return factor * weighted - values * (factor * factor * factor) * jnp.mean(
        weighted * values, axis=-1, keepdims=True
    )


def middle_back_kernel(*refs, chips):
    extra = refs[chips : 3 * chips]
    mid_ref, nf_ref, me_ref, gm_ref, gb_ref, out_ref = refs[3 * chips :]
    rows = mid_ref.shape[0]
    grad = extra[0][:rows, :].astype(F32) + norm_back(mid_ref[...], nf_ref[...], added(refs[:chips]))
    gm_ref[...] = grad
    branch = grad.astype(BF16)
    gb_ref[...] = branch
    for side in range(2):
        for r in range(chips):
            part = dot_nt(branch, extra[side * chips + r][rows:, :])
            out_ref[me_ref[0] ^ (2 * r + side)] = part.astype(BF16)


def middle_back(pieces, middle, norm_ffn, near_extra, far_extra, me):
    chips = len(pieces)
    rows, width = middle.shape
    vmem = pl.BlockSpec(memory_space=pltpu.VMEM)
    return pl.pallas_call(
        functools.partial(middle_back_kernel, chips=chips),
        in_specs=[vmem] * (3 * chips + 2) + [pl.BlockSpec(memory_space=pltpu.SMEM)],
        out_shape=[
            shaped((rows, width), F32), shaped((rows, width), BF16),
            shaped((2 * chips, rows, WIDE), BF16),
        ],
        compiler_params=params(False),
        cost_estimate=pl.CostEstimate(
            flops=2 * rows * width * 2 * chips * WIDE,
            bytes_accessed=rows * width * 12,
            transcendentals=0,
        ),
        name="middle_back",
    )(*pieces, *near_extra, *far_extra, middle, norm_ffn, me)


def input_back_kernel(*refs, chips):
    x_ref, gm_ref, na_ref, out_ref = refs[chips:]
    out_ref[...] = gm_ref[...] + norm_back(x_ref[...].astype(F32), na_ref[...], added(refs[:chips]))


def input_back(pieces, x, grad_middle, norm_attn):
    return pl.pallas_call(
        functools.partial(input_back_kernel, chips=len(pieces)),
        out_shape=shaped(x.shape, F32),
        compiler_params=params(False),
        name="input_back",
    )(*pieces, x, grad_middle, norm_attn)


def project_back_kernel(*refs, head_size):
    dq, qlin, klin, lanes = refs[0:2], refs[2:4], refs[4:6], refs[6:8]
    dk_ref, dv_ref, qg_ref, kg_ref = refs[8:12]
    gl, gain_ref = refs[12:14], refs[14]
    half = head_size // 2
    rows = qlin[0].shape[0]
    lane = lanes_of((rows, WIDE))
    blocks = head_blocks(head_size)

    @pl.when(pl.program_id(0) == 0)
    def _():
        gain_ref[...] = jnp.zeros_like(gain_ref)

    for side in range(2):
        cosine, sine = tables(lanes[side][:half, :], lanes[side][half : 2 * half, :])

        def back(grad, u, gain, at):
            grad = grad.astype(F32)
            grad = grad * cosine - partner(grad, lane, head_size) * sine
            factor = lax.rsqrt(head_sum(u * u, blocks) * (1.0 / head_size) + EPSILON)
            gain_ref[at : at + 1, :] += jnp.sum(grad * u * factor, axis=0, keepdims=True)
            weighted = grad * gain
            mean = head_sum(weighted * u, blocks) * (1.0 / head_size)
            return (factor * weighted - u * (factor * factor * factor) * mean).astype(BF16)

        gq = back(dq[side][...], qlin[side][...], qg_ref[...], 0)
        gk = back(dk_ref[side], klin[side][...], kg_ref[...], 1)
        gl[side][...] = jnp.concatenate([gq, gk, dv_ref[side]], axis=1)


def project_back(dq, qlin, klin, lane_rows, dk, dv, q_gain, k_gain, head_size, chips):
    half = qlin[0].shape[0]
    rows = half // chips
    count = lane_rows[0].shape[0]
    row_block = lambda cols: pl.BlockSpec((rows, cols), lambda i: (i, 0))
    both = pl.BlockSpec((2, rows, WIDE), lambda i: (0, i, 0))
    gain = shaped((8, WIDE), F32)
    return pl.pallas_call(
        functools.partial(project_back_kernel, head_size=head_size),
        grid=(chips,),
        in_specs=[row_block(WIDE)] * 6
        + [pl.BlockSpec((count, rows), lambda i: (0, i))] * 2
        + [both, both, whole(q_gain), whole(k_gain)],
        out_specs=[row_block(3 * WIDE), row_block(3 * WIDE), whole(gain)],
        out_shape=[shaped((half, 3 * WIDE), BF16)] * 2 + [gain],
        compiler_params=params(),
        cost_estimate=pl.CostEstimate(
            flops=2 * half * WIDE * 16 * WIDE, bytes_accessed=half * WIDE * 40, transcendentals=0
        ),
        name="project_back",
    )(*dq, *qlin, *klin, *lane_rows, dk, dv, q_gain, k_gain)


def spread_back_kernel(*refs, chips, near):
    gl_ref, w_ref = refs[:2]
    got = refs[2:3] if near else ()
    outs, w_s = refs[2 + len(got) : -1], refs[-1]
    step = pl.program_id(0)

    @pl.when(step == 0)
    def _():
        assemble(w_s, w_ref)

    out = dot_nt(gl_ref[...], w_s[...])
    if near:
        out = (out + got[0][...].astype(F32)).astype(BF16)
        for r in range(chips):

            @pl.when(step == r)
            def _(r=r):
                outs[r][...] = out

    else:
        outs[0][...] = out.astype(BF16)


def spread_back(gl, w, chips, got=None):
    half, wide = gl.shape
    width = math.prod(w.shape[:-1])
    rows = half // chips
    near = got is not None
    row_block = lambda cols: pl.BlockSpec((rows, cols), lambda i: (i, 0))
    out_shape = [shaped((rows, width), BF16)] * chips if near else [shaped((half, width), BF16)]
    return pl.pallas_call(
        functools.partial(spread_back_kernel, chips=chips, near=near),
        grid=(chips,),
        in_specs=[row_block(wide), whole(w)] + ([row_block(width)] if near else []),
        out_specs=[whole(a) for a in out_shape] if near else [row_block(width)],
        out_shape=out_shape,
        scratch_shapes=[pltpu.VMEM((width, wide), BF16)],
        compiler_params=params(),
        cost_estimate=pl.CostEstimate(
            flops=2 * half * width * wide, bytes_accessed=half * width * 4, transcendentals=0
        ),
        name="spread_back",
    )(gl, w, *([got] if near else []))


def last_kernel(in_ref, *refs, z_count, shard):
    outs, small_ref = refs[:-1], refs[-1]
    seq_count = in_ref.shape[0] // z_count
    small = None
    for s in range(seq_count):
        total = None
        for f in range(z_count):
            block = in_ref[s * z_count + f].astype(F32)
            total = block if total is None else total + block
        for i, out_ref in enumerate(outs):
            out_ref[:, s * WIDE : (s + 1) * WIDE] = total[:shard, i * WIDE : (i + 1) * WIDE]
        small = total[shard:] if small is None else small + total[shard:]
    small_ref[...] = small


def last_sums(blocks, z_count, shard):
    count, rows, wide = blocks.shape
    seq_count = count // z_count
    return pl.pallas_call(
        functools.partial(last_kernel, z_count=z_count, shard=shard),
        out_shape=[shaped((shard, seq_count * WIDE), F32)] * 3 + [shaped((rows - shard, wide), F32)],
        compiler_params=params(False),
        name="last_sums",
    )(blocks)


def swap(x, seq_count, bits):
    return lax.ppermute(x, "seq", [(i, i ^ bits) for i in range(seq_count)])


def to_chips(x, seq_count):
    return [x] + [swap(x, seq_count, 2 * r) for r in range(1, seq_count // 2)]


def spread_slots(slots, seq_count):
    return [slots[0]] + [swap(slots[r], seq_count, 2 * r) for r in range(1, len(slots))]


def after(values, *others):
    kept, _ = lax.optimization_barrier((values, others))
    return kept


def add_up(parts):
    total = parts[0].astype(F32)
    for part in parts[1:]:
        total = total + part.astype(F32)
    return total


def body(
    tokens, weight_query, weight_key, weight_value, weight_out, weight_gate, weight_up, weight_down,
    norm_attn, norm_ffn, query_gain, key_gain, variate_bias, variate_ids, sample_ids, time_ids,
    out_grad,
):
    seq_count = lax.axis_size("seq")
    z_count = lax.axis_size("fsdp")
    everyone = seq_count * z_count
    chips = seq_count // 2
    _, rows, width = tokens.shape
    heads = variate_bias.shape[1]
    head_size = query_gain.shape[0]
    half_size = head_size // 2
    shard = weight_query.shape[0]
    features = heads * head_size
    hidden = weight_gate.shape[1] // seq_count
    me = lax.axis_index("seq")
    x_own = tokens.reshape(rows, width)
    dout_own = out_grad.reshape(rows, width)

    columns = columns_by_device(
        (weight_query, weight_key, weight_value, weight_gate, weight_up), seq_count
    )
    columns = lax.all_to_all(columns, "seq", split_axis=0, concat_axis=0, tiled=True)
    w_out_rows = lax.all_gather(weight_out, "fsdp", axis=0, tiled=True)
    columns = after(columns, w_out_rows)
    w_qkv = jnp.broadcast_to(
        columns[None, :, :, : 3 * WIDE], (z_count, seq_count, shard, 3 * WIDE)
    )
    w_qkv = gathered(lax.all_to_all(w_qkv, "fsdp", split_axis=0, concat_axis=0, tiled=True))
    w_down = lax.all_gather(weight_down, "fsdp", axis=0, tiled=True)
    if features < WIDE:
        w_out_rows = jnp.pad(w_out_rows, ((0, WIDE - features), (0, 0)))
    gu_columns = columns[:, :, 3 * WIDE :]
    w_gu = gathered(lax.all_gather(gu_columns, "fsdp", axis=0, tiled=False))

    ids = jnp.concatenate([variate_ids, sample_ids, time_ids // 64, time_ids % 64], axis=0)
    ids = jnp.pad(ids.astype(BF16), ((0, 12), (0, width - rows)))
    packed = after(jnp.concatenate([x_own, ids], axis=0), columns, w_out_rows)
    near_x = to_chips(packed, seq_count)
    extra = after(jnp.concatenate([dout_own, w_out_rows], axis=0), near_x[1:2])
    stack_x = jnp.concatenate(after(near_x, w_qkv, gu_columns, extra), axis=0)
    far_x = swap(stack_x, seq_count, 1)
    near_extra = to_chips(extra, seq_count)

    gain_attn = norm_attn.reshape(1, width)
    gain_ffn = norm_ffn.reshape(1, width)
    q_gain = jnp.tile(query_gain, WIDE // head_size).reshape(1, WIDE)
    k_gain = jnp.tile(key_gain, WIDE // head_size).reshape(1, WIDE)
    frequency = (10000.0 ** (-2.0 * jnp.arange(half_size).astype(F32) / head_size))[:, None]

    def projected(x):
        return project(
            x, chips, w_qkv, gain_attn, q_gain, k_gain, frequency, variate_bias, head_size
        )

    near_all = projected(stack_x)
    far_all = projected(far_x)
    nin, q_lin, k_lin, lane_rows, q_aug, k_aug, k_trans, v_aug = zip(near_all, far_all)
    attend_near = attend(q_aug[0], k_aug, v_aug, head_size)
    attend_far = attend(after(q_aug[1], attend_near, near_extra[1:2]), k_aug, v_aug, head_size)
    far_extra = [swap(e, seq_count, 1) for e in after(near_extra, attend_far)]
    mixed, o_full, z_inverse = zip(attend_near, attend_far)
    own_parts = [to_chips(mixed[side], seq_count) for side in (0, 1)]
    own_parts[0] = after(own_parts[0], attend_far)
    sib_stack = [swap(jnp.concatenate(own_parts[side], axis=0), seq_count, 1) for side in (0, 1)]

    nm_far, inner_far, ggu_far, dout_far, gnm_far, lay_far = ffn(
        1, own_parts[1], sib_stack[0], far_x, near_extra, far_extra, w_gu, w_down, gain_ffn
    )
    nm_near, inner_near, ggu_near, dout_near, middle, mixed_own, *slots = ffn(
        0, own_parts[0], sib_stack[1], stack_x, near_extra, far_extra, w_gu, w_down, gain_ffn,
        swap(gnm_far, seq_count, 1), group=16 // chips,
    )

    gnm_parts = spread_slots(slots[:chips], seq_count)
    grad_gu, grad_down, gnf = ffn_grads(
        (nm_near, nm_far), (ggu_near, ggu_far), (inner_near, inner_far), (dout_near, dout_far),
        w_gu, seq_count, z_count, swap(slots[0][:8, :WIDE], seq_count, 1),
    )
    me_row = jnp.reshape(me, (1,))
    grad_middle, grad_branch, g_out = middle_back(
        after(gnm_parts, grad_gu, grad_down),
        middle, gain_ffn, near_extra, far_extra, me_row,
    )
    g_all = lax.all_to_all(g_out, "seq", split_axis=0, concat_axis=0, tiled=True)

    grad_gu = lax.psum_scatter(grad_gu, "fsdp", scatter_dimension=0, tiled=True)
    grad_gu = grad_gu.reshape(seq_count, shard, 2 * hidden)
    grad_down = lax.psum_scatter(grad_down, "fsdp", scatter_dimension=0, tiled=True)
    grad_out = dot_tn(mixed_own, grad_branch).astype(BF16)
    half_out = chips * WIDE
    out_slots = add_up([grad_out[:half_out], swap(grad_out[half_out:], seq_count, 1)])
    out_slots = out_slots.astype(BF16)
    lay_got = swap(after(lay_far, grad_branch), seq_count, 1)
    both_slots = []
    for r in range(chips):
        lay = add_up([slots[chips + r], lay_got[r * rows : (r + 1) * rows]]).astype(BF16)
        both_slots.append(jnp.concatenate([lay, out_slots[r * WIDE : (r + 1) * WIDE]], axis=0))
    both_parts = spread_slots(after(both_slots, g_all), seq_count)
    gu_got = lax.all_to_all(
        after(grad_gu, g_all), "seq", split_axis=0, concat_axis=0, tiled=True
    )

    dq_near, dq_far, dk, dv, bias_rows = attend_back(
        me_row, after(g_all, both_slots),
        q_aug, o_full, z_inverse, lane_rows, k_aug, k_trans, v_aug, head_size,
    )
    dq_far = after(dq_far, grad_gu, both_parts)
    gl_near, gl_far, gain_rows = project_back(
        (dq_near, dq_far), q_lin, k_lin, lane_rows, dk, dv, q_gain, k_gain, head_size, chips
    )
    (gni_far,) = spread_back(gl_far, w_qkv, chips)
    gni_got = swap(gni_far, seq_count, 1)
    grad_qkv, gna = pair_product(
        nin, (gl_near, gl_far), w_qkv, swap(gain_rows, seq_count, 1)
    )

    grad_qk_gain = gain_rows[:2, :features].reshape(2, heads, head_size).sum(axis=1)
    bias_cols = jnp.sum(bias_rows, axis=1).reshape(2, 2, 4).sum(axis=2)[:, :heads]
    bias_both = jnp.stack([bias_cols[0], bias_cols[1] - bias_cols[0]])
    bias_all = lax.dynamic_update_slice(
        jnp.zeros((2, heads * seq_count), F32), bias_both, (0, me * heads)
    )
    small = jnp.concatenate(
        [
            gna[0] / norm_attn,
            gnf / norm_ffn,
            grad_qk_gain.reshape(-1),
            bias_all.reshape(-1),
        ]
    )
    count = small.shape[0]
    small_rows = -(-count // (8 * 3 * WIDE)) * 8
    small = jnp.pad(small, (0, small_rows * 3 * WIDE - count)).astype(BF16)
    small = jnp.broadcast_to(small.reshape(1, small_rows, 3 * WIDE), (everyone, small_rows, 3 * WIDE))
    grad_qkv = after(grad_qkv, gu_got)
    blocks = jnp.concatenate([grad_qkv.reshape(everyone, shard, 3 * WIDE), small], axis=1)
    last = lax.all_to_all(blocks, ("seq", "fsdp"), split_axis=0, concat_axis=0, tiled=True)
    gni_slots = spread_back(
        gl_near, w_qkv, chips, after(gni_got, blocks)
    )
    gni_parts = spread_slots(gni_slots, seq_count)
    both = add_up(after(both_parts, gni_slots))
    grad_out = both[rows : rows + features]
    z_me = lax.axis_index("fsdp")
    bit = z_count // 2
    while bit:
        low, high = jnp.split(grad_out, 2, axis=0)
        upper = (z_me & bit) > 0
        away = jnp.where(upper, low, high).astype(BF16)
        away = lax.ppermute(away, "fsdp", [(i, i ^ bit) for i in range(z_count)])
        grad_out = jnp.where(upper, high, low) + away.astype(F32)
        bit //= 2
    in_grad = input_back(gni_parts, x_own, grad_middle, gain_attn)

    gu_got = after(gu_got, gni_slots)
    grad_down = after(grad_down, gni_parts[3:])
    layer_out = (middle + both[:rows]).astype(BF16)
    grad_gu = gu_got.transpose(1, 0, 2).astype(F32)
    grad_gate = grad_gu[:, :, :hidden].reshape(shard, seq_count * hidden)
    grad_up = grad_gu[:, :, hidden:].reshape(shard, seq_count * hidden)
    grad_down = grad_down.astype(F32)
    *grad_qkv, small = last_sums(after(last, in_grad, grad_out, grad_down), z_count, shard)
    grad_query, grad_key, grad_value = (
        g.reshape(shard, seq_count, WIDE)[:, :, :features].reshape(shard, width)
        if features < WIDE
        else g
        for g in grad_qkv
    )
    small = small.reshape(-1)
    cut = 2 * width + 2 * head_size
    grad_bias = lax.dynamic_slice(
        small[cut:count].reshape(2, heads * seq_count), (0, me * heads), (2, heads)
    )
    return (
        layer_out.reshape(tokens.shape),
        in_grad.reshape(tokens.shape),
        grad_query,
        grad_key,
        grad_value,
        grad_out,
        grad_gate,
        grad_up,
        grad_down,
        small[:width],
        small[width : 2 * width],
        small[2 * width : 2 * width + head_size],
        small[2 * width + head_size : cut],
        grad_bias,
    )


def solution(mesh):
    rows = P("fsdp", "seq", None)
    shards = P(("seq", "fsdp"), None)
    ids = P("fsdp", "seq")
    bias = P(None, "seq")
    return jax.shard_map(
        body,
        mesh=mesh,
        in_specs=(rows,) + (shards,) * 7 + (P(),) * 4 + (bias, ids, ids, ids, rows),
        out_specs=(rows, rows) + (shards,) * 7 + (P(),) * 4 + (bias,),
        check_vma=False,
    )
```

```python
import functools
import math

import jax
import jax.numpy as jnp
from jax import lax
from jax.experimental import pallas as pl
from jax.experimental.pallas import tpu as pltpu
from jax.sharding import PartitionSpec as P

EPSILON = 1e-06
FAR = -1e30
LOG2E = math.log2(math.e)
WIDE = 128
ROWS_T = 160
F32 = jnp.float32
BF16 = jnp.bfloat16


def dot_nn(left, right):
    return jnp.dot(left, right, preferred_element_type=F32)


def dot_nt(left, right):
    return lax.dot_general(left, right, (((1,), (1,)), ((), ())), preferred_element_type=F32)


def dot_tn(left, right):
    return lax.dot_general(left, right, (((0,), (0,)), ((), ())), preferred_element_type=F32)


def rms_factor(values):
    return lax.rsqrt(jnp.mean(values * values, axis=-1, keepdims=True) + EPSILON)


def lanes_of(shape):
    return lax.broadcasted_iota(jnp.int32, shape, len(shape) - 1)


def head_sum(values, blocks):
    high = values.astype(BF16)
    low = (values - high.astype(F32)).astype(BF16)
    return dot_nn(high, blocks) + dot_nn(low, blocks)


def head_blocks(head_size):
    row = lax.broadcasted_iota(jnp.int32, (WIDE, WIDE), 0) // head_size
    column = lax.broadcasted_iota(jnp.int32, (WIDE, WIDE), 1) // head_size
    return jnp.where(row == column, 1.0, 0.0).astype(BF16)


def partner(values, lane, head_size):
    half = head_size // 2
    up = pltpu.roll(values, WIDE - half, 1)
    down = pltpu.roll(values, half, 1)
    return jnp.where(lane % head_size < half, up, down)


def tables(cosine, sine):
    times = WIDE // (2 * cosine.shape[0])
    cos_rows = jnp.concatenate([cosine, cosine] * times, axis=0)
    sin_rows = jnp.concatenate([-sine, sine] * times, axis=0)
    return cos_rows.T, sin_rows.T


def params(grid=True):
    return pltpu.CompilerParams(
        vmem_limit_bytes=60 * 1024 * 1024,
        dimension_semantics=("arbitrary",) if grid else None,
    )


def whole(array):
    return pl.BlockSpec(array.shape, lambda *_: (0,) * len(array.shape))


def shaped(shape, dtype):
    return jax.ShapeDtypeStruct(shape, dtype)


ANY = pl.BlockSpec(memory_space=pl.ANY)


def assemble(out_ref, in_ref):
    if len(in_ref.shape) == 2:
        out_ref[...] = in_ref[...]
        return
    z_count, seq_count, shard, _ = in_ref.shape
    for f in range(z_count):
        for s in range(seq_count):
            at = (s * z_count + f) * shard
            out_ref[at : at + shard, :] = in_ref[f, s]


def gathered(w):
    if w.shape[2] % 16 == 0:
        return w
    return w.transpose(1, 0, 2, 3).reshape(-1, w.shape[-1])


def columns_kernel(*refs):
    *weights, out_ref = refs
    at = 0
    for w_ref in weights:
        wide = w_ref.shape[1] // out_ref.shape[0]
        for s in range(out_ref.shape[0]):
            out_ref[s, :, at : at + wide] = w_ref[:, s * wide : (s + 1) * wide]
        at += wide


def columns_by_device(weights, seq_count):
    shard = weights[0].shape[0]
    wides = [w.shape[1] // seq_count for w in weights]
    if shard % 16 == 0 and all(wide % WIDE == 0 for wide in wides):
        return pl.pallas_call(
            columns_kernel,
            out_shape=shaped((seq_count, shard, sum(wides)), BF16),
            compiler_params=params(False),
            name="columns",
        )(*weights)
    pieces = []
    for w, wide in zip(weights, wides):
        short = -wide % WIDE
        pieces.append(jnp.pad(w.reshape(shard, seq_count, wide), ((0, 0), (0, 0), (0, short))))
    return jnp.concatenate(pieces, axis=2).transpose(1, 0, 2)


def project_kernel(
    x_ref, w_ref, na_ref, qg_ref, kg_ref, freq_ref, bias_ref,
    nin_ref, qlin_ref, klin_ref, lane_ref, qa_ref, ka_ref, kt_ref, v1_ref, w_s, *, heads, head_size,
):
    half = head_size // 2
    rows = nin_ref.shape[0]

    @pl.when(pl.program_id(0) == 0)
    def _():
        assemble(w_s, w_ref)

    x = x_ref[:rows, :].astype(F32)
    ids = x_ref[rows:, :rows].astype(F32)
    nin = (x * rms_factor(x) * na_ref[...]).astype(BF16)
    nin_ref[...] = nin
    lin = dot_nn(nin, w_s[...])
    q, k, v = lin[:, :WIDE], lin[:, WIDE : 2 * WIDE], lin[:, 2 * WIDE :]
    qlin_ref[...] = q
    klin_ref[...] = k
    angles = freq_ref[...] * (ids[2:3] * 64.0 + ids[3:4])
    cosine, sine = jnp.cos(angles), jnp.sin(angles)
    lane_ref[...] = jnp.concatenate([cosine, sine, ids[:8]], axis=0)
    cosine, sine = tables(cosine, sine)
    lane = lanes_of((rows, WIDE))
    blocks = head_blocks(head_size)

    def finish(u, gain):
        factor = lax.rsqrt(head_sum(u * u, blocks) * (1.0 / head_size) + EPSILON)
        u = u * factor * gain
        return u * cosine + partner(u, lane, head_size) * sine

    q = finish(q, qg_ref[...]) * (LOG2E * head_size**-0.5)
    k = finish(k, kg_ref[...])
    few = ROWS_T - WIDE
    row = lax.broadcasted_iota(jnp.int32, (few, rows), 0)
    variate = ids[0:1].astype(jnp.int32)
    sample = ids[1:2].astype(jnp.int32)
    same_variate = (row % 4) == variate
    same_sample = (row - 10) == sample
    one = jnp.ones((few, rows), F32)
    nil = jnp.zeros((few, rows), F32)
    rest = jnp.zeros((WIDE - few, rows), F32)

    def columns(few_rows):
        return jnp.concatenate([few_rows, rest], axis=0).T

    aug_q = jnp.where(
        row < 8,
        jnp.where(same_variate, one, nil),
        jnp.where(row < 10, one, jnp.where((row < 13) & same_sample, one, nil)),
    )
    qa_ref[...] = jnp.concatenate([q, columns(aug_q)], axis=1).astype(BF16)
    k_t = k.T
    row_k = lax.broadcasted_iota(jnp.int32, (WIDE, rows), 0)
    for h in range(heads):
        first, second = bias_ref[0, h] * LOG2E, bias_ref[1, h] * LOG2E
        step_up = jnp.where(row < 8, first - second, second) * one
        high = step_up.astype(BF16).astype(F32)
        low = step_up - high
        far = jnp.where(same_sample, nil, FAR)
        plain = jnp.where(((row // 4) == 4 + h) & same_variate, one, nil)
        aug_k = jnp.where(
            row < 4,
            jnp.where(same_variate, high, nil),
            jnp.where(
                row < 8,
                jnp.where(same_variate, low, nil),
                jnp.where(
                    row == 8,
                    high,
                    jnp.where(row == 9, low, jnp.where(row < 13, far, plain)),
                ),
            ),
        )
        mine = (lane // head_size) == h
        mine_t = (row_k // head_size) == h
        ka_ref[h] = jnp.concatenate([jnp.where(mine, k, 0.0), columns(aug_k)], axis=1).astype(BF16)
        kt_ref[h] = jnp.concatenate([jnp.where(mine_t, k_t, 0.0), aug_k], axis=0).astype(BF16)
        ones_v = jnp.where((lane == h) | (lane == 2 + h), 1.0, 0.0)
        v1_ref[h] = jnp.concatenate([jnp.where(mine, v, 0.0), ones_v], axis=1).astype(BF16)


def project(x, chips, w, norm_attn, q_gain, k_gain, freq, bias, head_size):
    width, wide = x.shape[1], w.shape[-1]
    rows = x.shape[0] // chips - 16
    heads = bias.shape[1]
    half = chips * rows
    count = head_size + 8
    row_block = lambda cols: pl.BlockSpec((rows, cols), lambda i: (i, 0))
    lane_block = pl.BlockSpec((count, rows), lambda i: (0, i))
    head_block = pl.BlockSpec((heads, rows, 2 * WIDE), lambda i: (0, i, 0))
    return pl.pallas_call(
        functools.partial(project_kernel, heads=heads, head_size=head_size),
        grid=(chips,),
        in_specs=[pl.BlockSpec((rows + 16, width), lambda i: (i, 0))]
        + [whole(a) for a in (w, norm_attn, q_gain, k_gain, freq)]
        + [pl.BlockSpec(memory_space=pltpu.SMEM)],
        out_specs=[
            row_block(width), row_block(WIDE), row_block(WIDE), lane_block, row_block(2 * WIDE),
            head_block, pl.BlockSpec((heads, ROWS_T, rows), lambda i: (0, 0, i)), head_block,
        ],
        out_shape=[
            shaped((half, width), BF16),
            shaped((half, WIDE), F32),
            shaped((half, WIDE), F32),
            shaped((count, half), F32),
            shaped((half, 2 * WIDE), BF16),
            shaped((heads, half, 2 * WIDE), BF16),
            shaped((heads, ROWS_T, half), BF16),
            shaped((heads, half, 2 * WIDE), BF16),
        ],
        scratch_shapes=[pltpu.VMEM((width, wide), BF16)],
        compiler_params=params(),
        cost_estimate=pl.CostEstimate(
            flops=2 * half * width * 3 * WIDE, bytes_accessed=half * width * 8, transcendentals=0
        ),
        name="project",
    )(x, w, norm_attn, q_gain, k_gain, freq, bias)


def attend_kernel(qa_ref, ka0, ka1, v10, v11, mixed_ref, o_ref, zi_ref, *, heads, head_size, chunk):
    qa = qa_ref[...]
    rows = qa.shape[0]
    half = ka0.shape[1]
    lane = lanes_of((rows, WIDE))
    total = jnp.zeros((rows, WIDE), F32)
    inverse = jnp.ones((rows, WIDE), F32)
    for h in range(heads):
        acc = jnp.zeros((rows, 2 * WIDE), F32)
        for ka_ref, v1_ref in ((ka0, v10), (ka1, v11)):
            for c in range(half // chunk):
                part = pl.ds(c * chunk, chunk)
                e = jnp.exp2(dot_nt(qa, ka_ref[h, part, :])).astype(BF16)
                acc = acc + dot_nn(e, v1_ref[h, part, :])
        z_inv = 1.0 / acc[:, WIDE + h : WIDE + h + 1]
        total = total + acc[:, :WIDE] * z_inv
        inverse = jnp.where((lane // head_size) == h, z_inv, inverse)
    mixed_ref[...] = total.astype(BF16)
    o_ref[...] = total
    zi_ref[...] = inverse


def attend(qa, ka, v1, head_size, block=512, chunk=256):
    heads, half, _ = ka[0].shape
    out_block = pl.BlockSpec((block, WIDE), lambda i: (i, 0))
    return pl.pallas_call(
        functools.partial(attend_kernel, heads=heads, head_size=head_size, chunk=chunk),
        grid=(half // block,),
        in_specs=[pl.BlockSpec((block, 2 * WIDE), lambda i: (i, 0))]
        + [whole(a) for a in (*ka, *v1)],
        out_specs=[out_block, out_block, out_block],
        out_shape=[shaped((half, WIDE), BF16), shaped((half, WIDE), F32), shaped((half, WIDE), F32)],
        compiler_params=params(),
        cost_estimate=pl.CostEstimate(
            flops=2 * heads * half * half * 8 * WIDE,
            bytes_accessed=half * WIDE * 32,
            transcendentals=2 * heads * half * half,
        ),
        name="attend",
    )(qa, *ka, *v1)


def attend_back_kernel(*refs, chips, heads, head_size, chunk):
    me_ref, g_ref = refs[:2]
    at = 2
    qa, o, zi, lanes, ka, kt, v1 = [refs[at + 2 * n : at + 2 * n + 2] for n in range(7)]
    at += 14
    dq_refs = refs[at : at + 2]
    dk_ref, dv_ref, bias_ref, g_s, dk_s, dv_s = refs[at + 2 :]
    step = pl.program_id(0)

    @pl.when(step == 0)
    def _():
        dk_s[...] = jnp.zeros_like(dk_s)
        dv_s[...] = jnp.zeros_like(dv_s)
        bias_ref[...] = jnp.zeros_like(bias_ref)
        for j in range(2 * chips):
            g_s[j % 2, j // 2] = g_ref[me_ref[0] ^ j]

    for side in range(2):
        q_rows = qa[side][...]
        rows = q_rows.shape[0]
        half_len = ka[0].shape[1]
        lane = lanes_of((rows, WIDE))
        q = q_rows[:, :WIDE]
        gz = (g_s[side, step].astype(F32) * zi[side][...]).astype(BF16)
        inner = gz.astype(F32) * o[side][...]
        aug = jnp.zeros((rows, WIDE), F32)
        for h in range(heads):
            mean = -jnp.sum(
                jnp.where((lane // head_size) == h, inner, 0.0), axis=-1, keepdims=True
            ) * jnp.ones((rows, WIDE), F32)
            high = mean.astype(BF16).astype(F32)
            aug = jnp.where(lane == h, high, jnp.where(lane == 2 + h, mean - high, aug))
        ga = jnp.concatenate([gz, aug.astype(BF16)], axis=1)
        dq_t = jnp.zeros((ROWS_T, rows), F32)
        for h in range(heads):
            mine = (lane // head_size) == h
            q_h = jnp.where(mine, q, jnp.zeros_like(q))
            g_h = jnp.where(mine, gz, jnp.zeros_like(gz))
            for other in range(2):
                for c in range(half_len // chunk):
                    part = pl.ds(c * chunk, chunk)
                    e = jnp.exp2(dot_nt(ka[other][h, part, :], q_rows))
                    ds = (e * dot_nt(v1[other][h, part, :], ga)).astype(BF16)
                    dv_s[other, part, :] += dot_nn(e.astype(BF16), g_h)
                    dk_s[other, part, :] += dot_nn(ds, q_h)
                    dq_t = dq_t + dot_nn(kt[other][h, :, part], ds)
        dq_refs[side][...] = (dq_t[:WIDE].T * (head_size**-0.5)).astype(BF16)
        variate = lanes[side][head_size : head_size + 1, :].astype(jnp.int32)
        columns = dq_t[WIDE + 16 : WIDE + 24]
        row = lax.broadcasted_iota(jnp.int32, columns.shape, 0)
        bias_ref[...] += jnp.concatenate(
            [jnp.where((row % 4) == variate, columns, 0.0), columns], axis=0
        )

    @pl.when(step == pl.num_programs(0) - 1)
    def _():
        dk_ref[...] = (dk_s[...] * (1.0 / LOG2E)).astype(BF16)
        dv_ref[...] = dv_s[...].astype(BF16)


def attend_back(me, g, qa, o, zi, lane_rows, ka, kt, v1, head_size, chunk=1024):
    heads, half, _ = ka[0].shape
    chips = g.shape[0] // 2
    chunk = math.gcd(half, chunk)
    block = half // chips
    count = lane_rows[0].shape[0]
    row_block = lambda cols: pl.BlockSpec((block, cols), lambda i: (i, 0))
    lane_block = pl.BlockSpec((count, block), lambda i: (0, i))
    full = shaped((2, half, WIDE), BF16)
    return pl.pallas_call(
        functools.partial(
            attend_back_kernel, chips=chips, heads=heads, head_size=head_size, chunk=chunk
        ),
        grid=(chips,),
        in_specs=[pl.BlockSpec(memory_space=pltpu.SMEM), whole(g)]
        + [row_block(2 * WIDE)] * 2
        + [row_block(WIDE)] * 4
        + [lane_block] * 2
        + [whole(a) for a in (*ka, *kt, *v1)],
        out_specs=[row_block(WIDE)] * 2
        + [whole(full), whole(full), pl.BlockSpec((16, block), lambda i: (0, 0))],
        out_shape=[shaped((half, WIDE), BF16)] * 2 + [full, full, shaped((16, block), F32)],
        scratch_shapes=[
            pltpu.VMEM((2, chips, block, WIDE), BF16),
            pltpu.VMEM((2, half, WIDE), F32),
            pltpu.VMEM((2, half, WIDE), F32),
        ],
        compiler_params=params(),
        cost_estimate=pl.CostEstimate(
            flops=2 * heads * half * half * 32 * WIDE,
            bytes_accessed=half * WIDE * 64,
            transcendentals=4 * heads * half * half,
        ),
        name="attend_back",
    )(me, g, *qa, *o, *zi, *lane_rows, *ka, *kt, *v1)


def ffn_kernel(*refs, chips, group, near):
    mixed = refs[: 2 * chips]
    extra_parts = refs[2 * chips : 4 * chips]
    at = 4 * chips
    x_ref, wgu_ref, wd_ref, nf_ref = refs[at : at + 4]
    at += 4
    if near:
        got_ref = refs[at]
        at += 1
    nm_ref, inner_ref, ggu_ref, dout_ref = refs[at : at + 4]
    at += 4
    if near:
        mid_ref, mixed_ref = refs[at : at + 2]
        gnm_refs = refs[at + 2 : at + 2 + chips]
        lay_refs = refs[at + 2 + chips : at + 2 + 2 * chips]
        at += 2 + 2 * chips
    else:
        gnm_ref, lay_ref = refs[at : at + 2]
        at += 2
    w_s, wo_s, extra_s, sems = refs[at:]
    step = pl.program_id(0)
    rows = nm_ref.shape[0] // group

    @pl.when(step == 0)
    def _():
        copies = [
            pltpu.make_async_copy(part, extra_s.at[j], sems.at[j])
            for j, part in enumerate(extra_parts)
        ]
        for copy in copies:
            copy.start()
        assemble(w_s, wgu_ref)
        for j, copy in enumerate(copies):
            copy.wait()
            wo_s[j * WIDE : (j + 1) * WIDE, :] = extra_s[j, rows:, :]

    def own_order(block, r):
        if r % group == 0:
            return block
        slots = [(t ^ (r % group)) * rows for t in range(group)]
        return jnp.concatenate([block[at : at + rows] for at in slots], axis=0)

    cat = jnp.concatenate([own_order(m[...], j % chips) for j, m in enumerate(mixed)], axis=1)
    hidden = wd_ref.shape[0]
    x = [x_ref[t * (rows + 16) : t * (rows + 16) + rows, :] for t in range(group)]
    first = (0 if near else chips) + step * group
    dout = jnp.concatenate([extra_s[first + t, :rows, :] for t in range(group)], axis=0)
    dout_ref[...] = dout
    middle = jnp.concatenate(x, axis=0).astype(F32) + dot_nn(cat, wo_s[...])
    nm = (middle * rms_factor(middle) * nf_ref[...]).astype(BF16)
    nm_ref[...] = nm
    lin = dot_nn(nm, w_s[...])
    back = dot_nt(dout, wd_ref[...])
    gate, up = lin[:, :hidden], lin[:, hidden:]
    sig = jax.nn.sigmoid(gate)
    silu = gate * sig
    inner = (silu * up).astype(BF16)
    inner_ref[...] = inner
    g_gate = (back * up * (sig * (1.0 + gate * (1.0 - sig)))).astype(BF16)
    g_up = (back * silu).astype(BF16)
    ggu = jnp.concatenate([g_gate, g_up], axis=1)
    ggu_ref[...] = ggu
    gnm = dot_nt(ggu, w_s[...])
    lay = dot_nn(inner, wd_ref[...])
    if near:

        @pl.when(step == 0)
        def _():
            mid_ref[...] = middle[:rows]
            mixed_ref[...] = cat[:rows]

        gnm = (gnm + got_ref[...].astype(F32)).astype(BF16)
        lay = lay.astype(BF16)
        for r in range(chips):

            @pl.when(step == r // group)
            def _(r=r):
                at = (r % group) * rows
                gnm_refs[r][...] = gnm[at : at + rows]
                lay_refs[r][...] = lay[at : at + rows]

    else:
        gnm_ref[...] = gnm.astype(BF16)
        lay_ref[...] = lay.astype(BF16)


def ffn(
    side, own_parts, sib_stack, x, near_extra, far_extra, wgu, wd, norm_ffn, got=None, group=2
):
    chips = len(own_parts)
    group = math.gcd(chips, group)
    rows, width = near_extra[0].shape
    rows -= WIDE
    half = rows * chips
    block = rows * group
    steps = chips // group
    hidden = wd.shape[0]
    near = side == 0
    row_block = lambda cols: pl.BlockSpec((block, cols), lambda i: (i, 0))
    piece = lambda r: pl.BlockSpec((block, WIDE), lambda i: (i ^ (r // group), 0))
    stack = lambda r: pl.BlockSpec((block, WIDE), lambda i: (r * steps + (i ^ (r // group)), 0))
    out_shape = [
        shaped((half, width), BF16), shaped((half, hidden), BF16), shaped((half, 2 * hidden), BF16),
        shaped((half, width), BF16),
    ]
    out_specs = [row_block(width), row_block(hidden), row_block(2 * hidden), row_block(width)]
    if near:
        more = [shaped((rows, width), F32), shaped((rows, 2 * chips * WIDE), BF16)]
        more += [shaped((rows, width), BF16)] * (2 * chips)
        out_shape += more
        out_specs += [whole(a) for a in more]
    else:
        out_shape += [shaped((half, width), BF16)] * 2
        out_specs += [row_block(width)] * 2
    return pl.pallas_call(
        functools.partial(ffn_kernel, chips=chips, group=group, near=near),
        grid=(steps,),
        in_specs=[piece(r) for r in range(chips)]
        + [stack(r) for r in range(chips)]
        + [ANY] * (2 * chips)
        + [pl.BlockSpec((group * (rows + 16), width), lambda i: (i, 0))]
        + [whole(a) for a in (wgu, wd, norm_ffn)]
        + ([row_block(width)] if near else []),
        out_specs=out_specs,
        out_shape=out_shape,
        scratch_shapes=[
            pltpu.VMEM((width, 2 * hidden), BF16),
            pltpu.VMEM((2 * chips * WIDE, width), BF16),
            pltpu.VMEM((2 * chips, rows + WIDE, width), BF16),
            pltpu.SemaphoreType.DMA((2 * chips,)),
        ],
        compiler_params=params(),
        cost_estimate=pl.CostEstimate(
            flops=2 * half * width * (2 * chips * WIDE + 6 * hidden),
            bytes_accessed=half * width * 12,
            transcendentals=half * hidden,
        ),
        name="ffn_half",
    )(
        *own_parts, *[sib_stack] * chips, *near_extra, *far_extra, x, wgu, wd, norm_ffn,
        *([got] if near else []),
    )


def row_sums(product, w_ref):
    w = w_ref[...].astype(F32)
    if len(w.shape) == 4:
        z_count, parts, _, _ = w.shape
        w = jnp.concatenate([w[f, s] for s in range(parts) for f in range(z_count)], axis=0)
    total = jnp.sum(product * w, axis=1, keepdims=True)
    return (total * jnp.ones((product.shape[0], WIDE), F32)).T[:8]


def block_of(w, steps):
    if len(w.shape) == 2:
        return pl.BlockSpec((w.shape[0] // steps, w.shape[1]), lambda i: (i, 0))
    block = (w.shape[0], w.shape[1] // steps) + w.shape[2:]
    return pl.BlockSpec(block, lambda i: (0, i, 0, 0))


def ffn_grads_kernel(nm0, nm1, ggu0, ggu1, in0, in1, dout0, dout1, w_ref, _, gu_ref, gd_ref, sum_ref):
    gu = dot_tn(nm0[...], ggu0[...]) + dot_tn(nm1[...], ggu1[...])
    sum_ref[...] = row_sums(gu, w_ref)
    gu = gu.astype(BF16)
    if len(gu_ref.shape) == 2:
        gu_ref[...] = gu
    else:
        z_count, parts, shard, _ = gu_ref.shape
        for f in range(z_count):
            for s in range(parts):
                at = (s * z_count + f) * shard
                gu_ref[f, s] = gu[at : at + shard]
    gd_ref[...] = (dot_tn(in0[...], dout0[...]) + dot_tn(in1[...], dout1[...])).astype(BF16)


def ffn_grads(nm, ggu, inner, dout, w, seq_count, z_count, ticket):
    half, width = nm[0].shape
    hidden = inner[0].shape[1]
    shard = width // (seq_count * z_count)
    steps = max(1, min(4, hidden // WIDE))
    column_block = lambda cols: pl.BlockSpec((half, cols // steps), lambda i: (0, i))
    if shard % 16 == 0 and seq_count % steps == 0:
        gu = shaped((z_count, seq_count, shard, 2 * hidden), BF16)
        gu_spec = pl.BlockSpec(
            (z_count, seq_count // steps, shard, 2 * hidden), lambda i: (0, i, 0, 0)
        )
    else:
        gu = shaped((width, 2 * hidden), BF16)
        gu_spec = pl.BlockSpec((width // steps, 2 * hidden), lambda i: (i, 0))
    gu, gd, sums = pl.pallas_call(
        ffn_grads_kernel,
        grid=(steps,),
        in_specs=[column_block(width)] * 2
        + [whole(a) for a in ggu]
        + [column_block(hidden)] * 2
        + [whole(a) for a in dout]
        + [block_of(w, steps), ANY],
        out_specs=[
            gu_spec,
            pl.BlockSpec((hidden // steps, width), lambda i: (i, 0)),
            pl.BlockSpec((8, width // steps), lambda i: (0, i)),
        ],
        out_shape=[gu, shaped((hidden, width), BF16), shaped((8, width), F32)],
        compiler_params=params(),
        cost_estimate=pl.CostEstimate(
            flops=2 * half * width * 6 * hidden, bytes_accessed=half * width * 16, transcendentals=0
        ),
        name="ffn_grads",
    )(*nm, *ggu, *inner, *dout, w, ticket)
    if len(gu.shape) == 2:
        gu = gu.reshape(seq_count, z_count, shard, 2 * hidden).transpose(1, 0, 2, 3)
    return gu.reshape(width, 2 * hidden), gd, sums[0]


def pair_kernel(a0, a1, b0, b1, w_ref, _, out_ref, sum_ref):
    product = dot_tn(a0[...], b0[...]) + dot_tn(a1[...], b1[...])
    out_ref[...] = product.astype(BF16)
    sum_ref[...] = row_sums(product, w_ref)


def pair_product(left, right, w, ticket, steps=4):
    half, width = left[0].shape
    wide = right[0].shape[1]
    return pl.pallas_call(
        pair_kernel,
        grid=(steps,),
        in_specs=[pl.BlockSpec((half, width // steps), lambda i: (0, i))] * 2
        + [whole(a) for a in right]
        + [block_of(w, steps), ANY],
        out_specs=[
            pl.BlockSpec((width // steps, wide), lambda i: (i, 0)),
            pl.BlockSpec((8, width // steps), lambda i: (0, i)),
        ],
        out_shape=[shaped((width, wide), BF16), shaped((8, width), F32)],
        compiler_params=params(),
        cost_estimate=pl.CostEstimate(
            flops=4 * half * width * wide, bytes_accessed=half * width * 6, transcendentals=0
        ),
        name="pair_product",
    )(*left, *right, w, ticket)


def added(pieces):
    total = pieces[0][...].astype(F32)
    for piece in pieces[1:]:
        total = total + piece[...].astype(F32)
    return total


def norm_back(values, gain, incoming):
    factor = rms_factor(values)
    weighted = incoming * gain
    return factor * weighted - values * (factor * factor * factor) * jnp.mean(
        weighted * values, axis=-1, keepdims=True
    )


def middle_back_kernel(*refs, chips):
    extra = refs[chips : 3 * chips]
    mid_ref, nf_ref, me_ref, gm_ref, gb_ref, out_ref = refs[3 * chips :]
    rows = mid_ref.shape[0]
    grad = extra[0][:rows, :].astype(F32) + norm_back(mid_ref[...], nf_ref[...], added(refs[:chips]))
    gm_ref[...] = grad
    branch = grad.astype(BF16)
    gb_ref[...] = branch
    for side in range(2):
        for r in range(chips):
            part = dot_nt(branch, extra[side * chips + r][rows:, :])
            out_ref[me_ref[0] ^ (2 * r + side)] = part.astype(BF16)


def middle_back(pieces, middle, norm_ffn, near_extra, far_extra, me):
    chips = len(pieces)
    rows, width = middle.shape
    vmem = pl.BlockSpec(memory_space=pltpu.VMEM)
    return pl.pallas_call(
        functools.partial(middle_back_kernel, chips=chips),
        in_specs=[vmem] * (3 * chips + 2) + [pl.BlockSpec(memory_space=pltpu.SMEM)],
        out_shape=[
            shaped((rows, width), F32), shaped((rows, width), BF16),
            shaped((2 * chips, rows, WIDE), BF16),
        ],
        compiler_params=params(False),
        cost_estimate=pl.CostEstimate(
            flops=2 * rows * width * 2 * chips * WIDE,
            bytes_accessed=rows * width * 12,
            transcendentals=0,
        ),
        name="middle_back",
    )(*pieces, *near_extra, *far_extra, middle, norm_ffn, me)


def input_back_kernel(*refs, chips):
    x_ref, gm_ref, na_ref, out_ref = refs[chips:]
    out_ref[...] = gm_ref[...] + norm_back(x_ref[...].astype(F32), na_ref[...], added(refs[:chips]))


def input_back(pieces, x, grad_middle, norm_attn):
    return pl.pallas_call(
        functools.partial(input_back_kernel, chips=len(pieces)),
        out_shape=shaped(x.shape, F32),
        compiler_params=params(False),
        name="input_back",
    )(*pieces, x, grad_middle, norm_attn)


def project_back_kernel(*refs, head_size):
    dq, qlin, klin, lanes = refs[0:2], refs[2:4], refs[4:6], refs[6:8]
    dk_ref, dv_ref, qg_ref, kg_ref = refs[8:12]
    gl, gain_ref = refs[12:14], refs[14]
    half = head_size // 2
    rows = qlin[0].shape[0]
    lane = lanes_of((rows, WIDE))
    blocks = head_blocks(head_size)

    @pl.when(pl.program_id(0) == 0)
    def _():
        gain_ref[...] = jnp.zeros_like(gain_ref)

    for side in range(2):
        cosine, sine = tables(lanes[side][:half, :], lanes[side][half : 2 * half, :])

        def back(grad, u, gain, at):
            grad = grad.astype(F32)
            grad = grad * cosine - partner(grad, lane, head_size) * sine
            factor = lax.rsqrt(head_sum(u * u, blocks) * (1.0 / head_size) + EPSILON)
            gain_ref[at : at + 1, :] += jnp.sum(grad * u * factor, axis=0, keepdims=True)
            weighted = grad * gain
            mean = head_sum(weighted * u, blocks) * (1.0 / head_size)
            return (factor * weighted - u * (factor * factor * factor) * mean).astype(BF16)

        gq = back(dq[side][...], qlin[side][...], qg_ref[...], 0)
        gk = back(dk_ref[side], klin[side][...], kg_ref[...], 1)
        gl[side][...] = jnp.concatenate([gq, gk, dv_ref[side]], axis=1)


def project_back(dq, qlin, klin, lane_rows, dk, dv, q_gain, k_gain, head_size, chips):
    half = qlin[0].shape[0]
    rows = half // chips
    count = lane_rows[0].shape[0]
    row_block = lambda cols: pl.BlockSpec((rows, cols), lambda i: (i, 0))
    both = pl.BlockSpec((2, rows, WIDE), lambda i: (0, i, 0))
    gain = shaped((8, WIDE), F32)
    return pl.pallas_call(
        functools.partial(project_back_kernel, head_size=head_size),
        grid=(chips,),
        in_specs=[row_block(WIDE)] * 6
        + [pl.BlockSpec((count, rows), lambda i: (0, i))] * 2
        + [both, both, whole(q_gain), whole(k_gain)],
        out_specs=[row_block(3 * WIDE), row_block(3 * WIDE), whole(gain)],
        out_shape=[shaped((half, 3 * WIDE), BF16)] * 2 + [gain],
        compiler_params=params(),
        cost_estimate=pl.CostEstimate(
            flops=2 * half * WIDE * 16 * WIDE, bytes_accessed=half * WIDE * 40, transcendentals=0
        ),
        name="project_back",
    )(*dq, *qlin, *klin, *lane_rows, dk, dv, q_gain, k_gain)


def spread_back_kernel(*refs, chips, near):
    gl_ref, w_ref = refs[:2]
    got = refs[2:3] if near else ()
    outs, w_s = refs[2 + len(got) : -1], refs[-1]
    step = pl.program_id(0)

    @pl.when(step == 0)
    def _():
        assemble(w_s, w_ref)

    out = dot_nt(gl_ref[...], w_s[...])
    if near:
        out = (out + got[0][...].astype(F32)).astype(BF16)
        for r in range(chips):

            @pl.when(step == r)
            def _(r=r):
                outs[r][...] = out

    else:
        outs[0][...] = out.astype(BF16)


def spread_back(gl, w, chips, got=None):
    half, wide = gl.shape
    width = math.prod(w.shape[:-1])
    rows = half // chips
    near = got is not None
    row_block = lambda cols: pl.BlockSpec((rows, cols), lambda i: (i, 0))
    out_shape = [shaped((rows, width), BF16)] * chips if near else [shaped((half, width), BF16)]
    return pl.pallas_call(
        functools.partial(spread_back_kernel, chips=chips, near=near),
        grid=(chips,),
        in_specs=[row_block(wide), whole(w)] + ([row_block(width)] if near else []),
        out_specs=[whole(a) for a in out_shape] if near else [row_block(width)],
        out_shape=out_shape,
        scratch_shapes=[pltpu.VMEM((width, wide), BF16)],
        compiler_params=params(),
        cost_estimate=pl.CostEstimate(
            flops=2 * half * width * wide, bytes_accessed=half * width * 4, transcendentals=0
        ),
        name="spread_back",
    )(gl, w, *([got] if near else []))


def last_kernel(in_ref, *refs, z_count, shard):
    outs, small_ref = refs[:-1], refs[-1]
    seq_count = in_ref.shape[0] // z_count
    small = None
    for s in range(seq_count):
        total = None
        for f in range(z_count):
            block = in_ref[s * z_count + f].astype(F32)
            total = block if total is None else total + block
        for i, out_ref in enumerate(outs):
            out_ref[:, s * WIDE : (s + 1) * WIDE] = total[:shard, i * WIDE : (i + 1) * WIDE]
        small = total[shard:] if small is None else small + total[shard:]
    small_ref[...] = small


def last_sums(blocks, z_count, shard):
    count, rows, wide = blocks.shape
    seq_count = count // z_count
    return pl.pallas_call(
        functools.partial(last_kernel, z_count=z_count, shard=shard),
        out_shape=[shaped((shard, seq_count * WIDE), F32)] * 3 + [shaped((rows - shard, wide), F32)],
        compiler_params=params(False),
        name="last_sums",
    )(blocks)


def swap(x, seq_count, bits):
    return lax.ppermute(x, "seq", [(i, i ^ bits) for i in range(seq_count)])


def to_chips(x, seq_count):
    return [x] + [swap(x, seq_count, 2 * r) for r in range(1, seq_count // 2)]


def spread_slots(slots, seq_count):
    return [slots[0]] + [swap(slots[r], seq_count, 2 * r) for r in range(1, len(slots))]


def after(values, *others):
    kept, _ = lax.optimization_barrier((values, others))
    return kept


def add_up(parts):
    total = parts[0].astype(F32)
    for part in parts[1:]:
        total = total + part.astype(F32)
    return total


def body(
    tokens, weight_query, weight_key, weight_value, weight_out, weight_gate, weight_up, weight_down,
    norm_attn, norm_ffn, query_gain, key_gain, variate_bias, variate_ids, sample_ids, time_ids,
    out_grad,
):
    seq_count = lax.axis_size("seq")
    z_count = lax.axis_size("fsdp")
    everyone = seq_count * z_count
    chips = seq_count // 2
    _, rows, width = tokens.shape
    heads = variate_bias.shape[1]
    head_size = query_gain.shape[0]
    half_size = head_size // 2
    shard = weight_query.shape[0]
    features = heads * head_size
    hidden = weight_gate.shape[1] // seq_count
    me = lax.axis_index("seq")
    x_own = tokens.reshape(rows, width)
    dout_own = out_grad.reshape(rows, width)

    columns = columns_by_device(
        (weight_query, weight_key, weight_value, weight_gate, weight_up), seq_count
    )
    columns = lax.all_to_all(columns, "seq", split_axis=0, concat_axis=0, tiled=True)
    w_out_rows = lax.all_gather(weight_out, "fsdp", axis=0, tiled=True)
    columns = after(columns, w_out_rows)
    w_qkv = jnp.broadcast_to(
        columns[None, :, :, : 3 * WIDE], (z_count, seq_count, shard, 3 * WIDE)
    )
    w_qkv = gathered(lax.all_to_all(w_qkv, "fsdp", split_axis=0, concat_axis=0, tiled=True))
    w_down = lax.all_gather(weight_down, "fsdp", axis=0, tiled=True)
    if features < WIDE:
        w_out_rows = jnp.pad(w_out_rows, ((0, WIDE - features), (0, 0)))
    gu_columns = columns[:, :, 3 * WIDE :]
    w_gu = gathered(lax.all_gather(gu_columns, "fsdp", axis=0, tiled=False))

    ids = jnp.concatenate([variate_ids, sample_ids, time_ids // 64, time_ids % 64], axis=0)
    ids = jnp.pad(ids.astype(BF16), ((0, 12), (0, width - rows)))
    packed = after(jnp.concatenate([x_own, ids], axis=0), columns, w_out_rows)
    near_x = to_chips(packed, seq_count)
    extra = after(jnp.concatenate([dout_own, w_out_rows], axis=0), near_x[1:2])
    stack_x = jnp.concatenate(after(near_x, w_qkv, gu_columns, extra), axis=0)
    far_x = swap(stack_x, seq_count, 1)
    near_extra = to_chips(extra, seq_count)

    gain_attn = norm_attn.reshape(1, width)
    gain_ffn = norm_ffn.reshape(1, width)
    q_gain = jnp.tile(query_gain, WIDE // head_size).reshape(1, WIDE)
    k_gain = jnp.tile(key_gain, WIDE // head_size).reshape(1, WIDE)
    frequency = (10000.0 ** (-2.0 * jnp.arange(half_size).astype(F32) / head_size))[:, None]

    def projected(x):
        return project(
            x, chips, w_qkv, gain_attn, q_gain, k_gain, frequency, variate_bias, head_size
        )

    near_all = projected(stack_x)
    far_all = projected(far_x)
    nin, q_lin, k_lin, lane_rows, q_aug, k_aug, k_trans, v_aug = zip(near_all, far_all)
    attend_near = attend(q_aug[0], k_aug, v_aug, head_size)
    attend_far = attend(after(q_aug[1], attend_near, near_extra[1:2]), k_aug, v_aug, head_size)
    far_extra = [swap(e, seq_count, 1) for e in after(near_extra, attend_far)]
    mixed, o_full, z_inverse = zip(attend_near, attend_far)
    own_parts = [to_chips(mixed[side], seq_count) for side in (0, 1)]
    own_parts[0] = after(own_parts[0], attend_far)
    sib_stack = [swap(jnp.concatenate(own_parts[side], axis=0), seq_count, 1) for side in (0, 1)]

    nm_far, inner_far, ggu_far, dout_far, gnm_far, lay_far = ffn(
        1, own_parts[1], sib_stack[0], far_x, near_extra, far_extra, w_gu, w_down, gain_ffn
    )
    nm_near, inner_near, ggu_near, dout_near, middle, mixed_own, *slots = ffn(
        0, own_parts[0], sib_stack[1], stack_x, near_extra, far_extra, w_gu, w_down, gain_ffn,
        swap(gnm_far, seq_count, 1), group=16 // chips,
    )

    gnm_parts = spread_slots(slots[:chips], seq_count)
    grad_gu, grad_down, gnf = ffn_grads(
        (nm_near, nm_far), (ggu_near, ggu_far), (inner_near, inner_far), (dout_near, dout_far),
        w_gu, seq_count, z_count, swap(slots[0][:8, :WIDE], seq_count, 1),
    )
    me_row = jnp.reshape(me, (1,))
    grad_middle, grad_branch, g_out = middle_back(
        after(gnm_parts, grad_gu, grad_down),
        middle, gain_ffn, near_extra, far_extra, me_row,
    )
    g_all = lax.all_to_all(g_out, "seq", split_axis=0, concat_axis=0, tiled=True)

    grad_gu = lax.psum_scatter(grad_gu, "fsdp", scatter_dimension=0, tiled=True)
    grad_gu = grad_gu.reshape(seq_count, shard, 2 * hidden)
    grad_down = lax.psum_scatter(grad_down, "fsdp", scatter_dimension=0, tiled=True)
    grad_out = dot_tn(mixed_own, grad_branch).astype(BF16)
    half_out = chips * WIDE
    out_slots = add_up([grad_out[:half_out], swap(grad_out[half_out:], seq_count, 1)])
    out_slots = out_slots.astype(BF16)
    lay_got = swap(after(lay_far, grad_branch), seq_count, 1)
    both_slots = []
    for r in range(chips):
        lay = add_up([slots[chips + r], lay_got[r * rows : (r + 1) * rows]]).astype(BF16)
        both_slots.append(jnp.concatenate([lay, out_slots[r * WIDE : (r + 1) * WIDE]], axis=0))
    both_parts = spread_slots(after(both_slots, g_all), seq_count)
    gu_got = lax.all_to_all(
        after(grad_gu, g_all), "seq", split_axis=0, concat_axis=0, tiled=True
    )

    dq_near, dq_far, dk, dv, bias_rows = attend_back(
        me_row, after(g_all, both_slots),
        q_aug, o_full, z_inverse, lane_rows, k_aug, k_trans, v_aug, head_size,
    )
    dq_far = after(dq_far, grad_gu)
    gl_near, gl_far, gain_rows = project_back(
        (dq_near, dq_far), q_lin, k_lin, lane_rows, dk, dv, q_gain, k_gain, head_size, chips
    )
    (gni_far,) = spread_back(after(gl_far, both_parts), w_qkv, chips)
    gni_got = swap(gni_far, seq_count, 1)
    grad_qkv, gna = pair_product(
        nin, (gl_near, gl_far), w_qkv, swap(gain_rows, seq_count, 1)
    )

    grad_qk_gain = gain_rows[:2, :features].reshape(2, heads, head_size).sum(axis=1)
    bias_cols = jnp.sum(bias_rows, axis=1).reshape(2, 2, 4).sum(axis=2)[:, :heads]
    bias_both = jnp.stack([bias_cols[0], bias_cols[1] - bias_cols[0]])
    bias_all = lax.dynamic_update_slice(
        jnp.zeros((2, heads * seq_count), F32), bias_both, (0, me * heads)
    )
    small = jnp.concatenate(
        [
            gna[0] / norm_attn,
            gnf / norm_ffn,
            grad_qk_gain.reshape(-1),
            bias_all.reshape(-1),
        ]
    )
    count = small.shape[0]
    small_rows = -(-count // (8 * 3 * WIDE)) * 8
    small = jnp.pad(small, (0, small_rows * 3 * WIDE - count)).astype(BF16)
    small = jnp.broadcast_to(small.reshape(1, small_rows, 3 * WIDE), (everyone, small_rows, 3 * WIDE))
    grad_qkv = after(grad_qkv, gu_got)
    blocks = jnp.concatenate([grad_qkv.reshape(everyone, shard, 3 * WIDE), small], axis=1)
    last = lax.all_to_all(blocks, ("seq", "fsdp"), split_axis=0, concat_axis=0, tiled=True)
    gni_slots = spread_back(
        gl_near, w_qkv, chips, after(gni_got, blocks)
    )
    gni_parts = spread_slots(gni_slots, seq_count)
    both = add_up(after(both_parts, gni_slots))
    grad_out = both[rows : rows + features]
    z_me = lax.axis_index("fsdp")
    bit = z_count // 2
    while bit:
        low, high = jnp.split(grad_out, 2, axis=0)
        upper = (z_me & bit) > 0
        away = jnp.where(upper, low, high).astype(BF16)
        away = lax.ppermute(away, "fsdp", [(i, i ^ bit) for i in range(z_count)])
        grad_out = jnp.where(upper, high, low) + away.astype(F32)
        bit //= 2
    in_grad = input_back(gni_parts, x_own, grad_middle, gain_attn)

    gu_got = after(gu_got, gni_slots)
    grad_down = after(grad_down, gni_slots)
    layer_out = (middle + both[:rows]).astype(BF16)
    grad_gu = gu_got.transpose(1, 0, 2).astype(F32)
    grad_gate = grad_gu[:, :, :hidden].reshape(shard, seq_count * hidden)
    grad_up = grad_gu[:, :, hidden:].reshape(shard, seq_count * hidden)
    grad_down = grad_down.astype(F32)
    *grad_qkv, small = last_sums(after(last, in_grad, grad_out, grad_down), z_count, shard)
    grad_query, grad_key, grad_value = (
        g.reshape(shard, seq_count, WIDE)[:, :, :features].reshape(shard, width)
        if features < WIDE
        else g
        for g in grad_qkv
    )
    small = small.reshape(-1)
    cut = 2 * width + 2 * head_size
    grad_bias = lax.dynamic_slice(
        small[cut:count].reshape(2, heads * seq_count), (0, me * heads), (2, heads)
    )
    return (
        layer_out.reshape(tokens.shape),
        in_grad.reshape(tokens.shape),
        grad_query,
        grad_key,
        grad_value,
        grad_out,
        grad_gate,
        grad_up,
        grad_down,
        small[:width],
        small[width : 2 * width],
        small[2 * width : 2 * width + head_size],
        small[2 * width + head_size : cut],
        grad_bias,
    )


def solution(mesh):
    rows = P("fsdp", "seq", None)
    shards = P(("seq", "fsdp"), None)
    ids = P("fsdp", "seq")
    bias = P(None, "seq")
    return jax.shard_map(
        body,
        mesh=mesh,
        in_specs=(rows,) + (shards,) * 7 + (P(),) * 4 + (bias, ids, ids, ids, rows),
        out_specs=(rows, rows) + (shards,) * 7 + (P(),) * 4 + (bias,),
        check_vma=False,
    )
```

```python
import functools
import math

import jax
import jax.numpy as jnp
from jax import lax
from jax.experimental import pallas as pl
from jax.experimental.pallas import tpu as pltpu
from jax.sharding import PartitionSpec as P

EPSILON = 1e-06
FAR = -1e30
LOG2E = math.log2(math.e)
WIDE = 128
ROWS_T = 160
F32 = jnp.float32
BF16 = jnp.bfloat16


def dot_nn(left, right):
    return jnp.dot(left, right, preferred_element_type=F32)


def dot_nt(left, right):
    return lax.dot_general(left, right, (((1,), (1,)), ((), ())), preferred_element_type=F32)


def dot_tn(left, right):
    return lax.dot_general(left, right, (((0,), (0,)), ((), ())), preferred_element_type=F32)


def rms_factor(values):
    return lax.rsqrt(jnp.mean(values * values, axis=-1, keepdims=True) + EPSILON)


def lanes_of(shape):
    return lax.broadcasted_iota(jnp.int32, shape, len(shape) - 1)


def head_sum(values, blocks):
    high = values.astype(BF16)
    low = (values - high.astype(F32)).astype(BF16)
    return dot_nn(high, blocks) + dot_nn(low, blocks)


def head_blocks(head_size):
    row = lax.broadcasted_iota(jnp.int32, (WIDE, WIDE), 0) // head_size
    column = lax.broadcasted_iota(jnp.int32, (WIDE, WIDE), 1) // head_size
    return jnp.where(row == column, 1.0, 0.0).astype(BF16)


def partner(values, lane, head_size):
    half = head_size // 2
    up = pltpu.roll(values, WIDE - half, 1)
    down = pltpu.roll(values, half, 1)
    return jnp.where(lane % head_size < half, up, down)


def tables(cosine, sine):
    times = WIDE // (2 * cosine.shape[0])
    cos_rows = jnp.concatenate([cosine, cosine] * times, axis=0)
    sin_rows = jnp.concatenate([-sine, sine] * times, axis=0)
    return cos_rows.T, sin_rows.T


def params(grid=True):
    return pltpu.CompilerParams(
        vmem_limit_bytes=60 * 1024 * 1024,
        dimension_semantics=("arbitrary",) if grid else None,
    )


def whole(array):
    return pl.BlockSpec(array.shape, lambda *_: (0,) * len(array.shape))


def shaped(shape, dtype):
    return jax.ShapeDtypeStruct(shape, dtype)


ANY = pl.BlockSpec(memory_space=pl.ANY)


def assemble(out_ref, in_ref):
    if len(in_ref.shape) == 2:
        out_ref[...] = in_ref[...]
        return
    z_count, seq_count, shard, _ = in_ref.shape
    for f in range(z_count):
        for s in range(seq_count):
            at = (s * z_count + f) * shard
            out_ref[at : at + shard, :] = in_ref[f, s]


def gathered(w):
    if w.shape[2] % 16 == 0:
        return w
    return w.transpose(1, 0, 2, 3).reshape(-1, w.shape[-1])


def columns_kernel(*refs):
    *weights, out_ref = refs
    at = 0
    for w_ref in weights:
        wide = w_ref.shape[1] // out_ref.shape[0]
        for s in range(out_ref.shape[0]):
            out_ref[s, :, at : at + wide] = w_ref[:, s * wide : (s + 1) * wide]
        at += wide


def columns_by_device(weights, seq_count):
    shard = weights[0].shape[0]
    wides = [w.shape[1] // seq_count for w in weights]
    if shard % 16 == 0 and all(wide % WIDE == 0 for wide in wides):
        return pl.pallas_call(
            columns_kernel,
            out_shape=shaped((seq_count, shard, sum(wides)), BF16),
            compiler_params=params(False),
            name="columns",
        )(*weights)
    pieces = []
    for w, wide in zip(weights, wides):
        short = -wide % WIDE
        pieces.append(jnp.pad(w.reshape(shard, seq_count, wide), ((0, 0), (0, 0), (0, short))))
    return jnp.concatenate(pieces, axis=2).transpose(1, 0, 2)


def project_kernel(
    x_ref, w_ref, na_ref, qg_ref, kg_ref, freq_ref, bias_ref,
    nin_ref, qlin_ref, klin_ref, lane_ref, qa_ref, ka_ref, kt_ref, v1_ref, w_s, *, heads, head_size,
):
    half = head_size // 2
    rows = nin_ref.shape[0]

    @pl.when(pl.program_id(0) == 0)
    def _():
        assemble(w_s, w_ref)

    x = x_ref[:rows, :].astype(F32)
    ids = x_ref[rows:, :rows].astype(F32)
    nin = (x * rms_factor(x) * na_ref[...]).astype(BF16)
    nin_ref[...] = nin
    lin = dot_nn(nin, w_s[...])
    q, k, v = lin[:, :WIDE], lin[:, WIDE : 2 * WIDE], lin[:, 2 * WIDE :]
    qlin_ref[...] = q
    klin_ref[...] = k
    angles = freq_ref[...] * (ids[2:3] * 64.0 + ids[3:4])
    cosine, sine = jnp.cos(angles), jnp.sin(angles)
    lane_ref[...] = jnp.concatenate([cosine, sine, ids[:8]], axis=0)
    cosine, sine = tables(cosine, sine)
    lane = lanes_of((rows, WIDE))
    blocks = head_blocks(head_size)

    def finish(u, gain):
        factor = lax.rsqrt(head_sum(u * u, blocks) * (1.0 / head_size) + EPSILON)
        u = u * factor * gain
        return u * cosine + partner(u, lane, head_size) * sine

    q = finish(q, qg_ref[...]) * (LOG2E * head_size**-0.5)
    k = finish(k, kg_ref[...])
    few = ROWS_T - WIDE
    row = lax.broadcasted_iota(jnp.int32, (few, rows), 0)
    variate = ids[0:1].astype(jnp.int32)
    sample = ids[1:2].astype(jnp.int32)
    same_variate = (row % 4) == variate
    same_sample = (row - 10) == sample
    one = jnp.ones((few, rows), F32)
    nil = jnp.zeros((few, rows), F32)
    rest = jnp.zeros((WIDE - few, rows), F32)

    def columns(few_rows):
        return jnp.concatenate([few_rows, rest], axis=0).T

    aug_q = jnp.where(
        row < 8,
        jnp.where(same_variate, one, nil),
        jnp.where(row < 10, one, jnp.where((row < 13) & same_sample, one, nil)),
    )
    qa_ref[...] = jnp.concatenate([q, columns(aug_q)], axis=1).astype(BF16)
    k_t = k.T
    row_k = lax.broadcasted_iota(jnp.int32, (WIDE, rows), 0)
    for h in range(heads):
        first, second = bias_ref[0, h] * LOG2E, bias_ref[1, h] * LOG2E
        step_up = jnp.where(row < 8, first - second, second) * one
        high = step_up.astype(BF16).astype(F32)
        low = step_up - high
        far = jnp.where(same_sample, nil, FAR)
        plain = jnp.where(((row // 4) == 4 + h) & same_variate, one, nil)
        aug_k = jnp.where(
            row < 4,
            jnp.where(same_variate, high, nil),
            jnp.where(
                row < 8,
                jnp.where(same_variate, low, nil),
                jnp.where(
                    row == 8,
                    high,
                    jnp.where(row == 9, low, jnp.where(row < 13, far, plain)),
                ),
            ),
        )
        mine = (lane // head_size) == h
        mine_t = (row_k // head_size) == h
        ka_ref[h] = jnp.concatenate([jnp.where(mine, k, 0.0), columns(aug_k)], axis=1).astype(BF16)
        kt_ref[h] = jnp.concatenate([jnp.where(mine_t, k_t, 0.0), aug_k], axis=0).astype(BF16)
        ones_v = jnp.where((lane == h) | (lane == 2 + h), 1.0, 0.0)
        v1_ref[h] = jnp.concatenate([jnp.where(mine, v, 0.0), ones_v], axis=1).astype(BF16)


def project(x, chips, w, norm_attn, q_gain, k_gain, freq, bias, head_size):
    width, wide = x.shape[1], w.shape[-1]
    rows = x.shape[0] // chips - 16
    heads = bias.shape[1]
    half = chips * rows
    count = head_size + 8
    row_block = lambda cols: pl.BlockSpec((rows, cols), lambda i: (i, 0))
    lane_block = pl.BlockSpec((count, rows), lambda i: (0, i))
    head_block = pl.BlockSpec((heads, rows, 2 * WIDE), lambda i: (0, i, 0))
    return pl.pallas_call(
        functools.partial(project_kernel, heads=heads, head_size=head_size),
        grid=(chips,),
        in_specs=[pl.BlockSpec((rows + 16, width), lambda i: (i, 0))]
        + [whole(a) for a in (w, norm_attn, q_gain, k_gain, freq)]
        + [pl.BlockSpec(memory_space=pltpu.SMEM)],
        out_specs=[
            row_block(width), row_block(WIDE), row_block(WIDE), lane_block, row_block(2 * WIDE),
            head_block, pl.BlockSpec((heads, ROWS_T, rows), lambda i: (0, 0, i)), head_block,
        ],
        out_shape=[
            shaped((half, width), BF16),
            shaped((half, WIDE), F32),
            shaped((half, WIDE), F32),
            shaped((count, half), F32),
            shaped((half, 2 * WIDE), BF16),
            shaped((heads, half, 2 * WIDE), BF16),
            shaped((heads, ROWS_T, half), BF16),
            shaped((heads, half, 2 * WIDE), BF16),
        ],
        scratch_shapes=[pltpu.VMEM((width, wide), BF16)],
        compiler_params=params(),
        cost_estimate=pl.CostEstimate(
            flops=2 * half * width * 3 * WIDE, bytes_accessed=half * width * 8, transcendentals=0
        ),
        name="project",
    )(x, w, norm_attn, q_gain, k_gain, freq, bias)


def attend_kernel(qa_ref, ka0, ka1, v10, v11, mixed_ref, o_ref, zi_ref, *, heads, head_size, chunk):
    qa = qa_ref[...]
    rows = qa.shape[0]
    half = ka0.shape[1]
    lane = lanes_of((rows, WIDE))
    total = jnp.zeros((rows, WIDE), F32)
    inverse = jnp.ones((rows, WIDE), F32)
    for h in range(heads):
        acc = jnp.zeros((rows, 2 * WIDE), F32)
        for ka_ref, v1_ref in ((ka0, v10), (ka1, v11)):
            for c in range(half // chunk):
                part = pl.ds(c * chunk, chunk)
                e = jnp.exp2(dot_nt(qa, ka_ref[h, part, :])).astype(BF16)
                acc = acc + dot_nn(e, v1_ref[h, part, :])
        z_inv = 1.0 / acc[:, WIDE + h : WIDE + h + 1]
        total = total + acc[:, :WIDE] * z_inv
        inverse = jnp.where((lane // head_size) == h, z_inv, inverse)
    mixed_ref[...] = total.astype(BF16)
    o_ref[...] = total
    zi_ref[...] = inverse


def attend(qa, ka, v1, head_size, block=512, chunk=256):
    heads, half, _ = ka[0].shape
    out_block = pl.BlockSpec((block, WIDE), lambda i: (i, 0))
    return pl.pallas_call(
        functools.partial(attend_kernel, heads=heads, head_size=head_size, chunk=chunk),
        grid=(half // block,),
        in_specs=[pl.BlockSpec((block, 2 * WIDE), lambda i: (i, 0))]
        + [whole(a) for a in (*ka, *v1)],
        out_specs=[out_block, out_block, out_block],
        out_shape=[shaped((half, WIDE), BF16), shaped((half, WIDE), F32), shaped((half, WIDE), F32)],
        compiler_params=params(),
        cost_estimate=pl.CostEstimate(
            flops=2 * heads * half * half * 8 * WIDE,
            bytes_accessed=half * WIDE * 32,
            transcendentals=2 * heads * half * half,
        ),
        name="attend",
    )(qa, *ka, *v1)


def attend_back_kernel(*refs, chips, heads, head_size, chunk):
    me_ref, g_ref = refs[:2]
    at = 2
    qa, o, zi, lanes, ka, kt, v1 = [refs[at + 2 * n : at + 2 * n + 2] for n in range(7)]
    at += 14
    dq_refs = refs[at : at + 2]
    dk_ref, dv_ref, bias_ref, g_s, dk_s, dv_s = refs[at + 2 :]
    step = pl.program_id(0)

    @pl.when(step == 0)
    def _():
        dk_s[...] = jnp.zeros_like(dk_s)
        dv_s[...] = jnp.zeros_like(dv_s)
        bias_ref[...] = jnp.zeros_like(bias_ref)
        for j in range(2 * chips):
            g_s[j % 2, j // 2] = g_ref[me_ref[0] ^ j]

    for side in range(2):
        q_rows = qa[side][...]
        rows = q_rows.shape[0]
        half_len = ka[0].shape[1]
        lane = lanes_of((rows, WIDE))
        q = q_rows[:, :WIDE]
        gz = (g_s[side, step].astype(F32) * zi[side][...]).astype(BF16)
        inner = gz.astype(F32) * o[side][...]
        aug = jnp.zeros((rows, WIDE), F32)
        for h in range(heads):
            mean = -jnp.sum(
                jnp.where((lane // head_size) == h, inner, 0.0), axis=-1, keepdims=True
            ) * jnp.ones((rows, WIDE), F32)
            high = mean.astype(BF16).astype(F32)
            aug = jnp.where(lane == h, high, jnp.where(lane == 2 + h, mean - high, aug))
        ga = jnp.concatenate([gz, aug.astype(BF16)], axis=1)
        dq_t = jnp.zeros((ROWS_T, rows), F32)
        for h in range(heads):
            mine = (lane // head_size) == h
            q_h = jnp.where(mine, q, jnp.zeros_like(q))
            g_h = jnp.where(mine, gz, jnp.zeros_like(gz))
            for other in range(2):
                for c in range(half_len // chunk):
                    part = pl.ds(c * chunk, chunk)
                    e = jnp.exp2(dot_nt(ka[other][h, part, :], q_rows))
                    ds = (e * dot_nt(v1[other][h, part, :], ga)).astype(BF16)
                    dv_s[other, part, :] += dot_nn(e.astype(BF16), g_h)
                    dk_s[other, part, :] += dot_nn(ds, q_h)
                    dq_t = dq_t + dot_nn(kt[other][h, :, part], ds)
        dq_refs[side][...] = (dq_t[:WIDE].T * (head_size**-0.5)).astype(BF16)
        variate = lanes[side][head_size : head_size + 1, :].astype(jnp.int32)
        columns = dq_t[WIDE + 16 : WIDE + 24]
        row = lax.broadcasted_iota(jnp.int32, columns.shape, 0)
        bias_ref[...] += jnp.concatenate(
            [jnp.where((row % 4) == variate, columns, 0.0), columns], axis=0
        )

    @pl.when(step == pl.num_programs(0) - 1)
    def _():
        dk_ref[...] = (dk_s[...] * (1.0 / LOG2E)).astype(BF16)
        dv_ref[...] = dv_s[...].astype(BF16)


def attend_back(me, g, qa, o, zi, lane_rows, ka, kt, v1, head_size, chunk=1024):
    heads, half, _ = ka[0].shape
    chips = g.shape[0] // 2
    chunk = math.gcd(half, chunk)
    block = half // chips
    count = lane_rows[0].shape[0]
    row_block = lambda cols: pl.BlockSpec((block, cols), lambda i: (i, 0))
    lane_block = pl.BlockSpec((count, block), lambda i: (0, i))
    full = shaped((2, half, WIDE), BF16)
    return pl.pallas_call(
        functools.partial(
            attend_back_kernel, chips=chips, heads=heads, head_size=head_size, chunk=chunk
        ),
        grid=(chips,),
        in_specs=[pl.BlockSpec(memory_space=pltpu.SMEM), whole(g)]
        + [row_block(2 * WIDE)] * 2
        + [row_block(WIDE)] * 4
        + [lane_block] * 2
        + [whole(a) for a in (*ka, *kt, *v1)],
        out_specs=[row_block(WIDE)] * 2
        + [whole(full), whole(full), pl.BlockSpec((16, block), lambda i: (0, 0))],
        out_shape=[shaped((half, WIDE), BF16)] * 2 + [full, full, shaped((16, block), F32)],
        scratch_shapes=[
            pltpu.VMEM((2, chips, block, WIDE), BF16),
            pltpu.VMEM((2, half, WIDE), F32),
            pltpu.VMEM((2, half, WIDE), F32),
        ],
        compiler_params=params(),
        cost_estimate=pl.CostEstimate(
            flops=2 * heads * half * half * 32 * WIDE,
            bytes_accessed=half * WIDE * 64,
            transcendentals=4 * heads * half * half,
        ),
        name="attend_back",
    )(me, g, *qa, *o, *zi, *lane_rows, *ka, *kt, *v1)


def ffn_kernel(*refs, chips, group, near):
    mixed = refs[: 2 * chips]
    extra_parts = refs[2 * chips : 4 * chips]
    at = 4 * chips
    x_ref, wgu_ref, wd_ref, nf_ref = refs[at : at + 4]
    at += 4
    if near:
        got_ref = refs[at]
        at += 1
    nm_ref, inner_ref, ggu_ref, dout_ref = refs[at : at + 4]
    at += 4
    if near:
        mid_ref, mixed_ref = refs[at : at + 2]
        gnm_refs = refs[at + 2 : at + 2 + chips]
        lay_refs = refs[at + 2 + chips : at + 2 + 2 * chips]
        at += 2 + 2 * chips
    else:
        gnm_ref, lay_ref = refs[at : at + 2]
        at += 2
    w_s, wo_s, extra_s, sems = refs[at:]
    step = pl.program_id(0)
    rows = nm_ref.shape[0] // group

    @pl.when(step == 0)
    def _():
        copies = [
            pltpu.make_async_copy(part, extra_s.at[j], sems.at[j])
            for j, part in enumerate(extra_parts)
        ]
        for copy in copies:
            copy.start()
        assemble(w_s, wgu_ref)
        for j, copy in enumerate(copies):
            copy.wait()
            wo_s[j * WIDE : (j + 1) * WIDE, :] = extra_s[j, rows:, :]

    def own_order(block, r):
        if r % group == 0:
            return block
        slots = [(t ^ (r % group)) * rows for t in range(group)]
        return jnp.concatenate([block[at : at + rows] for at in slots], axis=0)

    cat = jnp.concatenate([own_order(m[...], j % chips) for j, m in enumerate(mixed)], axis=1)
    hidden = wd_ref.shape[0]
    x = [x_ref[t * (rows + 16) : t * (rows + 16) + rows, :] for t in range(group)]
    first = (0 if near else chips) + step * group
    dout = jnp.concatenate([extra_s[first + t, :rows, :] for t in range(group)], axis=0)
    dout_ref[...] = dout
    middle = jnp.concatenate(x, axis=0).astype(F32) + dot_nn(cat, wo_s[...])
    nm = (middle * rms_factor(middle) * nf_ref[...]).astype(BF16)
    nm_ref[...] = nm
    lin = dot_nn(nm, w_s[...])
    back = dot_nt(dout, wd_ref[...])
    gate, up = lin[:, :hidden], lin[:, hidden:]
    sig = jax.nn.sigmoid(gate)
    silu = gate * sig
    inner = (silu * up).astype(BF16)
    inner_ref[...] = inner
    g_gate = (back * up * (sig * (1.0 + gate * (1.0 - sig)))).astype(BF16)
    g_up = (back * silu).astype(BF16)
    ggu = jnp.concatenate([g_gate, g_up], axis=1)
    ggu_ref[...] = ggu
    gnm = dot_nt(ggu, w_s[...])
    lay = dot_nn(inner, wd_ref[...])
    if near:

        @pl.when(step == 0)
        def _():
            mid_ref[...] = middle[:rows]
            mixed_ref[...] = cat[:rows]

        gnm = (gnm + got_ref[...].astype(F32)).astype(BF16)
        lay = lay.astype(BF16)
        for r in range(chips):

            @pl.when(step == r // group)
            def _(r=r):
                at = (r % group) * rows
                gnm_refs[r][...] = gnm[at : at + rows]
                lay_refs[r][...] = lay[at : at + rows]

    else:
        gnm_ref[...] = gnm.astype(BF16)
        lay_ref[...] = lay.astype(BF16)


def ffn(
    side, own_parts, sib_stack, x, near_extra, far_extra, wgu, wd, norm_ffn, got=None, group=2
):
    chips = len(own_parts)
    group = math.gcd(chips, group)
    rows, width = near_extra[0].shape
    rows -= WIDE
    half = rows * chips
    block = rows * group
    steps = chips // group
    hidden = wd.shape[0]
    near = side == 0
    row_block = lambda cols: pl.BlockSpec((block, cols), lambda i: (i, 0))
    piece = lambda r: pl.BlockSpec((block, WIDE), lambda i: (i ^ (r // group), 0))
    stack = lambda r: pl.BlockSpec((block, WIDE), lambda i: (r * steps + (i ^ (r // group)), 0))
    out_shape = [
        shaped((half, width), BF16), shaped((half, hidden), BF16), shaped((half, 2 * hidden), BF16),
        shaped((half, width), BF16),
    ]
    out_specs = [row_block(width), row_block(hidden), row_block(2 * hidden), row_block(width)]
    if near:
        more = [shaped((rows, width), F32), shaped((rows, 2 * chips * WIDE), BF16)]
        more += [shaped((rows, width), BF16)] * (2 * chips)
        out_shape += more
        out_specs += [whole(a) for a in more]
    else:
        out_shape += [shaped((half, width), BF16)] * 2
        out_specs += [row_block(width)] * 2
    return pl.pallas_call(
        functools.partial(ffn_kernel, chips=chips, group=group, near=near),
        grid=(steps,),
        in_specs=[piece(r) for r in range(chips)]
        + [stack(r) for r in range(chips)]
        + [ANY] * (2 * chips)
        + [pl.BlockSpec((group * (rows + 16), width), lambda i: (i, 0))]
        + [whole(a) for a in (wgu, wd, norm_ffn)]
        + ([row_block(width)] if near else []),
        out_specs=out_specs,
        out_shape=out_shape,
        scratch_shapes=[
            pltpu.VMEM((width, 2 * hidden), BF16),
            pltpu.VMEM((2 * chips * WIDE, width), BF16),
            pltpu.VMEM((2 * chips, rows + WIDE, width), BF16),
            pltpu.SemaphoreType.DMA((2 * chips,)),
        ],
        compiler_params=params(),
        cost_estimate=pl.CostEstimate(
            flops=2 * half * width * (2 * chips * WIDE + 6 * hidden),
            bytes_accessed=half * width * 12,
            transcendentals=half * hidden,
        ),
        name="ffn_half",
    )(
        *own_parts, *[sib_stack] * chips, *near_extra, *far_extra, x, wgu, wd, norm_ffn,
        *([got] if near else []),
    )


def row_sums(product, w_ref):
    w = w_ref[...].astype(F32)
    if len(w.shape) == 4:
        z_count, parts, _, _ = w.shape
        w = jnp.concatenate([w[f, s] for s in range(parts) for f in range(z_count)], axis=0)
    total = jnp.sum(product * w, axis=1, keepdims=True)
    return (total * jnp.ones((product.shape[0], WIDE), F32)).T[:8]


def block_of(w, steps):
    if len(w.shape) == 2:
        return pl.BlockSpec((w.shape[0] // steps, w.shape[1]), lambda i: (i, 0))
    block = (w.shape[0], w.shape[1] // steps) + w.shape[2:]
    return pl.BlockSpec(block, lambda i: (0, i, 0, 0))


def ffn_grads_kernel(nm0, nm1, ggu0, ggu1, in0, in1, dout0, dout1, w_ref, _, gu_ref, gd_ref, sum_ref):
    gu = dot_tn(nm0[...], ggu0[...]) + dot_tn(nm1[...], ggu1[...])
    sum_ref[...] = row_sums(gu, w_ref)
    gu = gu.astype(BF16)
    if len(gu_ref.shape) == 2:
        gu_ref[...] = gu
    else:
        z_count, parts, shard, _ = gu_ref.shape
        for f in range(z_count):
            for s in range(parts):
                at = (s * z_count + f) * shard
                gu_ref[f, s] = gu[at : at + shard]
    gd_ref[...] = (dot_tn(in0[...], dout0[...]) + dot_tn(in1[...], dout1[...])).astype(BF16)


def ffn_grads(nm, ggu, inner, dout, w, seq_count, z_count, ticket):
    half, width = nm[0].shape
    hidden = inner[0].shape[1]
    shard = width // (seq_count * z_count)
    steps = max(1, min(4, hidden // WIDE))
    column_block = lambda cols: pl.BlockSpec((half, cols // steps), lambda i: (0, i))
    if shard % 16 == 0 and seq_count % steps == 0:
        gu = shaped((z_count, seq_count, shard, 2 * hidden), BF16)
        gu_spec = pl.BlockSpec(
            (z_count, seq_count // steps, shard, 2 * hidden), lambda i: (0, i, 0, 0)
        )
    else:
        gu = shaped((width, 2 * hidden), BF16)
        gu_spec = pl.BlockSpec((width // steps, 2 * hidden), lambda i: (i, 0))
    gu, gd, sums = pl.pallas_call(
        ffn_grads_kernel,
        grid=(steps,),
        in_specs=[column_block(width)] * 2
        + [whole(a) for a in ggu]
        + [column_block(hidden)] * 2
        + [whole(a) for a in dout]
        + [block_of(w, steps), ANY],
        out_specs=[
            gu_spec,
            pl.BlockSpec((hidden // steps, width), lambda i: (i, 0)),
            pl.BlockSpec((8, width // steps), lambda i: (0, i)),
        ],
        out_shape=[gu, shaped((hidden, width), BF16), shaped((8, width), F32)],
        compiler_params=params(),
        cost_estimate=pl.CostEstimate(
            flops=2 * half * width * 6 * hidden, bytes_accessed=half * width * 16, transcendentals=0
        ),
        name="ffn_grads",
    )(*nm, *ggu, *inner, *dout, w, ticket)
    if len(gu.shape) == 2:
        gu = gu.reshape(seq_count, z_count, shard, 2 * hidden).transpose(1, 0, 2, 3)
    return gu.reshape(width, 2 * hidden), gd, sums[0]


def pair_kernel(a0, a1, b0, b1, w_ref, _, out_ref, sum_ref):
    product = dot_tn(a0[...], b0[...]) + dot_tn(a1[...], b1[...])
    out_ref[...] = product.astype(BF16)
    sum_ref[...] = row_sums(product, w_ref)


def pair_product(left, right, w, ticket, steps=4):
    half, width = left[0].shape
    wide = right[0].shape[1]
    return pl.pallas_call(
        pair_kernel,
        grid=(steps,),
        in_specs=[pl.BlockSpec((half, width // steps), lambda i: (0, i))] * 2
        + [whole(a) for a in right]
        + [block_of(w, steps), ANY],
        out_specs=[
            pl.BlockSpec((width // steps, wide), lambda i: (i, 0)),
            pl.BlockSpec((8, width // steps), lambda i: (0, i)),
        ],
        out_shape=[shaped((width, wide), BF16), shaped((8, width), F32)],
        compiler_params=params(),
        cost_estimate=pl.CostEstimate(
            flops=4 * half * width * wide, bytes_accessed=half * width * 6, transcendentals=0
        ),
        name="pair_product",
    )(*left, *right, w, ticket)


def added(pieces):
    total = pieces[0][...].astype(F32)
    for piece in pieces[1:]:
        total = total + piece[...].astype(F32)
    return total


def norm_back(values, gain, incoming):
    factor = rms_factor(values)
    weighted = incoming * gain
    return factor * weighted - values * (factor * factor * factor) * jnp.mean(
        weighted * values, axis=-1, keepdims=True
    )


def middle_back_kernel(*refs, chips):
    extra = refs[chips : 3 * chips]
    mid_ref, nf_ref, me_ref, gm_ref, gb_ref, out_ref = refs[3 * chips :]
    rows = mid_ref.shape[0]
    grad = extra[0][:rows, :].astype(F32) + norm_back(mid_ref[...], nf_ref[...], added(refs[:chips]))
    gm_ref[...] = grad
    branch = grad.astype(BF16)
    gb_ref[...] = branch
    for side in range(2):
        for r in range(chips):
            part = dot_nt(branch, extra[side * chips + r][rows:, :])
            out_ref[me_ref[0] ^ (2 * r + side)] = part.astype(BF16)


def middle_back(pieces, middle, norm_ffn, near_extra, far_extra, me):
    chips = len(pieces)
    rows, width = middle.shape
    vmem = pl.BlockSpec(memory_space=pltpu.VMEM)
    return pl.pallas_call(
        functools.partial(middle_back_kernel, chips=chips),
        in_specs=[vmem] * (3 * chips + 2) + [pl.BlockSpec(memory_space=pltpu.SMEM)],
        out_shape=[
            shaped((rows, width), F32), shaped((rows, width), BF16),
            shaped((2 * chips, rows, WIDE), BF16),
        ],
        compiler_params=params(False),
        cost_estimate=pl.CostEstimate(
            flops=2 * rows * width * 2 * chips * WIDE,
            bytes_accessed=rows * width * 12,
            transcendentals=0,
        ),
        name="middle_back",
    )(*pieces, *near_extra, *far_extra, middle, norm_ffn, me)


def input_back_kernel(*refs, chips):
    x_ref, gm_ref, na_ref, out_ref = refs[chips:]
    out_ref[...] = gm_ref[...] + norm_back(x_ref[...].astype(F32), na_ref[...], added(refs[:chips]))


def input_back(pieces, x, grad_middle, norm_attn):
    return pl.pallas_call(
        functools.partial(input_back_kernel, chips=len(pieces)),
        out_shape=shaped(x.shape, F32),
        compiler_params=params(False),
        name="input_back",
    )(*pieces, x, grad_middle, norm_attn)


def project_back_kernel(*refs, head_size):
    dq, qlin, klin, lanes = refs[0:2], refs[2:4], refs[4:6], refs[6:8]
    dk_ref, dv_ref, qg_ref, kg_ref = refs[8:12]
    gl, gain_ref = refs[12:14], refs[14]
    half = head_size // 2
    rows = qlin[0].shape[0]
    lane = lanes_of((rows, WIDE))
    blocks = head_blocks(head_size)

    @pl.when(pl.program_id(0) == 0)
    def _():
        gain_ref[...] = jnp.zeros_like(gain_ref)

    for side in range(2):
        cosine, sine = tables(lanes[side][:half, :], lanes[side][half : 2 * half, :])

        def back(grad, u, gain, at):
            grad = grad.astype(F32)
            grad = grad * cosine - partner(grad, lane, head_size) * sine
            factor = lax.rsqrt(head_sum(u * u, blocks) * (1.0 / head_size) + EPSILON)
            gain_ref[at : at + 1, :] += jnp.sum(grad * u * factor, axis=0, keepdims=True)
            weighted = grad * gain
            mean = head_sum(weighted * u, blocks) * (1.0 / head_size)
            return (factor * weighted - u * (factor * factor * factor) * mean).astype(BF16)

        gq = back(dq[side][...], qlin[side][...], qg_ref[...], 0)
        gk = back(dk_ref[side], klin[side][...], kg_ref[...], 1)
        gl[side][...] = jnp.concatenate([gq, gk, dv_ref[side]], axis=1)


def project_back(dq, qlin, klin, lane_rows, dk, dv, q_gain, k_gain, head_size, chips):
    half = qlin[0].shape[0]
    rows = half // chips
    count = lane_rows[0].shape[0]
    row_block = lambda cols: pl.BlockSpec((rows, cols), lambda i: (i, 0))
    both = pl.BlockSpec((2, rows, WIDE), lambda i: (0, i, 0))
    gain = shaped((8, WIDE), F32)
    return pl.pallas_call(
        functools.partial(project_back_kernel, head_size=head_size),
        grid=(chips,),
        in_specs=[row_block(WIDE)] * 6
        + [pl.BlockSpec((count, rows), lambda i: (0, i))] * 2
        + [both, both, whole(q_gain), whole(k_gain)],
        out_specs=[row_block(3 * WIDE), row_block(3 * WIDE), whole(gain)],
        out_shape=[shaped((half, 3 * WIDE), BF16)] * 2 + [gain],
        compiler_params=params(),
        cost_estimate=pl.CostEstimate(
            flops=2 * half * WIDE * 16 * WIDE, bytes_accessed=half * WIDE * 40, transcendentals=0
        ),
        name="project_back",
    )(*dq, *qlin, *klin, *lane_rows, dk, dv, q_gain, k_gain)


def spread_back_kernel(*refs, chips, near):
    gl_ref, w_ref = refs[:2]
    got = refs[2:3] if near else ()
    outs, w_s = refs[2 + len(got) : -1], refs[-1]
    step = pl.program_id(0)

    @pl.when(step == 0)
    def _():
        assemble(w_s, w_ref)

    out = dot_nt(gl_ref[...], w_s[...])
    if near:
        out = (out + got[0][...].astype(F32)).astype(BF16)
        for r in range(chips):

            @pl.when(step == r)
            def _(r=r):
                outs[r][...] = out

    else:
        outs[0][...] = out.astype(BF16)


def spread_back(gl, w, chips, got=None):
    half, wide = gl.shape
    width = math.prod(w.shape[:-1])
    rows = half // chips
    near = got is not None
    row_block = lambda cols: pl.BlockSpec((rows, cols), lambda i: (i, 0))
    out_shape = [shaped((rows, width), BF16)] * chips if near else [shaped((half, width), BF16)]
    return pl.pallas_call(
        functools.partial(spread_back_kernel, chips=chips, near=near),
        grid=(chips,),
        in_specs=[row_block(wide), whole(w)] + ([row_block(width)] if near else []),
        out_specs=[whole(a) for a in out_shape] if near else [row_block(width)],
        out_shape=out_shape,
        scratch_shapes=[pltpu.VMEM((width, wide), BF16)],
        compiler_params=params(),
        cost_estimate=pl.CostEstimate(
            flops=2 * half * width * wide, bytes_accessed=half * width * 4, transcendentals=0
        ),
        name="spread_back",
    )(gl, w, *([got] if near else []))


def last_kernel(in_ref, *refs, z_count, shard):
    outs, small_ref = refs[:-1], refs[-1]
    seq_count = in_ref.shape[0] // z_count
    small = None
    for s in range(seq_count):
        total = None
        for f in range(z_count):
            block = in_ref[s * z_count + f].astype(F32)
            total = block if total is None else total + block
        for i, out_ref in enumerate(outs):
            out_ref[:, s * WIDE : (s + 1) * WIDE] = total[:shard, i * WIDE : (i + 1) * WIDE]
        small = total[shard:] if small is None else small + total[shard:]
    small_ref[...] = small


def last_sums(blocks, z_count, shard):
    count, rows, wide = blocks.shape
    seq_count = count // z_count
    return pl.pallas_call(
        functools.partial(last_kernel, z_count=z_count, shard=shard),
        out_shape=[shaped((shard, seq_count * WIDE), F32)] * 3 + [shaped((rows - shard, wide), F32)],
        compiler_params=params(False),
        name="last_sums",
    )(blocks)


def swap(x, seq_count, bits):
    return lax.ppermute(x, "seq", [(i, i ^ bits) for i in range(seq_count)])


def to_chips(x, seq_count):
    return [x] + [swap(x, seq_count, 2 * r) for r in range(1, seq_count // 2)]


def spread_slots(slots, seq_count):
    return [slots[0]] + [swap(slots[r], seq_count, 2 * r) for r in range(1, len(slots))]


def after(values, *others):
    kept, _ = lax.optimization_barrier((values, others))
    return kept


def add_up(parts):
    total = parts[0].astype(F32)
    for part in parts[1:]:
        total = total + part.astype(F32)
    return total


def body(
    tokens, weight_query, weight_key, weight_value, weight_out, weight_gate, weight_up, weight_down,
    norm_attn, norm_ffn, query_gain, key_gain, variate_bias, variate_ids, sample_ids, time_ids,
    out_grad,
):
    seq_count = lax.axis_size("seq")
    z_count = lax.axis_size("fsdp")
    everyone = seq_count * z_count
    chips = seq_count // 2
    _, rows, width = tokens.shape
    heads = variate_bias.shape[1]
    head_size = query_gain.shape[0]
    half_size = head_size // 2
    shard = weight_query.shape[0]
    features = heads * head_size
    hidden = weight_gate.shape[1] // seq_count
    me = lax.axis_index("seq")
    x_own = tokens.reshape(rows, width)
    dout_own = out_grad.reshape(rows, width)

    columns = columns_by_device(
        (weight_query, weight_key, weight_value, weight_gate, weight_up), seq_count
    )
    columns = lax.all_to_all(columns, "seq", split_axis=0, concat_axis=0, tiled=True)
    w_out_rows = lax.all_gather(weight_out, "fsdp", axis=0, tiled=True)
    columns = after(columns, w_out_rows)
    w_qkv = jnp.broadcast_to(
        columns[None, :, :, : 3 * WIDE], (z_count, seq_count, shard, 3 * WIDE)
    )
    w_qkv = gathered(lax.all_to_all(w_qkv, "fsdp", split_axis=0, concat_axis=0, tiled=True))
    w_down = lax.all_gather(weight_down, "fsdp", axis=0, tiled=True)
    if features < WIDE:
        w_out_rows = jnp.pad(w_out_rows, ((0, WIDE - features), (0, 0)))
    gu_columns = columns[:, :, 3 * WIDE :]
    w_gu = gathered(lax.all_gather(gu_columns, "fsdp", axis=0, tiled=False))

    ids = jnp.concatenate([variate_ids, sample_ids, time_ids // 64, time_ids % 64], axis=0)
    ids = jnp.pad(ids.astype(BF16), ((0, 12), (0, width - rows)))
    packed = after(jnp.concatenate([x_own, ids], axis=0), columns, w_out_rows)
    near_x = to_chips(packed, seq_count)
    extra = after(jnp.concatenate([dout_own, w_out_rows], axis=0), near_x[1:2])
    stack_x = jnp.concatenate(after(near_x, w_qkv, gu_columns, extra), axis=0)
    far_x = swap(stack_x, seq_count, 1)
    near_extra = to_chips(extra, seq_count)

    gain_attn = norm_attn.reshape(1, width)
    gain_ffn = norm_ffn.reshape(1, width)
    q_gain = jnp.tile(query_gain, WIDE // head_size).reshape(1, WIDE)
    k_gain = jnp.tile(key_gain, WIDE // head_size).reshape(1, WIDE)
    frequency = (10000.0 ** (-2.0 * jnp.arange(half_size).astype(F32) / head_size))[:, None]

    def projected(x):
        return project(
            x, chips, w_qkv, gain_attn, q_gain, k_gain, frequency, variate_bias, head_size
        )

    near_all = projected(stack_x)
    far_all = projected(far_x)
    nin, q_lin, k_lin, lane_rows, q_aug, k_aug, k_trans, v_aug = zip(near_all, far_all)
    attend_near = attend(q_aug[0], k_aug, v_aug, head_size)
    attend_far = attend(after(q_aug[1], attend_near, near_extra[1:2]), k_aug, v_aug, head_size)
    far_extra = [swap(e, seq_count, 1) for e in after(near_extra, attend_far)]
    mixed, o_full, z_inverse = zip(attend_near, attend_far)
    sent = (mixed[0], after(mixed[1], near_extra[1:]))
    own_parts = [to_chips(m, seq_count) for m in sent]
    own_parts[0] = after(own_parts[0], attend_far)
    sib_stack = [swap(jnp.concatenate(own_parts[side], axis=0), seq_count, 1) for side in (0, 1)]

    nm_far, inner_far, ggu_far, dout_far, gnm_far, lay_far = ffn(
        1, own_parts[1], sib_stack[0], far_x, near_extra, far_extra, w_gu, w_down, gain_ffn
    )
    nm_near, inner_near, ggu_near, dout_near, middle, mixed_own, *slots = ffn(
        0, own_parts[0], sib_stack[1], stack_x, near_extra, far_extra, w_gu, w_down, gain_ffn,
        swap(gnm_far, seq_count, 1), group=16 // chips,
    )

    gnm_parts = spread_slots(slots[:chips], seq_count)
    grad_gu, grad_down, gnf = ffn_grads(
        (nm_near, nm_far), (ggu_near, ggu_far), (inner_near, inner_far), (dout_near, dout_far),
        w_gu, seq_count, z_count, swap(slots[0][:8, :WIDE], seq_count, 1),
    )
    me_row = jnp.reshape(me, (1,))
    grad_middle, grad_branch, g_out = middle_back(
        after(gnm_parts, grad_gu, grad_down),
        middle, gain_ffn, near_extra, far_extra, me_row,
    )
    g_all = lax.all_to_all(g_out, "seq", split_axis=0, concat_axis=0, tiled=True)

    grad_gu = lax.psum_scatter(grad_gu, "fsdp", scatter_dimension=0, tiled=True)
    grad_gu = grad_gu.reshape(seq_count, shard, 2 * hidden)
    grad_down = lax.psum_scatter(grad_down, "fsdp", scatter_dimension=0, tiled=True)
    grad_out = dot_tn(mixed_own, grad_branch).astype(BF16)
    half_out = chips * WIDE
    out_slots = add_up([grad_out[:half_out], swap(grad_out[half_out:], seq_count, 1)])
    out_slots = out_slots.astype(BF16)
    lay_got = swap(after(lay_far, grad_branch), seq_count, 1)
    both_slots = []
    for r in range(chips):
        lay = add_up([slots[chips + r], lay_got[r * rows : (r + 1) * rows]]).astype(BF16)
        both_slots.append(jnp.concatenate([lay, out_slots[r * WIDE : (r + 1) * WIDE]], axis=0))
    both_parts = spread_slots(after(both_slots, g_all), seq_count)
    gu_got = lax.all_to_all(
        after(grad_gu, g_all), "seq", split_axis=0, concat_axis=0, tiled=True
    )

    dq_near, dq_far, dk, dv, bias_rows = attend_back(
        me_row, after(g_all, both_slots),
        q_aug, o_full, z_inverse, lane_rows, k_aug, k_trans, v_aug, head_size,
    )
    dq_far = after(dq_far, grad_gu)
    gl_near, gl_far, gain_rows = project_back(
        (dq_near, dq_far), q_lin, k_lin, lane_rows, dk, dv, q_gain, k_gain, head_size, chips
    )
    (gni_far,) = spread_back(after(gl_far, both_parts), w_qkv, chips)
    gni_got = swap(gni_far, seq_count, 1)
    grad_qkv, gna = pair_product(
        nin, (gl_near, gl_far), w_qkv, swap(gain_rows, seq_count, 1)
    )

    grad_qk_gain = gain_rows[:2, :features].reshape(2, heads, head_size).sum(axis=1)
    bias_cols = jnp.sum(bias_rows, axis=1).reshape(2, 2, 4).sum(axis=2)[:, :heads]
    bias_both = jnp.stack([bias_cols[0], bias_cols[1] - bias_cols[0]])
    bias_all = lax.dynamic_update_slice(
        jnp.zeros((2, heads * seq_count), F32), bias_both, (0, me * heads)
    )
    small = jnp.concatenate(
        [
            gna[0] / norm_attn,
            gnf / norm_ffn,
            grad_qk_gain.reshape(-1),
            bias_all.reshape(-1),
        ]
    )
    count = small.shape[0]
    small_rows = -(-count // (8 * 3 * WIDE)) * 8
    small = jnp.pad(small, (0, small_rows * 3 * WIDE - count)).astype(BF16)
    small = jnp.broadcast_to(small.reshape(1, small_rows, 3 * WIDE), (everyone, small_rows, 3 * WIDE))
    grad_qkv = after(grad_qkv, gu_got)
    blocks = jnp.concatenate([grad_qkv.reshape(everyone, shard, 3 * WIDE), small], axis=1)
    last = lax.all_to_all(blocks, ("seq", "fsdp"), split_axis=0, concat_axis=0, tiled=True)
    gni_slots = spread_back(
        gl_near, w_qkv, chips, after(gni_got, blocks)
    )
    gni_parts = spread_slots(gni_slots, seq_count)
    both = add_up(after(both_parts, gni_slots))
    grad_out = both[rows : rows + features]
    z_me = lax.axis_index("fsdp")
    bit = z_count // 2
    while bit:
        low, high = jnp.split(grad_out, 2, axis=0)
        upper = (z_me & bit) > 0
        away = jnp.where(upper, low, high).astype(BF16)
        away = lax.ppermute(away, "fsdp", [(i, i ^ bit) for i in range(z_count)])
        grad_out = jnp.where(upper, high, low) + away.astype(F32)
        bit //= 2
    in_grad = input_back(gni_parts, x_own, grad_middle, gain_attn)

    gu_got = after(gu_got, gni_slots)
    grad_down = after(grad_down, gni_slots)
    layer_out = (middle + both[:rows]).astype(BF16)
    grad_gu = gu_got.transpose(1, 0, 2).astype(F32)
    grad_gate = grad_gu[:, :, :hidden].reshape(shard, seq_count * hidden)
    grad_up = grad_gu[:, :, hidden:].reshape(shard, seq_count * hidden)
    grad_down = grad_down.astype(F32)
    *grad_qkv, small = last_sums(after(last, in_grad, grad_out, grad_down), z_count, shard)
    grad_query, grad_key, grad_value = (
        g.reshape(shard, seq_count, WIDE)[:, :, :features].reshape(shard, width)
        if features < WIDE
        else g
        for g in grad_qkv
    )
    small = small.reshape(-1)
    cut = 2 * width + 2 * head_size
    grad_bias = lax.dynamic_slice(
        small[cut:count].reshape(2, heads * seq_count), (0, me * heads), (2, heads)
    )
    return (
        layer_out.reshape(tokens.shape),
        in_grad.reshape(tokens.shape),
        grad_query,
        grad_key,
        grad_value,
        grad_out,
        grad_gate,
        grad_up,
        grad_down,
        small[:width],
        small[width : 2 * width],
        small[2 * width : 2 * width + head_size],
        small[2 * width + head_size : cut],
        grad_bias,
    )


def solution(mesh):
    rows = P("fsdp", "seq", None)
    shards = P(("seq", "fsdp"), None)
    ids = P("fsdp", "seq")
    bias = P(None, "seq")
    return jax.shard_map(
        body,
        mesh=mesh,
        in_specs=(rows,) + (shards,) * 7 + (P(),) * 4 + (bias, ids, ids, ids, rows),
        out_specs=(rows, rows) + (shards,) * 7 + (P(),) * 4 + (bias,),
        check_vma=False,
    )
```
